128 devices in a mesh: fsdp: 128 (over x, y, z, core).
Axes of the slice: x: 4, y: 4, z: 4, core: 2. Of those that a mesh axis runs over, the one named last changes fastest.
Arguments:
- hidden_in: bfloat16 [16384, 1024], P('fsdp'), may hold values from -6 to 6
- cotangent: bfloat16 [16384, 1024], P('fsdp'), may hold values from -6 to 6
- seq_lengths: int32 [512], replicated, may hold values from 1 to 125, as said below
- seq_owner: int32 [512], replicated, may hold values from 0 to 127, as said below
- routes: int32 [16384, 8], P('fsdp'), may hold values from 0 to 31, all different within a row; in each aligned block of 128 rows (0 to 127, 128 to 255, ...) at most 36 rows name the same one
- query_key_value_weight: bfloat16 [2, 1024, 2048], P(None, 'fsdp'), may hold values from -0.25 to 0.25
- out_weight: bfloat16 [2, 1024, 1024], P(None, 'fsdp'), may hold values from -0.75 to 0.75
- router_weight: bfloat16 [2, 1024, 32], P(None, 'fsdp'), may hold values from -0.09375 to 0.09375
- gain_attn: bfloat16 [2, 1024], P(None, 'fsdp'), may hold values from 0.5 to 1.5
- gain_mlp: bfloat16 [2, 1024], P(None, 'fsdp'), may hold values from 0.5 to 1.5
- expert_in: bfloat16 [2, 16384, 2048], P(None, 'fsdp'), may hold values from -0.1875 to 0.1875
- expert_out: bfloat16 [2, 16384, 1024], P(None, 'fsdp'), may hold values from -1 to 1
Outputs:
- out_hidden: bfloat16 [16384, 1024], P('fsdp')
- grad_hidden: float32 [16384, 1024], P('fsdp')
- grad_qkv: float32 [2, 1024, 2048], P(None, 'fsdp')
- grad_out_proj: float32 [2, 1024, 1024], P(None, 'fsdp')
- grad_router: float32 [2, 1024, 32], P(None, 'fsdp')
- grad_gain_attn: float32 [2, 1024], P(None, 'fsdp')
- grad_gain_mlp: float32 [2, 1024], P(None, 'fsdp')
- grad_expert_in: float32 [2, 16384, 2048], P(None, 'fsdp')
- grad_expert_out: float32 [2, 16384, 1024], P(None, 'fsdp')
The draws below stay inside these ranges and needn't reach their ends.
Inputs may be any that keep to these rules, and one draw needn't show every extreme that they name: `routes`: of the rows of one device (128 rows, aligned blocks), no expert is named by more than 36, and in every draw some expert is named by exactly 36 of one device's rows. `seq_lengths`: the 4 sequences of one device sum to at most 128 tokens; some sequence has exactly 125. `seq_owner`: every device owns exactly 4 sequences.
All inputs are finite; a program needn't handle non-finite values.
Results may differ from the reference program's by a relative error of at most 0.035.
Values may be sent and summed in bfloat16 or wider, within the bound.
No kernel may reach another device: no remote copies, remote signals or barrier semaphores. Data moves between devices by JAX's collectives and lax.ppermute only.
A program may use at most 320 MiB of HBM per device.

```python
import math
import jax
import jax.numpy as jnp
import numpy as np
from jax import lax

MODEL_WIDTH = 1024
QUERY_HEADS = 16
KEY_VALUE_HEADS = 8
HEAD_SIZE = 64
E = 32
F = 512
TOPK = 8
LAYER_COUNT = 2
SEQ_DEV = 4
TOK_DEV = 128
CAP = 36
TOKENS = 16384
NSEQ = 512
N_FSDP = 128


def layout_draw(key):
    device_count = NSEQ // SEQ_DEV
    key_total, key_cut, key_full, key_order = jax.random.split(key, 4)
    totals = jax.random.randint(key_total, (device_count,), TOK_DEV // 2, TOK_DEV + 1)
    full_device = jax.random.randint(key_full, (), 0, device_count)
    candidates = jnp.arange(1, TOK_DEV, dtype=jnp.int32)
    cut_keys = jax.random.split(key_cut, device_count)

    def cuts_of(one_key, total_len):
        shuffled = jax.random.permutation(one_key, candidates)
        ranking = jnp.arange(TOK_DEV - 1, dtype=jnp.int32)
        scoring = jnp.where(shuffled < total_len, ranking, ranking + TOK_DEV)
        picked = shuffled[jnp.argsort(scoring, stable=True)[:SEQ_DEV - 1]]
        marker = jnp.concatenate([jnp.zeros((1,), jnp.int32), jnp.sort(picked), total_len[None]])
        return marker[1:] - marker[:-1]
    lengths = jax.vmap(cuts_of)(cut_keys, totals)
    extreme = jnp.concatenate([jnp.full((1,), TOK_DEV - SEQ_DEV + 1, jnp.int32), jnp.ones((SEQ_DEV - 1,), jnp.int32)])
    lengths = jnp.where((jnp.arange(device_count) == full_device)[:, None], extreme[None, :], lengths)
    owners = jnp.broadcast_to(jnp.arange(device_count, dtype=jnp.int32)[:, None], (device_count, SEQ_DEV))
    placing = jax.random.permutation(key_order, NSEQ)
    seq_lengths = jnp.zeros((NSEQ,), jnp.int32).at[placing].set(lengths.reshape(-1).astype(jnp.int32))
    seq_owner = jnp.zeros((NSEQ,), jnp.int32).at[placing].set(owners.reshape(-1))
    return (seq_lengths, seq_owner)


def draw_seq_lengths(key, part):
    shared = layout_draw(key)
    return shared[0]


def draw_seq_owner(key, part):
    shared = layout_draw(key)
    return shared[1]


def levels(key, extent, shards, smallest, top_value):
    level, own = 1.0, jax.random.fold_in(key, 6)
    for axis_at, blocks in shards:
        steps = jnp.exp(jax.random.uniform(jax.random.fold_in(own, axis_at), (blocks,), jnp.float32, smallest / len(shards), top_value / len(shards)))
        level = level * jnp.repeat(steps, extent[axis_at] // blocks).reshape([-1 if axis == axis_at else 1 for axis in range(len(extent))])
    return level


def assign_block(stream_key, own, number, rows, count, top, limit, lean):
    sequence = jax.random.permutation(stream_key, count)
    crowded, ordinary = portions_of(count, rows * top, limit, lean, True), portions_of(count, rows * top, limit, lean, False)
    places = jnp.arange(count)

    def named(tallies, rotation):
        used = int((tallies > 0).sum())
        fixed = max(1, used // 4)
        passed = fixed + (places - fixed + rotation * (used - fixed)) % max(1, count - fixed)
        return jnp.zeros((count,), jnp.int32).at[sequence[jnp.where(places < fixed, places, passed)]].set(jnp.asarray(tallies, jnp.int32))

    tallies = jnp.where(number % 4 == 0, named(crowded, number // 4), named(ordinary, number - number // 4 - 1))
    mixed = jax.random.permutation(jax.random.fold_in(own, 3), count)
    donor, taker = mixed[0:count // 2 * 2:2], mixed[1:count // 2 * 2:2]
    room = jnp.minimum(tallies[donor] - 1, limit - tallies[taker]) // 2
    room = jnp.where((donor == sequence[0]) | (taker == sequence[0]) | (tallies[taker] == 0), 0, jnp.maximum(room, 0))
    passed = jax.random.randint(jax.random.fold_in(own, 4), (count // 2,), 0, 1 << 20) % (room + 1)
    tallies = tallies.at[donor].add(-passed).at[taker].add(passed)
    items = jnp.searchsorted(jnp.cumsum(tallies), jnp.arange(rows * top), side="right").astype(jnp.int32)
    listing = items.reshape(top, rows).T
    listing = listing[jax.random.permutation(jax.random.fold_in(own, 1), rows)]
    rotation = jax.random.randint(jax.random.fold_in(own, 2), (rows, 1), 0, top)
    return jnp.take_along_axis(listing, (jnp.arange(top)[None, :] + rotation) % top, axis=1)


def portions_of(amount, total, limit, skew, full):
    loads = [(1 << 20) // math.isqrt(standing ** skew) + 1 for standing in range(1, amount + 1)]
    largest = limit if full else min(limit, max(-(-total // amount), total * loads[0] // sum(loads)))
    least = 1 if total - largest >= amount - 1 else 0
    counts, rest = [largest] + [least] * (amount - 1), total - largest - least * (amount - 1)
    while rest > 0:
        free = [i for i in range(1, amount) if counts[i] < largest] or [i for i in range(1, amount) if counts[i] < limit]
        whole, budget = sum([loads[i] for i in free]), rest
        for i in free:
            extra = min(limit - counts[i], max(1, budget * loads[i] // whole), rest)
            counts[i] = counts[i] + extra
            rest = rest - extra
    return np.array(counts)


def bell_draw(key, shape, scale, most, cuts=(), held_as=jnp.bfloat16):
    loudness = levels(key, shape, cuts, -0.22, 0.18) if cuts else 1.0
    values = jax.random.normal(key, shape, jnp.float32) * scale * loudness
    return jnp.minimum(jnp.maximum(values, -most), most).astype(held_as)


def setup_inputs(seed: int = 0) -> dict:
    keys = jax.random.split(jax.random.key(seed), 13)
    hidden_in = bell_draw(keys[0], (TOKENS, MODEL_WIDTH), 1.0, 6.0, ((0, 128),))
    cotangent = bell_draw(keys[1], (TOKENS, MODEL_WIDTH), 1.0, 6.0, ((0, 128),))
    seq_lengths = draw_seq_lengths(jax.random.fold_in(keys[12], 71), 0)
    seq_owner = draw_seq_owner(jax.random.fold_in(keys[12], 71), 0)
    routes_keys = jax.random.split(jax.random.fold_in(keys[4], 1), TOKENS // TOK_DEV)
    routes_turns = jax.random.permutation(jax.random.fold_in(keys[4], 3), TOKENS // TOK_DEV)
    routes = jax.vmap(lambda own, number: assign_block(jax.random.fold_in(keys[4], 2), own, number, TOK_DEV, E, TOPK, CAP, 1))(routes_keys, routes_turns).reshape((TOKENS, TOPK))
    query_key_value_weight = bell_draw(keys[5], (LAYER_COUNT, MODEL_WIDTH, (QUERY_HEADS + 2 * KEY_VALUE_HEADS) * HEAD_SIZE), (MODEL_WIDTH // 2) ** -0.5, 0.25, ((1, 128),))
    out_weight = bell_draw(keys[6], (LAYER_COUNT, QUERY_HEADS * HEAD_SIZE, MODEL_WIDTH), (QUERY_HEADS * HEAD_SIZE // 16) ** -0.5, 0.75, ((1, 128),))
    router_weight = bell_draw(keys[7], (LAYER_COUNT, MODEL_WIDTH, E), (4 * MODEL_WIDTH) ** -0.5, 0.09375, ((1, 128),))
    gain_attn = jnp.clip(1.0 + 0.1 * jax.random.normal(keys[8], (LAYER_COUNT, MODEL_WIDTH), jnp.float32), 0.5, 1.5).astype(jnp.bfloat16)
    gain_mlp = jnp.clip(1.0 + 0.1 * jax.random.normal(keys[9], (LAYER_COUNT, MODEL_WIDTH), jnp.float32), 0.5, 1.5).astype(jnp.bfloat16)
    expert_in = bell_draw(keys[10], (LAYER_COUNT, E * F, 2 * MODEL_WIDTH), MODEL_WIDTH ** -0.5, 0.1875, ((1, 128),))
    expert_out = bell_draw(keys[11], (LAYER_COUNT, E * F, MODEL_WIDTH), (F // 16) ** -0.5, 1.0, ((1, 128),))
    return dict(hidden_in=hidden_in, cotangent=cotangent, seq_lengths=seq_lengths, seq_owner=seq_owner, routes=routes, query_key_value_weight=query_key_value_weight, out_weight=out_weight, router_weight=router_weight, gain_attn=gain_attn, gain_mlp=gain_mlp, expert_in=expert_in, expert_out=expert_out)


EPSILON = 1e-06
ROPE_BASE = 10000.0
MASKED = -1e+30
HIGHEST = lax.Precision.HIGHEST

@jax.custom_vjp
def reduced_precision(v):
    return lax.optimization_barrier(v.astype(jnp.bfloat16)).astype(jnp.float32)

@jax.custom_vjp
def reduced_backward(v):
    return v

def low_keep(v):
    return (reduced_precision(v), None)

def low_pass(kept, grad):
    return (grad,)

def back_keep(v):
    return (v, None)

def back_low(kept, grad):
    return (reduced_precision(grad),)
reduced_precision.defvjp(low_keep, low_pass)
reduced_backward.defvjp(back_keep, back_low)

def seq_layout(seq_lengths, seq_owner, device):
    owned_seq = seq_owner == device
    ranking = jnp.cumsum(owned_seq.astype(jnp.int32)) - 1
    counter = jnp.arange(SEQ_DEV, dtype=jnp.int32)
    picker = (owned_seq[None, :] & (ranking[None, :] == counter[:, None])).astype(jnp.int32)
    own_lengths = lax.optimization_barrier(jnp.sum(picker * seq_lengths[None, :], axis=1))
    seq_ends = jnp.cumsum(own_lengths)
    slot_ids = jnp.arange(TOK_DEV, dtype=jnp.int32)
    segment = lax.optimization_barrier(jnp.sum((slot_ids[:, None] >= seq_ends[None, :]).astype(jnp.int32), axis=1))
    seq_starts = seq_ends - own_lengths
    first_slot = lax.optimization_barrier(jnp.sum(jnp.where(segment[:, None] == counter[None, :], seq_starts[None, :], 0), axis=1))
    position = slot_ids - first_slot
    allowed = (segment[:, None] == segment[None, :]) & (slot_ids[:, None] >= slot_ids[None, :])
    return (position, segment < SEQ_DEV, allowed)

def rope_tables(position):
    half_size = HEAD_SIZE // 2
    exponent = jnp.arange(half_size, dtype=jnp.float32) * (2.0 / HEAD_SIZE)
    frequency = jnp.exp(-math.log(ROPE_BASE) * exponent)
    angles = position.astype(jnp.float32)[:, None] * frequency[None, :]
    return (jnp.cos(angles), jnp.sin(angles))

def apply_rotation(values, cosine_table, sine_values):
    half_size = values.shape[-1] // 2
    first_half = values[..., :half_size]
    second_half = values[..., half_size:]
    cos_wide = cosine_table[:, None, :]
    sin_wide = sine_values[:, None, :]
    return jnp.concatenate([first_half * cos_wide - second_half * sin_wide, second_half * cos_wide + first_half * sin_wide], axis=-1)

def dispatch_index(route_block, live_row):
    row_count = route_block.shape[0]
    onehot = ((route_block[:, :, None] == jnp.arange(E, dtype=jnp.int32)[None, None, :]) & live_row[:, None, None]).astype(jnp.int32)
    flat_hits = onehot.reshape(row_count * TOPK, E)
    earlier = jnp.cumsum(flat_hits, axis=0) - flat_hits
    slot_number = lax.optimization_barrier(jnp.sum(earlier * flat_hits, axis=1))
    valid_row = jnp.repeat(live_row, TOPK)
    flat_index = jnp.where(valid_row, route_block.reshape(-1) * CAP + slot_number, E * CAP)
    return (flat_index.astype(jnp.int32), valid_row)

def attention_block(hidden, gain_one, qkv_full, out_full, live, allowed, cosine_table, sine_values):
    token_total = hidden.shape[0]
    query_width = QUERY_HEADS * HEAD_SIZE
    key_value_width = KEY_VALUE_HEADS * HEAD_SIZE
    inverse = lax.rsqrt(lax.optimization_barrier(jnp.mean(hidden * hidden, axis=-1, keepdims=True)) + EPSILON)
    normed_low = reduced_precision(hidden * inverse * gain_one)
    projected_rows = reduced_backward(jnp.dot(normed_low, qkv_full, precision=HIGHEST))
    rotated_query = reduced_precision(reduced_backward(apply_rotation(projected_rows[:, :query_width].reshape(token_total, QUERY_HEADS, HEAD_SIZE), cosine_table, sine_values)))
    rotated_query = rotated_query.reshape(token_total, KEY_VALUE_HEADS, QUERY_HEADS // KEY_VALUE_HEADS, HEAD_SIZE)
    rotated_key = reduced_precision(reduced_backward(apply_rotation(projected_rows[:, query_width:query_width + key_value_width].reshape(token_total, KEY_VALUE_HEADS, HEAD_SIZE), cosine_table, sine_values)))
    reduced_value = reduced_precision(reduced_backward(projected_rows[:, query_width + key_value_width:].reshape(token_total, KEY_VALUE_HEADS, HEAD_SIZE)))
    scores = reduced_backward(jnp.einsum('tkgd,ukd->kgtu', rotated_query, rotated_key, precision=HIGHEST) * HEAD_SIZE ** (-0.5))
    scores = jnp.where(allowed[None, None], scores, MASKED)
    biggest = lax.optimization_barrier(jnp.max(scores, axis=-1, keepdims=True))
    exp_scores = jnp.exp(scores - biggest)
    softmaxed = exp_scores / lax.optimization_barrier(jnp.sum(exp_scores, axis=-1, keepdims=True))
    mixed = jnp.einsum('kgtu,ukd->tkgd', reduced_precision(softmaxed), reduced_value, precision=HIGHEST).reshape(token_total, query_width)
    mixed_low = reduced_precision(reduced_backward(mixed * live[:, None]))
    return hidden + reduced_backward(jnp.dot(mixed_low, out_full, precision=HIGHEST))

def expert_block(hidden, gain_two, router_full, expert_in_l, expert_out_l, live, route_block, flat_index):
    token_total = hidden.shape[0]
    group_size = N_FSDP // E
    unit_rows = F // group_size
    inverse = lax.rsqrt(lax.optimization_barrier(jnp.mean(hidden * hidden, axis=-1, keepdims=True)) + EPSILON)
    routed_in = reduced_precision(hidden * inverse * gain_two)
    logits = reduced_backward(jnp.dot(routed_in, router_full, precision=HIGHEST))
    chosen = jnp.take_along_axis(logits, route_block, axis=1)
    top_logit = lax.optimization_barrier(jnp.max(chosen, axis=-1, keepdims=True))
    exp_chosen = jnp.exp(chosen - top_logit)
    gate_live = exp_chosen / lax.optimization_barrier(jnp.sum(exp_chosen, axis=-1, keepdims=True)) * live[:, None]
    repeated = jnp.repeat(routed_in, TOPK, axis=0)
    dispatched = jnp.zeros((E * CAP, MODEL_WIDTH), jnp.float32).at[flat_index].set(repeated, mode='drop')
    rows_all = reduced_backward(jnp.broadcast_to(dispatched.reshape(E, 1, CAP, MODEL_WIDTH), (E, group_size, CAP, MODEL_WIDTH)))
    weight_in = expert_in_l.reshape(E, group_size, unit_rows, 2 * MODEL_WIDTH)
    weight_out = expert_out_l.reshape(E, group_size, unit_rows, MODEL_WIDTH)
    gate_pre = reduced_backward(jnp.einsum('escd,esrd->escr', rows_all, weight_in[..., :MODEL_WIDTH], precision=HIGHEST))
    up_pre = reduced_backward(jnp.einsum('escd,esrd->escr', rows_all, weight_in[..., MODEL_WIDTH:], precision=HIGHEST))
    units = reduced_precision(jax.nn.silu(gate_pre) * up_pre)
    parts = reduced_precision(jnp.einsum('escr,esrd->escd', units, weight_out, precision=HIGHEST))
    summed = reduced_backward(lax.optimization_barrier(jnp.sum(parts, axis=1))).reshape(E * CAP, MODEL_WIDTH)
    picked = summed[jnp.clip(flat_index, 0, E * CAP - 1)].reshape(token_total, TOPK, MODEL_WIDTH)
    return hidden + lax.optimization_barrier(jnp.sum(gate_live[:, :, None] * picked, axis=1))

def reference(hidden_in, cotangent, seq_lengths, seq_owner, routes, query_key_value_weight, out_weight, router_weight, gain_attn, gain_mlp, expert_in, expert_out):
    params = tuple((array.astype(jnp.float32) for array in (query_key_value_weight, out_weight, router_weight, gain_attn, gain_mlp, expert_in, expert_out)))
    route_blocks = routes.reshape(N_FSDP, TOK_DEV, TOPK)

    def forward(hidden_all, weights):
        qkv_all, out_all, router_all, gain_one_all, gain_two_all, expert_in_all, expert_out_all = weights

        def one_device(inputs):
            hidden, device, route_block = inputs
            position, live_row, allowed = seq_layout(seq_lengths, seq_owner, device)
            live = live_row.astype(jnp.float32)
            cosine_table, sine_values = rope_tables(position)
            flat_index = dispatch_index(route_block, live_row)[0]
            for layer_index in range(LAYER_COUNT):
                hidden = attention_block(hidden, gain_one_all[layer_index], qkv_all[layer_index], out_all[layer_index], live, allowed, cosine_table, sine_values)
                hidden = expert_block(hidden, gain_two_all[layer_index], router_all[layer_index], expert_in_all[layer_index], expert_out_all[layer_index], live, route_block, flat_index)
            return hidden
        outputs = lax.map(jax.checkpoint(one_device), (hidden_all.reshape(N_FSDP, TOK_DEV, MODEL_WIDTH), jnp.arange(N_FSDP, dtype=jnp.int32), route_blocks))
        return outputs.reshape(N_FSDP * TOK_DEV, MODEL_WIDTH)
    result, pull = jax.vjp(forward, hidden_in.astype(jnp.float32), params)
    grad_x, grad_w = pull(cotangent.astype(jnp.float32))
    return (result.astype(jnp.bfloat16), grad_x, grad_w[0], grad_w[1], grad_w[2], grad_w[3], grad_w[4], grad_w[5], grad_w[6])
```

```python
import math

import jax
import jax.numpy as jnp
from jax import lax
from jax.sharding import Mesh, PartitionSpec as P

MODEL_WIDTH = 1024
QUERY_HEADS = 16
KEY_VALUE_HEADS = 8
HEAD_SIZE = 64
E = 32
TOPK = 8
LAYER_COUNT = 2
SEQ_DEV = 4
TOK_DEV = 128
CAP = 36


EPSILON = 1e-06
ROPE_BASE = 10000.0
MASKED = -1e30

ROOM = 40
ROWS = E * ROOM
AXES = ("x", "y", "zh", "zl", "c")
EXPERT_AXES = ("x", "y", "zh")
CHIP_AXES = ("x", "y", "zh", "zl")
SWAP = [(0, 1), (1, 0)]


def sent_together(arrays, axis, dim, along):
    widths = [math.prod(a.shape[along:]) for a in arrays]
    both = jnp.concatenate(
        [a.reshape(*a.shape[:along], w) for a, w in zip(arrays, widths)], axis=along
    )
    out = lax.all_gather(both, axis, axis=dim, tiled=True)
    pieces = jnp.split(out, [sum(widths[:k]) for k in range(1, len(widths))], axis=along)
    return tuple((b.reshape(*out.shape[:along], *a.shape[along:]) for a, b in zip(arrays, pieces)))


def seq_layout(seq_lengths, seq_owner, device):
    owned_seq = seq_owner == device
    ranking = jnp.cumsum(owned_seq.astype(jnp.int32)) - 1
    counter = jnp.arange(SEQ_DEV, dtype=jnp.int32)
    picker = (owned_seq[None, :] & (ranking[None, :] == counter[:, None])).astype(jnp.int32)
    own_lengths = jnp.sum(picker * seq_lengths[None, :], axis=1)
    seq_ends = jnp.cumsum(own_lengths)
    slot_ids = jnp.arange(TOK_DEV, dtype=jnp.int32)
    segment = jnp.sum((slot_ids[:, None] >= seq_ends[None, :]).astype(jnp.int32), axis=1)
    seq_starts = seq_ends - own_lengths
    first_slot = jnp.sum(
        jnp.where(segment[:, None] == counter[None, :], seq_starts[None, :], 0), axis=1
    )
    position = slot_ids - first_slot
    allowed = (segment[:, None] == segment[None, :]) & (slot_ids[:, None] >= slot_ids[None, :])
    return (position, segment < SEQ_DEV, allowed)


def rope_tables(position):
    half_size = HEAD_SIZE // 2
    exponent = jnp.arange(half_size, dtype=jnp.float32) * (2.0 / HEAD_SIZE)
    frequency = jnp.exp(-math.log(ROPE_BASE) * exponent)
    angles = position.astype(jnp.float32)[:, None] * frequency[None, :]
    return (jnp.cos(angles), jnp.sin(angles))


def apply_rotation(values, cosine_table, sine_values):
    half_size = values.shape[-1] // 2
    first_half = values[..., :half_size]
    second_half = values[..., half_size:]
    cos_wide = cosine_table[:, None, :]
    sin_wide = sine_values[:, None, :]
    return jnp.concatenate(
        [
            first_half * cos_wide - second_half * sin_wide,
            second_half * cos_wide + first_half * sin_wide,
        ],
        axis=-1,
    )


def unrotate(grad_rot, cosine_table, sine_values):
    half_size = grad_rot.shape[-1] // 2
    first_half = grad_rot[..., :half_size]
    second_half = grad_rot[..., half_size:]
    cos_wide = cosine_table[:, None, :]
    sin_wide = sine_values[:, None, :]
    return jnp.concatenate(
        [
            first_half * cos_wide + second_half * sin_wide,
            second_half * cos_wide - first_half * sin_wide,
        ],
        axis=-1,
    )


def rounded(values):
    return lax.optimization_barrier(values.astype(jnp.bfloat16)).astype(jnp.float32)


def dispatch_table(route_block, live_row):
    experts = jnp.arange(E, dtype=jnp.int32)
    routed = jnp.any(route_block[:, :, None] == experts[None, None, :], axis=1)
    hits = (routed & live_row[:, None]).astype(jnp.bfloat16)
    slot_ids = jnp.arange(TOK_DEV, dtype=jnp.int32)
    before = (slot_ids[None, :] < slot_ids[:, None]).astype(jnp.bfloat16)
    rank = jnp.dot(before, hits, preferred_element_type=jnp.float32)
    code = jnp.where(hits > 0, rank, -1.0).astype(jnp.bfloat16)
    spread = spread_table()
    wide = jnp.dot(code, spread, preferred_element_type=jnp.float32)
    place = (jnp.arange(ROWS, dtype=jnp.int32) % ROOM).astype(jnp.float32)
    chosen = (wide == place[None, :]).astype(jnp.bfloat16)
    return routed, chosen


def spread_table():
    rows = jnp.arange(ROWS, dtype=jnp.int32) // ROOM
    return (jnp.arange(E, dtype=jnp.int32)[:, None] == rows[None, :]).astype(jnp.bfloat16)


def trade_rows(rows):
    return lax.all_to_all(
        rows.reshape(E, ROOM, MODEL_WIDTH), EXPERT_AXES, split_axis=0, concat_axis=0, tiled=True
    ).reshape(ROWS, MODEL_WIDTH)


def gather_expert(own):
    pair = jnp.concatenate([own, lax.ppermute(own, "zl", SWAP)], axis=0)
    return jnp.concatenate([pair, lax.ppermute(pair, "c", SWAP)], axis=0)


def scatter_expert(grad):
    half = grad.shape[0] // 2
    quarter = half // 2
    kept, given = grad[:half], grad[half:].astype(jnp.bfloat16)
    kept = kept + lax.ppermute(given, "c", SWAP).astype(jnp.float32)
    own, other = kept[:quarter], kept[quarter:].astype(jnp.bfloat16)
    return own + lax.ppermute(other, "zl", SWAP).astype(jnp.float32)


def scatter_dense(grad):
    width = grad.shape[1]
    core = lax.axis_index("c")
    blocks = grad.reshape(64, 2, MODEL_WIDTH // 128, width)
    given = lax.dynamic_slice_in_dim(blocks, 1 - core, 1, axis=1).astype(jnp.bfloat16)
    kept = lax.dynamic_slice_in_dim(blocks, core, 1, axis=1)
    kept = kept + lax.ppermute(given, "c", SWAP).astype(jnp.float32)
    kept = kept.reshape(64, MODEL_WIDTH // 128, width).astype(jnp.bfloat16)
    parts = lax.all_to_all(kept, CHIP_AXES, split_axis=0, concat_axis=0, tiled=True)
    return jnp.sum(parts.astype(jnp.float32), axis=0)


def norm_back(grad_norm, normed, inverse):
    return inverse * (grad_norm - normed * jnp.mean(grad_norm * normed, axis=-1, keepdims=True))


def probabilities(rotated_query, rotated_key, allowed):
    scores = jnp.einsum(
        "tkgd,ukd->kgtu", rotated_query, rotated_key, preferred_element_type=jnp.float32
    ) * HEAD_SIZE ** (-0.5)
    scores = jnp.where(allowed[None, None], scores, MASKED)
    biggest = jnp.max(scores, axis=-1, keepdims=True)
    exp_scores = jnp.exp(scores - biggest)
    return exp_scores / jnp.sum(exp_scores, axis=-1, keepdims=True)


def attend_forward(hidden, weights, live, allowed, cosine_table, sine_values):
    qkv_full, out_full, router_full, gain_one, gain_two = weights
    token_total = hidden.shape[0]
    query_width = QUERY_HEADS * HEAD_SIZE
    key_value_width = KEY_VALUE_HEADS * HEAD_SIZE
    inverse = lax.rsqrt(jnp.mean(hidden * hidden, axis=-1, keepdims=True) + EPSILON)
    normed = hidden * inverse
    normed_low = (normed * gain_one.astype(jnp.float32)).astype(jnp.bfloat16)
    projected_rows = jnp.dot(normed_low, qkv_full, preferred_element_type=jnp.float32)
    rotated_query = apply_rotation(
        projected_rows[:, :query_width].reshape(token_total, QUERY_HEADS, HEAD_SIZE),
        cosine_table,
        sine_values,
    ).astype(jnp.bfloat16)
    rotated_query = rotated_query.reshape(
        token_total, KEY_VALUE_HEADS, QUERY_HEADS // KEY_VALUE_HEADS, HEAD_SIZE
    )
    rotated_key = apply_rotation(
        projected_rows[:, query_width : query_width + key_value_width].reshape(
            token_total, KEY_VALUE_HEADS, HEAD_SIZE
        ),
        cosine_table,
        sine_values,
    ).astype(jnp.bfloat16)
    reduced_value = (
        projected_rows[:, query_width + key_value_width :]
        .reshape(token_total, KEY_VALUE_HEADS, HEAD_SIZE)
        .astype(jnp.bfloat16)
    )
    softmaxed = probabilities(rotated_query, rotated_key, allowed)
    mixed = jnp.einsum(
        "kgtu,ukd->tkgd",
        softmaxed.astype(jnp.bfloat16),
        reduced_value,
        preferred_element_type=jnp.float32,
    )
    mixed_low = (mixed.reshape(token_total, query_width) * live[:, None]).astype(jnp.bfloat16)
    attn_out = jnp.dot(mixed_low, out_full, preferred_element_type=jnp.float32)
    return (
        hidden + attn_out,
        (inverse, normed, normed_low, rotated_query, rotated_key, reduced_value, mixed_low),
    )


def expert_forward(hidden, weights, expert_in_l, expert_out_l, live, routed, chosen):
    qkv_full, out_full, router_full, gain_one, gain_two = weights
    inverse_two = lax.rsqrt(jnp.mean(hidden * hidden, axis=-1, keepdims=True) + EPSILON)
    normed_two = hidden * inverse_two
    routed_in = (normed_two * gain_two.astype(jnp.float32)).astype(jnp.bfloat16)
    rows = lax.dot_general(
        chosen, routed_in, (((0,), (0,)), ((), ())), preferred_element_type=jnp.float32
    ).astype(jnp.bfloat16)
    rows_here = trade_rows(rows)
    logits = jnp.dot(routed_in, router_full, preferred_element_type=jnp.float32)
    masked = jnp.where(routed, logits, MASKED)
    exp_chosen = jnp.where(routed, jnp.exp(masked - jnp.max(masked, axis=-1, keepdims=True)), 0.0)
    gate_prob = exp_chosen / jnp.sum(exp_chosen, axis=-1, keepdims=True)
    gate_wide = jnp.dot(
        gate_prob.astype(jnp.bfloat16), spread_table(), preferred_element_type=jnp.float32
    ).astype(jnp.bfloat16)
    mixing = gate_wide * chosen
    gate_pre = lax.dot_general(
        rows_here,
        expert_in_l[:, :MODEL_WIDTH],
        (((1,), (1,)), ((), ())),
        preferred_element_type=jnp.float32,
    )
    up_pre = lax.dot_general(
        rows_here,
        expert_in_l[:, MODEL_WIDTH:],
        (((1,), (1,)), ((), ())),
        preferred_element_type=jnp.float32,
    )
    units = (jax.nn.silu(gate_pre) * up_pre).astype(jnp.bfloat16)
    results = jnp.dot(units, expert_out_l, preferred_element_type=jnp.float32).astype(jnp.bfloat16)
    returned = trade_rows(results)
    result = hidden + jnp.dot(mixing, returned, preferred_element_type=jnp.float32)
    stash = (inverse_two, normed_two, routed_in, gate_prob, mixing, returned)
    return result, stash + (gate_pre, up_pre, rows_here)


def expert_backward(grad_out, weights, expert_in_l, expert_out_l, chosen, expert_stash):
    qkv_full, out_full, router_full, gain_one, gain_two = weights
    (
        inverse_two,
        normed_two,
        routed_in,
        gate_prob,
        mixing,
        returned,
        gate_pre,
        up_pre,
        rows_here,
    ) = expert_stash
    grad_out_low = grad_out.astype(jnp.bfloat16)
    slot_grads = lax.dot_general(
        mixing, grad_out_low, (((0,), (0,)), ((), ())), preferred_element_type=jnp.float32
    ).astype(jnp.bfloat16)
    grad_rows = trade_rows(slot_grads)
    products = lax.dot_general(
        grad_out_low, returned, (((1,), (1,)), ((), ())), preferred_element_type=jnp.float32
    )
    grad_gate = lax.dot_general(
        products * chosen.astype(jnp.float32),
        spread_table().astype(jnp.float32),
        (((1,), (1,)), ((), ())),
        precision=lax.Precision.HIGHEST,
        preferred_element_type=jnp.float32,
    )
    grad_chosen = gate_prob * (grad_gate - jnp.sum(gate_prob * grad_gate, axis=-1, keepdims=True))
    grad_logits = grad_chosen.astype(jnp.bfloat16)
    router_grad = lax.dot_general(
        routed_in, grad_logits, (((0,), (0,)), ((), ())), preferred_element_type=jnp.float32
    )
    grad_routed = lax.dot_general(
        grad_logits, router_full, (((1,), (1,)), ((), ())), preferred_element_type=jnp.float32
    )
    sigmoid_pre = jax.nn.sigmoid(gate_pre)
    activated = gate_pre * sigmoid_pre
    units = (activated * up_pre).astype(jnp.bfloat16)
    grad_units = lax.dot_general(
        grad_rows, expert_out_l, (((1,), (1,)), ((), ())), preferred_element_type=jnp.float32
    )
    grad_gate_pre = (
        grad_units * up_pre * (sigmoid_pre * (1.0 + gate_pre * (1.0 - sigmoid_pre)))
    ).astype(jnp.bfloat16)
    grad_up_pre = (grad_units * activated).astype(jnp.bfloat16)
    grad_in_rows = jnp.dot(
        grad_gate_pre, expert_in_l[:, :MODEL_WIDTH], preferred_element_type=jnp.float32
    )
    grad_in_rows = (
        grad_in_rows
        + jnp.dot(grad_up_pre, expert_in_l[:, MODEL_WIDTH:], preferred_element_type=jnp.float32)
    ).astype(jnp.bfloat16)
    grad_slots = trade_rows(grad_in_rows)
    out_grad = lax.dot_general(
        units, grad_rows, (((0,), (0,)), ((), ())), preferred_element_type=jnp.float32
    )
    gate_w_grad = lax.dot_general(
        grad_gate_pre, rows_here, (((0,), (0,)), ((), ())), preferred_element_type=jnp.float32
    )
    up_w_grad = lax.dot_general(
        grad_up_pre, rows_here, (((0,), (0,)), ((), ())), preferred_element_type=jnp.float32
    )
    in_grad = jnp.concatenate([scatter_expert(gate_w_grad), scatter_expert(up_w_grad)], axis=1)
    out_grad = scatter_expert(out_grad)
    grad_routed = grad_routed + jnp.dot(chosen, grad_slots, preferred_element_type=jnp.float32)
    gain_two_grad = jnp.sum(grad_routed * normed_two, axis=0)
    grad_h1 = grad_out + norm_back(
        grad_routed * gain_two.astype(jnp.float32), normed_two, inverse_two
    )
    return (grad_h1, router_grad, gain_two_grad, in_grad, out_grad)


def attend_backward(grad_h1, weights, live, allowed, cosine_table, sine_values, attn_stash):
    qkv_full, out_full, router_full, gain_one, gain_two = weights
    inverse, normed, normed_low, rotated_query, rotated_key, reduced_value, mixed_low = attn_stash
    token_total = grad_h1.shape[0]
    query_width = QUERY_HEADS * HEAD_SIZE
    key_value_width = KEY_VALUE_HEADS * HEAD_SIZE
    grad_low = grad_h1.astype(jnp.bfloat16)
    proj_grad = lax.dot_general(
        mixed_low, grad_low, (((0,), (0,)), ((), ())), preferred_element_type=jnp.float32
    )
    mixed_gradient = lax.dot_general(
        grad_low, out_full, (((1,), (1,)), ((), ())), preferred_element_type=jnp.float32
    ).astype(jnp.bfloat16)
    mixed_gradient = jnp.where(live[:, None] > 0.5, mixed_gradient, jnp.zeros_like(mixed_gradient))
    mixed_gradient = mixed_gradient.reshape(
        token_total, KEY_VALUE_HEADS, QUERY_HEADS // KEY_VALUE_HEADS, HEAD_SIZE
    )
    softmaxed = probabilities(rotated_query, rotated_key, allowed)
    grad_probs = jnp.einsum(
        "tkgd,ukd->kgtu", mixed_gradient, reduced_value, preferred_element_type=jnp.float32
    )
    grad_value = jnp.einsum(
        "kgtu,tkgd->ukd",
        softmaxed.astype(jnp.bfloat16),
        mixed_gradient,
        preferred_element_type=jnp.float32,
    )
    grad_scores = (
        softmaxed * (grad_probs - jnp.sum(softmaxed * grad_probs, axis=-1, keepdims=True))
    ).astype(jnp.bfloat16)
    grad_query = jnp.einsum(
        "kgtu,ukd->tkgd", grad_scores, rotated_key, preferred_element_type=jnp.float32
    ) * HEAD_SIZE ** (-0.5)
    grad_key = jnp.einsum(
        "kgtu,tkgd->ukd", grad_scores, rotated_query, preferred_element_type=jnp.float32
    ) * HEAD_SIZE ** (-0.5)
    grad_query = unrotate(
        rounded(grad_query.reshape(token_total, QUERY_HEADS, HEAD_SIZE)), cosine_table, sine_values
    ).astype(jnp.bfloat16)
    grad_key = unrotate(rounded(grad_key), cosine_table, sine_values).astype(jnp.bfloat16)
    grad_proj = jnp.concatenate(
        [
            grad_query.reshape(token_total, query_width),
            grad_key.reshape(token_total, key_value_width),
            grad_value.astype(jnp.bfloat16).reshape(token_total, key_value_width),
        ],
        axis=1,
    )
    qkv_grad = lax.dot_general(
        normed_low, grad_proj, (((0,), (0,)), ((), ())), preferred_element_type=jnp.float32
    )
    grad_normed = lax.dot_general(
        grad_proj, qkv_full, (((1,), (1,)), ((), ())), preferred_element_type=jnp.float32
    )
    gain_one_grad = jnp.sum(grad_normed * normed, axis=0)
    grad_input = grad_h1 + norm_back(grad_normed * gain_one.astype(jnp.float32), normed, inverse)
    return (grad_input, qkv_grad, proj_grad, gain_one_grad)


def on_device(
    hidden_in,
    cotangent,
    seq_lengths,
    seq_owner,
    routes,
    query_key_value_weight,
    out_weight,
    router_weight,
    gain_attn,
    gain_mlp,
    expert_in,
    expert_out,
):
    layers = range(LAYER_COUNT)
    device = lax.axis_index(AXES)
    dense = [
        sent_together(
            (
                query_key_value_weight[layer],
                out_weight[layer],
                router_weight[layer],
                gain_attn[layer],
                gain_mlp[layer],
            ),
            AXES,
            0,
            1,
        )
        for layer in layers
    ]
    experts_in = [gather_expert(expert_in[layer]) for layer in layers]
    experts_out = [gather_expert(expert_out[layer]) for layer in layers]
    position, live_row, allowed = seq_layout(seq_lengths, seq_owner, device)
    live = live_row.astype(jnp.float32)
    cosine_table, sine_values = rope_tables(position)
    routed, chosen = dispatch_table(routes, live_row)
    hidden = hidden_in.astype(jnp.float32)
    saved_layers = []
    for layer in layers:
        hidden, attn_stash = attend_forward(
            hidden, dense[layer], live, allowed, cosine_table, sine_values
        )
        hidden, expert_stash = expert_forward(
            hidden, dense[layer], experts_in[layer], experts_out[layer], live, routed, chosen
        )
        saved_layers.append((attn_stash, expert_stash))
    output_low = hidden.astype(jnp.bfloat16)
    grad_hidden = cotangent.astype(jnp.float32)
    layer_grads = [None] * LAYER_COUNT
    for layer in reversed(layers):
        attn_stash, expert_stash = saved_layers[layer]
        grad_hidden, router_grad, gain_two_grad, in_grad, out_grad = expert_backward(
            grad_hidden, dense[layer], experts_in[layer], experts_out[layer], chosen, expert_stash
        )
        grad_hidden, qkv_grad, proj_grad, gain_one_grad = attend_backward(
            grad_hidden, dense[layer], live, allowed, cosine_table, sine_values, attn_stash
        )
        small = jnp.concatenate(
            [
                router_grad,
                gain_one_grad[:, None],
                gain_two_grad[:, None],
                jnp.zeros((MODEL_WIDTH, 128 - E - 2), jnp.float32),
            ],
            axis=1,
        )
        small = scatter_dense(small)
        layer_grads[layer] = (
            scatter_dense(qkv_grad),
            scatter_dense(proj_grad),
            small[:, :E],
            small[:, E],
            small[:, E + 1],
            in_grad,
            out_grad,
        )
    stacked = tuple(
        jnp.stack([layer_grads[layer][member] for layer in layers]) for member in range(7)
    )
    return (output_low, grad_hidden) + stacked


def solution(mesh):
    grid = Mesh(mesh.devices.reshape(4, 4, 2, 2, 2), AXES)
    placed = (
        P(AXES, None),
        P(AXES, None),
        P(),
        P(),
        P(AXES, None),
        P(None, AXES, None),
        P(None, AXES, None),
        P(None, AXES, None),
        P(None, AXES),
        P(None, AXES),
        P(None, AXES, None),
        P(None, AXES, None),
    )
    return jax.shard_map(
        on_device,
        mesh=grid,
        in_specs=placed,
        out_specs=(
            P(AXES, None),
            P(AXES, None),
            P(None, AXES, None),
            P(None, AXES, None),
            P(None, AXES, None),
            P(None, AXES),
            P(None, AXES),
            P(None, AXES, None),
            P(None, AXES, None),
        ),
        check_vma=False,
    )
```

```python
import math

import jax
import jax.numpy as jnp
from jax import lax
from jax.sharding import Mesh, PartitionSpec as P

MODEL_WIDTH = 1024
QUERY_HEADS = 16
KEY_VALUE_HEADS = 8
HEAD_SIZE = 64
E = 32
TOPK = 8
LAYER_COUNT = 2
SEQ_DEV = 4
TOK_DEV = 128
CAP = 36


EPSILON = 1e-06
ROPE_BASE = 10000.0
MASKED = -1e30

ROOM = 40
ROWS = E * ROOM
AXES = ("x", "y", "zh", "zl", "c")
EXPERT_AXES = ("x", "y", "zh")
CHIP_AXES = ("x", "y", "zh", "zl")
SWAP = [(0, 1), (1, 0)]


def sent_together(arrays, axis, dim, along):
    widths = [math.prod(a.shape[along:]) for a in arrays]
    both = jnp.concatenate(
        [a.reshape(*a.shape[:along], w) for a, w in zip(arrays, widths)], axis=along
    )
    out = lax.all_gather(both, axis, axis=dim, tiled=True)
    pieces = jnp.split(out, [sum(widths[:k]) for k in range(1, len(widths))], axis=along)
    return tuple((b.reshape(*out.shape[:along], *a.shape[along:]) for a, b in zip(arrays, pieces)))


def seq_layout(seq_lengths, seq_owner, device):
    owned_seq = seq_owner == device
    ranking = jnp.cumsum(owned_seq.astype(jnp.int32)) - 1
    counter = jnp.arange(SEQ_DEV, dtype=jnp.int32)
    picker = (owned_seq[None, :] & (ranking[None, :] == counter[:, None])).astype(jnp.int32)
    own_lengths = jnp.sum(picker * seq_lengths[None, :], axis=1)
    seq_ends = jnp.cumsum(own_lengths)
    slot_ids = jnp.arange(TOK_DEV, dtype=jnp.int32)
    segment = jnp.sum((slot_ids[:, None] >= seq_ends[None, :]).astype(jnp.int32), axis=1)
    seq_starts = seq_ends - own_lengths
    first_slot = jnp.sum(
        jnp.where(segment[:, None] == counter[None, :], seq_starts[None, :], 0), axis=1
    )
    position = slot_ids - first_slot
    allowed = (segment[:, None] == segment[None, :]) & (slot_ids[:, None] >= slot_ids[None, :])
    return (position, segment < SEQ_DEV, allowed)


def rope_tables(position):
    half_size = HEAD_SIZE // 2
    exponent = jnp.arange(half_size, dtype=jnp.float32) * (2.0 / HEAD_SIZE)
    frequency = jnp.exp(-math.log(ROPE_BASE) * exponent)
    angles = position.astype(jnp.float32)[:, None] * frequency[None, :]
    return (jnp.cos(angles), jnp.sin(angles))


def apply_rotation(values, cosine_table, sine_values):
    half_size = values.shape[-1] // 2
    first_half = values[..., :half_size]
    second_half = values[..., half_size:]
    cos_wide = cosine_table[:, None, :]
    sin_wide = sine_values[:, None, :]
    return jnp.concatenate(
        [
            first_half * cos_wide - second_half * sin_wide,
            second_half * cos_wide + first_half * sin_wide,
        ],
        axis=-1,
    )


def unrotate(grad_rot, cosine_table, sine_values):
    half_size = grad_rot.shape[-1] // 2
    first_half = grad_rot[..., :half_size]
    second_half = grad_rot[..., half_size:]
    cos_wide = cosine_table[:, None, :]
    sin_wide = sine_values[:, None, :]
    return jnp.concatenate(
        [
            first_half * cos_wide + second_half * sin_wide,
            second_half * cos_wide - first_half * sin_wide,
        ],
        axis=-1,
    )


def rounded(values):
    return lax.optimization_barrier(values.astype(jnp.bfloat16)).astype(jnp.float32)


def dispatch_table(route_block, live_row):
    experts = jnp.arange(E, dtype=jnp.int32)
    routed = jnp.any(route_block[:, :, None] == experts[None, None, :], axis=1)
    hits = (routed & live_row[:, None]).astype(jnp.bfloat16)
    slot_ids = jnp.arange(TOK_DEV, dtype=jnp.int32)
    before = (slot_ids[None, :] < slot_ids[:, None]).astype(jnp.bfloat16)
    rank = jnp.dot(before, hits, preferred_element_type=jnp.float32)
    code = jnp.where(hits > 0, rank, -1.0).astype(jnp.bfloat16)
    spread = spread_table()
    wide = jnp.dot(code, spread, preferred_element_type=jnp.float32)
    place = (jnp.arange(ROWS, dtype=jnp.int32) % ROOM).astype(jnp.float32)
    chosen = (wide == place[None, :]).astype(jnp.bfloat16)
    return routed, chosen


def spread_table():
    rows = jnp.arange(ROWS, dtype=jnp.int32) // ROOM
    return (jnp.arange(E, dtype=jnp.int32)[:, None] == rows[None, :]).astype(jnp.bfloat16)


def trade_rows(rows):
    return lax.all_to_all(
        rows.reshape(E, ROOM, MODEL_WIDTH), EXPERT_AXES, split_axis=0, concat_axis=0, tiled=True
    ).reshape(ROWS, MODEL_WIDTH)


def gather_expert(own):
    pair = jnp.concatenate([own, lax.ppermute(own, "zl", SWAP)], axis=0)
    return jnp.concatenate([pair, lax.ppermute(pair, "c", SWAP)], axis=0)


def scatter_expert(grad):
    half = grad.shape[0] // 2
    quarter = half // 2
    kept, given = grad[:half], grad[half:].astype(jnp.bfloat16)
    kept = kept + lax.ppermute(given, "c", SWAP).astype(jnp.float32)
    own, other = kept[:quarter], kept[quarter:].astype(jnp.bfloat16)
    return own + lax.ppermute(other, "zl", SWAP).astype(jnp.float32)


def scatter_dense(grad):
    width = grad.shape[1]
    core = lax.axis_index("c")
    blocks = grad.reshape(64, 2, MODEL_WIDTH // 128, width)
    given = lax.dynamic_slice_in_dim(blocks, 1 - core, 1, axis=1).astype(jnp.bfloat16)
    kept = lax.dynamic_slice_in_dim(blocks, core, 1, axis=1)
    kept = kept + lax.ppermute(given, "c", SWAP).astype(jnp.float32)
    kept = kept.reshape(64, MODEL_WIDTH // 128, width).astype(jnp.bfloat16)
    parts = lax.all_to_all(kept, CHIP_AXES, split_axis=0, concat_axis=0, tiled=True)
    return jnp.sum(parts.astype(jnp.float32), axis=0)


def norm_back(grad_norm, normed, inverse):
    return inverse * (grad_norm - normed * jnp.mean(grad_norm * normed, axis=-1, keepdims=True))


def probabilities(rotated_query, rotated_key, allowed):
    scores = jnp.einsum(
        "tkgd,ukd->kgtu", rotated_query, rotated_key, preferred_element_type=jnp.float32
    ) * HEAD_SIZE ** (-0.5)
    scores = jnp.where(allowed[None, None], scores, MASKED)
    biggest = jnp.max(scores, axis=-1, keepdims=True)
    exp_scores = jnp.exp(scores - biggest)
    return exp_scores / jnp.sum(exp_scores, axis=-1, keepdims=True)


def attend_forward(hidden, weights, live, allowed, cosine_table, sine_values):
    qkv_full, out_full, router_full, gain_one, gain_two = weights
    token_total = hidden.shape[0]
    query_width = QUERY_HEADS * HEAD_SIZE
    key_value_width = KEY_VALUE_HEADS * HEAD_SIZE
    inverse = lax.rsqrt(jnp.mean(hidden * hidden, axis=-1, keepdims=True) + EPSILON)
    normed = hidden * inverse
    normed_low = (normed * gain_one.astype(jnp.float32)).astype(jnp.bfloat16)
    projected_rows = jnp.dot(normed_low, qkv_full, preferred_element_type=jnp.float32)
    rotated_query = apply_rotation(
        projected_rows[:, :query_width].reshape(token_total, QUERY_HEADS, HEAD_SIZE),
        cosine_table,
        sine_values,
    ).astype(jnp.bfloat16)
    rotated_query = rotated_query.reshape(
        token_total, KEY_VALUE_HEADS, QUERY_HEADS // KEY_VALUE_HEADS, HEAD_SIZE
    )
    rotated_key = apply_rotation(
        projected_rows[:, query_width : query_width + key_value_width].reshape(
            token_total, KEY_VALUE_HEADS, HEAD_SIZE
        ),
        cosine_table,
        sine_values,
    ).astype(jnp.bfloat16)
    reduced_value = (
        projected_rows[:, query_width + key_value_width :]
        .reshape(token_total, KEY_VALUE_HEADS, HEAD_SIZE)
        .astype(jnp.bfloat16)
    )
    softmaxed = probabilities(rotated_query, rotated_key, allowed)
    mixed = jnp.einsum(
        "kgtu,ukd->tkgd",
        softmaxed.astype(jnp.bfloat16),
        reduced_value,
        preferred_element_type=jnp.float32,
    )
    mixed_low = (mixed.reshape(token_total, query_width) * live[:, None]).astype(jnp.bfloat16)
    attn_out = jnp.dot(mixed_low, out_full, preferred_element_type=jnp.float32)
    return (
        hidden + attn_out,
        (inverse, normed, normed_low, rotated_query, rotated_key, reduced_value, mixed_low),
    )


def route_rows(hidden, weights, routed, chosen):
    qkv_full, out_full, router_full, gain_one, gain_two = weights
    inverse_two = lax.rsqrt(jnp.mean(hidden * hidden, axis=-1, keepdims=True) + EPSILON)
    normed_two = hidden * inverse_two
    routed_in = (normed_two * gain_two.astype(jnp.float32)).astype(jnp.bfloat16)
    rows = lax.dot_general(
        chosen, routed_in, (((0,), (0,)), ((), ())), preferred_element_type=jnp.float32
    ).astype(jnp.bfloat16)
    logits = jnp.dot(routed_in, router_full, preferred_element_type=jnp.float32)
    masked = jnp.where(routed, logits, MASKED)
    exp_chosen = jnp.where(routed, jnp.exp(masked - jnp.max(masked, axis=-1, keepdims=True)), 0.0)
    gate_prob = exp_chosen / jnp.sum(exp_chosen, axis=-1, keepdims=True)
    gate_wide = jnp.dot(
        gate_prob.astype(jnp.bfloat16), spread_table(), preferred_element_type=jnp.float32
    ).astype(jnp.bfloat16)
    return rows, (inverse_two, normed_two, routed_in, gate_prob, gate_wide * chosen)


def slot_gradients(grad_out, mixing):
    return lax.dot_general(
        mixing,
        grad_out.astype(jnp.bfloat16),
        (((0,), (0,)), ((), ())),
        preferred_element_type=jnp.float32,
    ).astype(jnp.bfloat16)


def feed_forward(rows_here, expert_in_l, expert_out_l):
    gate_pre = lax.dot_general(
        rows_here,
        expert_in_l[:, :MODEL_WIDTH],
        (((1,), (1,)), ((), ())),
        preferred_element_type=jnp.float32,
    )
    up_pre = lax.dot_general(
        rows_here,
        expert_in_l[:, MODEL_WIDTH:],
        (((1,), (1,)), ((), ())),
        preferred_element_type=jnp.float32,
    )
    units = (jax.nn.silu(gate_pre) * up_pre).astype(jnp.bfloat16)
    results = jnp.dot(units, expert_out_l, preferred_element_type=jnp.float32).astype(jnp.bfloat16)
    return results, (gate_pre, up_pre)


def feed_backward(grad_rows, rows_here, pre, expert_in_l, expert_out_l):
    gate_pre, up_pre = pre
    sigmoid_pre = jax.nn.sigmoid(gate_pre)
    activated = gate_pre * sigmoid_pre
    units = (activated * up_pre).astype(jnp.bfloat16)
    grad_units = lax.dot_general(
        grad_rows, expert_out_l, (((1,), (1,)), ((), ())), preferred_element_type=jnp.float32
    )
    grad_gate_pre = (
        grad_units * up_pre * (sigmoid_pre * (1.0 + gate_pre * (1.0 - sigmoid_pre)))
    ).astype(jnp.bfloat16)
    grad_up_pre = (grad_units * activated).astype(jnp.bfloat16)
    grad_in_rows = jnp.dot(
        grad_gate_pre, expert_in_l[:, :MODEL_WIDTH], preferred_element_type=jnp.float32
    )
    grad_in_rows = (
        grad_in_rows
        + jnp.dot(grad_up_pre, expert_in_l[:, MODEL_WIDTH:], preferred_element_type=jnp.float32)
    ).astype(jnp.bfloat16)
    out_grad = lax.dot_general(
        units, grad_rows, (((0,), (0,)), ((), ())), preferred_element_type=jnp.float32
    )
    gate_w_grad = lax.dot_general(
        grad_gate_pre, rows_here, (((0,), (0,)), ((), ())), preferred_element_type=jnp.float32
    )
    up_w_grad = lax.dot_general(
        grad_up_pre, rows_here, (((0,), (0,)), ((), ())), preferred_element_type=jnp.float32
    )
    return grad_in_rows, (gate_w_grad, up_w_grad, out_grad)


def route_backward(grad_out, weights, chosen, returned, stash):
    qkv_full, out_full, router_full, gain_one, gain_two = weights
    inverse_two, normed_two, routed_in, gate_prob, mixing = stash
    products = lax.dot_general(
        grad_out.astype(jnp.bfloat16),
        returned,
        (((1,), (1,)), ((), ())),
        preferred_element_type=jnp.float32,
    )
    grad_gate = lax.dot_general(
        products * chosen.astype(jnp.float32),
        spread_table().astype(jnp.float32),
        (((1,), (1,)), ((), ())),
        precision=lax.Precision.HIGHEST,
        preferred_element_type=jnp.float32,
    )
    grad_chosen = gate_prob * (grad_gate - jnp.sum(gate_prob * grad_gate, axis=-1, keepdims=True))
    grad_logits = grad_chosen.astype(jnp.bfloat16)
    router_grad = lax.dot_general(
        routed_in, grad_logits, (((0,), (0,)), ((), ())), preferred_element_type=jnp.float32
    )
    grad_routed = lax.dot_general(
        grad_logits, router_full, (((1,), (1,)), ((), ())), preferred_element_type=jnp.float32
    )
    return router_grad, grad_routed


def rows_backward(grad_out, weights, chosen, grad_slots, grad_routed, stash):
    qkv_full, out_full, router_full, gain_one, gain_two = weights
    inverse_two, normed_two, routed_in, gate_prob, mixing = stash
    grad_routed = grad_routed + jnp.dot(chosen, grad_slots, preferred_element_type=jnp.float32)
    gain_two_grad = jnp.sum(grad_routed * normed_two, axis=0)
    grad_h1 = grad_out + norm_back(
        grad_routed * gain_two.astype(jnp.float32), normed_two, inverse_two
    )
    return grad_h1, gain_two_grad


def attend_backward(grad_h1, weights, live, allowed, cosine_table, sine_values, attn_stash):
    qkv_full, out_full, router_full, gain_one, gain_two = weights
    inverse, normed, normed_low, rotated_query, rotated_key, reduced_value, mixed_low = attn_stash
    token_total = grad_h1.shape[0]
    query_width = QUERY_HEADS * HEAD_SIZE
    key_value_width = KEY_VALUE_HEADS * HEAD_SIZE
    grad_low = grad_h1.astype(jnp.bfloat16)
    proj_grad = lax.dot_general(
        mixed_low, grad_low, (((0,), (0,)), ((), ())), preferred_element_type=jnp.float32
    )
    mixed_gradient = lax.dot_general(
        grad_low, out_full, (((1,), (1,)), ((), ())), preferred_element_type=jnp.float32
    ).astype(jnp.bfloat16)
    mixed_gradient = jnp.where(live[:, None] > 0.5, mixed_gradient, jnp.zeros_like(mixed_gradient))
    mixed_gradient = mixed_gradient.reshape(
        token_total, KEY_VALUE_HEADS, QUERY_HEADS // KEY_VALUE_HEADS, HEAD_SIZE
    )
    softmaxed = probabilities(rotated_query, rotated_key, allowed)
    grad_probs = jnp.einsum(
        "tkgd,ukd->kgtu", mixed_gradient, reduced_value, preferred_element_type=jnp.float32
    )
    grad_value = jnp.einsum(
        "kgtu,tkgd->ukd",
        softmaxed.astype(jnp.bfloat16),
        mixed_gradient,
        preferred_element_type=jnp.float32,
    )
    grad_scores = (
        softmaxed * (grad_probs - jnp.sum(softmaxed * grad_probs, axis=-1, keepdims=True))
    ).astype(jnp.bfloat16)
    grad_query = jnp.einsum(
        "kgtu,ukd->tkgd", grad_scores, rotated_key, preferred_element_type=jnp.float32
    ) * HEAD_SIZE ** (-0.5)
    grad_key = jnp.einsum(
        "kgtu,tkgd->ukd", grad_scores, rotated_query, preferred_element_type=jnp.float32
    ) * HEAD_SIZE ** (-0.5)
    grad_query = unrotate(
        rounded(grad_query.reshape(token_total, QUERY_HEADS, HEAD_SIZE)), cosine_table, sine_values
    ).astype(jnp.bfloat16)
    grad_key = unrotate(rounded(grad_key), cosine_table, sine_values).astype(jnp.bfloat16)
    grad_proj = jnp.concatenate(
        [
            grad_query.reshape(token_total, query_width),
            grad_key.reshape(token_total, key_value_width),
            grad_value.astype(jnp.bfloat16).reshape(token_total, key_value_width),
        ],
        axis=1,
    )
    qkv_grad = lax.dot_general(
        normed_low, grad_proj, (((0,), (0,)), ((), ())), preferred_element_type=jnp.float32
    )
    grad_normed = lax.dot_general(
        grad_proj, qkv_full, (((1,), (1,)), ((), ())), preferred_element_type=jnp.float32
    )
    gain_one_grad = jnp.sum(grad_normed * normed, axis=0)
    grad_input = grad_h1 + norm_back(grad_normed * gain_one.astype(jnp.float32), normed, inverse)
    return (grad_input, qkv_grad, proj_grad, gain_one_grad)


def on_device(
    hidden_in,
    cotangent,
    seq_lengths,
    seq_owner,
    routes,
    query_key_value_weight,
    out_weight,
    router_weight,
    gain_attn,
    gain_mlp,
    expert_in,
    expert_out,
):
    layers = range(LAYER_COUNT)
    last = LAYER_COUNT - 1
    device = lax.axis_index(AXES)
    own_dense = [
        (
            query_key_value_weight[layer],
            out_weight[layer],
            router_weight[layer],
            gain_attn[layer],
            gain_mlp[layer],
        )
        for layer in layers
    ]
    experts = [
        (gather_expert(expert_in[layer]), gather_expert(expert_out[layer])) for layer in layers
    ]
    dense = []
    for layer in layers:
        dense.append(sent_together(own_dense[layer], AXES, 0, 1))
        if layer == 0:
            dense[0], experts, own_dense = lax.optimization_barrier((dense[0], experts, own_dense))
    position, live_row, allowed = seq_layout(seq_lengths, seq_owner, device)
    live = live_row.astype(jnp.float32)
    cosine_table, sine_values = rope_tables(position)
    routed, chosen = dispatch_table(routes, live_row)
    hidden = hidden_in.astype(jnp.float32)
    grad_hidden = cotangent.astype(jnp.float32)
    saved = []
    for layer in layers:
        hidden, attn_stash = attend_forward(
            hidden, dense[layer], live, allowed, cosine_table, sine_values
        )
        rows, route_stash = route_rows(hidden, dense[layer], routed, chosen)
        rows_here = trade_rows(rows)
        grad_rows = None
        if layer == last:
            slots = slot_gradients(grad_hidden, route_stash[-1])
            slots, rows_here = lax.optimization_barrier((slots, rows_here))
            grad_rows = trade_rows(slots)
        results, pre = feed_forward(rows_here, *experts[layer])
        returned = trade_rows(results)
        hidden = hidden + jnp.dot(route_stash[-1], returned, preferred_element_type=jnp.float32)
        saved.append((attn_stash, route_stash, rows_here, pre, returned, grad_rows))
    output_low = hidden.astype(jnp.bfloat16)
    layer_grads = [None] * LAYER_COUNT
    for layer in reversed(layers):
        attn_stash, route_stash, rows_here, pre, returned, grad_rows = saved[layer]
        if grad_rows is None:
            grad_rows = trade_rows(slot_gradients(grad_hidden, route_stash[-1]))
        grad_in_rows, expert_grads = feed_backward(grad_rows, rows_here, pre, *experts[layer])
        grad_slots = trade_rows(grad_in_rows)
        router_grad, grad_routed = route_backward(
            grad_hidden, dense[layer], chosen, returned, route_stash
        )
        grad_slots, expert_grads = lax.optimization_barrier((grad_slots, expert_grads))
        gate_w_grad, up_w_grad, out_grad = [scatter_expert(g) for g in expert_grads]
        grad_h1, gain_two_grad = rows_backward(
            grad_hidden, dense[layer], chosen, grad_slots, grad_routed, route_stash
        )
        grad_hidden, qkv_grad, proj_grad, gain_one_grad = attend_backward(
            grad_h1, dense[layer], live, allowed, cosine_table, sine_values, attn_stash
        )
        query_width = qkv_grad.shape[1]
        fill = jnp.zeros((MODEL_WIDTH, 128 - E - 2), jnp.float32)
        small = [router_grad, gain_one_grad[:, None], gain_two_grad[:, None], fill]
        if layer == last:
            done = scatter_dense(jnp.concatenate([qkv_grad, proj_grad] + small, axis=1))
            qkv_done, proj_done = done[:, :query_width], done[:, query_width:-128]
            small_done = done[:, -128:]
        else:
            proj_done = scatter_dense(proj_grad)
            done = scatter_dense(jnp.concatenate([qkv_grad] + small, axis=1))
            qkv_done, small_done = done[:, :query_width], done[:, -128:]
        layer_grads[layer] = (
            qkv_done,
            proj_done,
            small_done[:, :E],
            small_done[:, E],
            small_done[:, E + 1],
            jnp.concatenate([gate_w_grad, up_w_grad], axis=1),
            out_grad,
        )
    stacked = tuple(
        jnp.stack([layer_grads[layer][member] for layer in layers]) for member in range(7)
    )
    return (output_low, grad_hidden) + stacked


def solution(mesh):
    grid = Mesh(mesh.devices.reshape(4, 4, 2, 2, 2), AXES)
    placed = (
        P(AXES, None),
        P(AXES, None),
        P(),
        P(),
        P(AXES, None),
        P(None, AXES, None),
        P(None, AXES, None),
        P(None, AXES, None),
        P(None, AXES),
        P(None, AXES),
        P(None, AXES, None),
        P(None, AXES, None),
    )
    return jax.shard_map(
        on_device,
        mesh=grid,
        in_specs=placed,
        out_specs=(
            P(AXES, None),
            P(AXES, None),
            P(None, AXES, None),
            P(None, AXES, None),
            P(None, AXES, None),
            P(None, AXES),
            P(None, AXES),
            P(None, AXES, None),
            P(None, AXES, None),
        ),
        check_vma=False,
    )
```

```python
import math

import jax
import jax.numpy as jnp
from jax import lax
from jax.sharding import Mesh, PartitionSpec as P

MODEL_WIDTH = 1024
QUERY_HEADS = 16
KEY_VALUE_HEADS = 8
HEAD_SIZE = 64
E = 32
TOPK = 8
LAYER_COUNT = 2
SEQ_DEV = 4
TOK_DEV = 128
CAP = 36


EPSILON = 1e-06
ROPE_BASE = 10000.0
MASKED = -1e30

ROOM = 40
ROWS = E * ROOM
AXES = ("x", "y", "zh", "zl", "c")
EXPERT_AXES = ("x", "y", "zh")
CHIP_AXES = ("x", "y", "zh", "zl")
Z_AXES = ("zh", "zl")
PLANE_AXES = ("x", "y")
DENSE_WIDTHS = (2048, 1024, E, 1, 1)
HALF = MODEL_WIDTH // 2
SWAP = [(0, 1), (1, 0)]


def sent_together(arrays, axis):
    both = jnp.concatenate([a.reshape(a.shape[0], -1) for a in arrays], axis=1)
    return lax.all_gather(both, axis, axis=0, tiled=True)


def sent_by_chips(own):
    core = lax.axis_index("c")
    copies = jnp.broadcast_to(own[None], (64,) + own.shape)
    mine = lax.all_to_all(copies, CHIP_AXES, split_axis=0, concat_axis=0, tiled=True)
    other = lax.ppermute(mine, "c", SWAP)
    pair = [jnp.where(core == 0, mine, other), jnp.where(core == 0, other, mine)]
    return jnp.stack(pair, axis=1).reshape(MODEL_WIDTH, -1)


def cut_weights(gathered, widths):
    at, pieces = 0, []
    for width in widths:
        pieces.append(gathered[:, at : at + width])
        at += width
    return tuple(pieces[:-2]) + (pieces[-2][:, 0], pieces[-1][:, 0])


def seq_layout(seq_lengths, seq_owner, device):
    owned_seq = seq_owner == device
    ranking = jnp.cumsum(owned_seq.astype(jnp.int32)) - 1
    counter = jnp.arange(SEQ_DEV, dtype=jnp.int32)
    picker = (owned_seq[None, :] & (ranking[None, :] == counter[:, None])).astype(jnp.int32)
    own_lengths = jnp.sum(picker * seq_lengths[None, :], axis=1)
    seq_ends = jnp.cumsum(own_lengths)
    slot_ids = jnp.arange(TOK_DEV, dtype=jnp.int32)
    segment = jnp.sum((slot_ids[:, None] >= seq_ends[None, :]).astype(jnp.int32), axis=1)
    seq_starts = seq_ends - own_lengths
    first_slot = jnp.sum(
        jnp.where(segment[:, None] == counter[None, :], seq_starts[None, :], 0), axis=1
    )
    position = slot_ids - first_slot
    allowed = (segment[:, None] == segment[None, :]) & (slot_ids[:, None] >= slot_ids[None, :])
    return (position, segment < SEQ_DEV, allowed)


def rope_tables(position):
    half_size = HEAD_SIZE // 2
    exponent = jnp.arange(half_size, dtype=jnp.float32) * (2.0 / HEAD_SIZE)
    frequency = jnp.exp(-math.log(ROPE_BASE) * exponent)
    angles = position.astype(jnp.float32)[:, None] * frequency[None, :]
    return (jnp.cos(angles), jnp.sin(angles))


def apply_rotation(values, cosine_table, sine_values):
    half_size = values.shape[-1] // 2
    first_half = values[..., :half_size]
    second_half = values[..., half_size:]
    cos_wide = cosine_table[:, None, :]
    sin_wide = sine_values[:, None, :]
    return jnp.concatenate(
        [
            first_half * cos_wide - second_half * sin_wide,
            second_half * cos_wide + first_half * sin_wide,
        ],
        axis=-1,
    )


def unrotate(grad_rot, cosine_table, sine_values):
    half_size = grad_rot.shape[-1] // 2
    first_half = grad_rot[..., :half_size]
    second_half = grad_rot[..., half_size:]
    cos_wide = cosine_table[:, None, :]
    sin_wide = sine_values[:, None, :]
    return jnp.concatenate(
        [
            first_half * cos_wide + second_half * sin_wide,
            second_half * cos_wide - first_half * sin_wide,
        ],
        axis=-1,
    )


def rounded(values):
    return lax.optimization_barrier(values.astype(jnp.bfloat16)).astype(jnp.float32)


def dispatch_table(route_block, live_row):
    experts = jnp.arange(E, dtype=jnp.int32)
    routed = jnp.any(route_block[:, :, None] == experts[None, None, :], axis=1)
    hits = (routed & live_row[:, None]).astype(jnp.bfloat16)
    slot_ids = jnp.arange(TOK_DEV, dtype=jnp.int32)
    before = (slot_ids[None, :] < slot_ids[:, None]).astype(jnp.bfloat16)
    rank = jnp.dot(before, hits, preferred_element_type=jnp.float32)
    code = jnp.where(hits > 0, rank, -1.0).astype(jnp.bfloat16)
    spread = spread_table()
    wide = jnp.dot(code, spread, preferred_element_type=jnp.float32)
    place = (jnp.arange(ROWS, dtype=jnp.int32) % ROOM).astype(jnp.float32)
    chosen = (wide == place[None, :]).astype(jnp.bfloat16)
    return routed, chosen


def spread_table():
    rows = jnp.arange(ROWS, dtype=jnp.int32) // ROOM
    return (jnp.arange(E, dtype=jnp.int32)[:, None] == rows[None, :]).astype(jnp.bfloat16)


def trade_rows(rows):
    return lax.all_to_all(
        rows.reshape(E, ROOM, MODEL_WIDTH), EXPERT_AXES, split_axis=0, concat_axis=0, tiled=True
    ).reshape(ROWS, MODEL_WIDTH)


def gather_expert(own):
    pair = jnp.concatenate([own, lax.ppermute(own, "zl", SWAP)], axis=0)
    return jnp.concatenate([pair, lax.ppermute(pair, "c", SWAP)], axis=0)


def scatter_expert(grad):
    half = grad.shape[0] // 2
    quarter = half // 2
    kept, given = grad[:half], grad[half:].astype(jnp.bfloat16)
    kept = kept + lax.ppermute(given, "c", SWAP).astype(jnp.float32)
    own, other = kept[:quarter], kept[quarter:].astype(jnp.bfloat16)
    return own + lax.ppermute(other, "zl", SWAP).astype(jnp.float32)


def order_table():
    at = jnp.arange(MODEL_WIDTH, dtype=jnp.int32)
    core = (at // HALF + lax.axis_index("c")) % 2
    depth, plane, row = at // 128 % 4, at // 8 % 16, at % 8
    source = (plane * 4 + depth) * 16 + core * 8 + row
    return (at[:, None] == source[None, :]).astype(jnp.bfloat16)


def reorder(values, order):
    return jnp.dot(values, order, preferred_element_type=jnp.float32).astype(jnp.bfloat16)


def weight_halves(left, right):
    pair = (((0,), (0,)), ((), ()))
    kept = lax.dot_general(left[:, :HALF], right, pair, preferred_element_type=jnp.float32)
    given = lax.dot_general(left[:, HALF:], right, pair, preferred_element_type=jnp.float32)
    return kept, given.astype(jnp.bfloat16)


def small_halves(router_grad, gain_one_grad, gain_two_grad, order):
    fill = jnp.zeros((MODEL_WIDTH, 128 - E - 2), jnp.float32)
    small = jnp.concatenate(
        [router_grad, gain_one_grad[:, None], gain_two_grad[:, None], fill], axis=1
    ).astype(jnp.bfloat16)
    moved = lax.dot_general(
        order, small, (((0,), (0,)), ((), ())), preferred_element_type=jnp.float32
    )
    return moved[:HALF], moved[HALF:].astype(jnp.bfloat16)


def core_sum(halves):
    kept, given = halves
    return (kept + lax.ppermute(given, "c", SWAP).astype(jnp.float32)).astype(jnp.bfloat16)


def chip_sum(parts):
    parts = parts.reshape(64, 8, -1)
    parts = lax.all_to_all(parts, Z_AXES + PLANE_AXES, split_axis=0, concat_axis=0, tiled=True)
    return jnp.sum(parts.astype(jnp.float32), axis=0)


def chip_sum_aside(parts):
    parts = lax.psum_scatter(parts, Z_AXES, scatter_dimension=0, tiled=True)
    return lax.psum_scatter(parts, PLANE_AXES, scatter_dimension=0, tiled=True).astype(jnp.float32)


def norm_back(grad_norm, normed, inverse):
    return inverse * (grad_norm - normed * jnp.mean(grad_norm * normed, axis=-1, keepdims=True))


def probabilities(rotated_query, rotated_key, allowed):
    scores = jnp.einsum(
        "tkgd,ukd->kgtu", rotated_query, rotated_key, preferred_element_type=jnp.float32
    ) * HEAD_SIZE ** (-0.5)
    scores = jnp.where(allowed[None, None], scores, MASKED)
    biggest = jnp.max(scores, axis=-1, keepdims=True)
    exp_scores = jnp.exp(scores - biggest)
    return exp_scores / jnp.sum(exp_scores, axis=-1, keepdims=True)


def attend_forward(hidden, qkv_full, gain_one, live, allowed, cosine_table, sine_values):
    token_total = hidden.shape[0]
    query_width = QUERY_HEADS * HEAD_SIZE
    key_value_width = KEY_VALUE_HEADS * HEAD_SIZE
    inverse = lax.rsqrt(jnp.mean(hidden * hidden, axis=-1, keepdims=True) + EPSILON)
    normed = hidden * inverse
    normed_low = (normed * gain_one.astype(jnp.float32)).astype(jnp.bfloat16)
    projected_rows = jnp.dot(normed_low, qkv_full, preferred_element_type=jnp.float32)
    rotated_query = apply_rotation(
        projected_rows[:, :query_width].reshape(token_total, QUERY_HEADS, HEAD_SIZE),
        cosine_table,
        sine_values,
    ).astype(jnp.bfloat16)
    rotated_query = rotated_query.reshape(
        token_total, KEY_VALUE_HEADS, QUERY_HEADS // KEY_VALUE_HEADS, HEAD_SIZE
    )
    rotated_key = apply_rotation(
        projected_rows[:, query_width : query_width + key_value_width].reshape(
            token_total, KEY_VALUE_HEADS, HEAD_SIZE
        ),
        cosine_table,
        sine_values,
    ).astype(jnp.bfloat16)
    reduced_value = (
        projected_rows[:, query_width + key_value_width :]
        .reshape(token_total, KEY_VALUE_HEADS, HEAD_SIZE)
        .astype(jnp.bfloat16)
    )
    softmaxed = probabilities(rotated_query, rotated_key, allowed)
    mixed = jnp.einsum(
        "kgtu,ukd->tkgd",
        softmaxed.astype(jnp.bfloat16),
        reduced_value,
        preferred_element_type=jnp.float32,
    )
    mixed_low = (mixed.reshape(token_total, query_width) * live[:, None]).astype(jnp.bfloat16)
    return inverse, normed, normed_low, rotated_query, rotated_key, reduced_value, mixed_low


def route_rows(hidden, weights, routed, chosen):
    qkv_full, out_full, router_full, gain_one, gain_two = weights
    inverse_two = lax.rsqrt(jnp.mean(hidden * hidden, axis=-1, keepdims=True) + EPSILON)
    normed_two = hidden * inverse_two
    routed_in = (normed_two * gain_two.astype(jnp.float32)).astype(jnp.bfloat16)
    rows = lax.dot_general(
        chosen, routed_in, (((0,), (0,)), ((), ())), preferred_element_type=jnp.float32
    ).astype(jnp.bfloat16)
    logits = jnp.dot(routed_in, router_full, preferred_element_type=jnp.float32)
    masked = jnp.where(routed, logits, MASKED)
    exp_chosen = jnp.where(routed, jnp.exp(masked - jnp.max(masked, axis=-1, keepdims=True)), 0.0)
    gate_prob = exp_chosen / jnp.sum(exp_chosen, axis=-1, keepdims=True)
    gate_wide = jnp.dot(
        gate_prob.astype(jnp.bfloat16), spread_table(), preferred_element_type=jnp.float32
    ).astype(jnp.bfloat16)
    return rows, (inverse_two, normed_two, routed_in, gate_prob, gate_wide * chosen)


def slot_gradients(grad_out, mixing):
    return lax.dot_general(
        mixing,
        grad_out.astype(jnp.bfloat16),
        (((0,), (0,)), ((), ())),
        preferred_element_type=jnp.float32,
    ).astype(jnp.bfloat16)


def feed_forward(rows_here, expert_in_l, expert_out_l):
    gate_pre = lax.dot_general(
        rows_here,
        expert_in_l[:, :MODEL_WIDTH],
        (((1,), (1,)), ((), ())),
        preferred_element_type=jnp.float32,
    )
    up_pre = lax.dot_general(
        rows_here,
        expert_in_l[:, MODEL_WIDTH:],
        (((1,), (1,)), ((), ())),
        preferred_element_type=jnp.float32,
    )
    units = (jax.nn.silu(gate_pre) * up_pre).astype(jnp.bfloat16)
    results = jnp.dot(units, expert_out_l, preferred_element_type=jnp.float32).astype(jnp.bfloat16)
    return results, (gate_pre, up_pre)


def feed_backward(grad_rows, rows_here, pre, expert_in_l, expert_out_l):
    gate_pre, up_pre = pre
    sigmoid_pre = jax.nn.sigmoid(gate_pre)
    activated = gate_pre * sigmoid_pre
    units = (activated * up_pre).astype(jnp.bfloat16)
    grad_units = lax.dot_general(
        grad_rows, expert_out_l, (((1,), (1,)), ((), ())), preferred_element_type=jnp.float32
    )
    grad_gate_pre = (
        grad_units * up_pre * (sigmoid_pre * (1.0 + gate_pre * (1.0 - sigmoid_pre)))
    ).astype(jnp.bfloat16)
    grad_up_pre = (grad_units * activated).astype(jnp.bfloat16)
    grad_in_rows = jnp.dot(
        grad_gate_pre, expert_in_l[:, :MODEL_WIDTH], preferred_element_type=jnp.float32
    )
    grad_in_rows = (
        grad_in_rows
        + jnp.dot(grad_up_pre, expert_in_l[:, MODEL_WIDTH:], preferred_element_type=jnp.float32)
    ).astype(jnp.bfloat16)
    out_grad = lax.dot_general(
        units, grad_rows, (((0,), (0,)), ((), ())), preferred_element_type=jnp.float32
    )
    gate_w_grad = lax.dot_general(
        grad_gate_pre, rows_here, (((0,), (0,)), ((), ())), preferred_element_type=jnp.float32
    )
    up_w_grad = lax.dot_general(
        grad_up_pre, rows_here, (((0,), (0,)), ((), ())), preferred_element_type=jnp.float32
    )
    return grad_in_rows, (gate_w_grad, up_w_grad, out_grad)


def route_backward(grad_out, weights, chosen, returned, stash):
    qkv_full, out_full, router_full, gain_one, gain_two = weights
    inverse_two, normed_two, routed_in, gate_prob, mixing = stash
    products = lax.dot_general(
        grad_out.astype(jnp.bfloat16),
        returned,
        (((1,), (1,)), ((), ())),
        preferred_element_type=jnp.float32,
    )
    grad_gate = lax.dot_general(
        products * chosen.astype(jnp.float32),
        spread_table().astype(jnp.float32),
        (((1,), (1,)), ((), ())),
        precision=lax.Precision.HIGHEST,
        preferred_element_type=jnp.float32,
    )
    grad_chosen = gate_prob * (grad_gate - jnp.sum(gate_prob * grad_gate, axis=-1, keepdims=True))
    grad_logits = grad_chosen.astype(jnp.bfloat16)
    router_grad = lax.dot_general(
        routed_in, grad_logits, (((0,), (0,)), ((), ())), preferred_element_type=jnp.float32
    )
    grad_routed = lax.dot_general(
        grad_logits, router_full, (((1,), (1,)), ((), ())), preferred_element_type=jnp.float32
    )
    return router_grad, grad_routed


def rows_backward(grad_out, weights, chosen, grad_slots, grad_routed, stash):
    qkv_full, out_full, router_full, gain_one, gain_two = weights
    inverse_two, normed_two, routed_in, gate_prob, mixing = stash
    grad_routed = grad_routed + jnp.dot(chosen, grad_slots, preferred_element_type=jnp.float32)
    gain_two_grad = jnp.sum(grad_routed * normed_two, axis=0)
    grad_h1 = grad_out + norm_back(
        grad_routed * gain_two.astype(jnp.float32), normed_two, inverse_two
    )
    return grad_h1, gain_two_grad


def attend_backward(
    grad_h1, weights, live, allowed, cosine_table, sine_values, attn_stash, attn_moved, mixed_moved
):
    qkv_full, out_full, router_full, gain_one, gain_two = weights
    inverse, normed, normed_low, rotated_query, rotated_key, reduced_value, mixed_low = attn_stash
    token_total = grad_h1.shape[0]
    query_width = QUERY_HEADS * HEAD_SIZE
    key_value_width = KEY_VALUE_HEADS * HEAD_SIZE
    grad_low = grad_h1.astype(jnp.bfloat16)
    proj_halves = weight_halves(mixed_moved, grad_low)
    mixed_gradient = lax.dot_general(
        grad_low, out_full, (((1,), (1,)), ((), ())), preferred_element_type=jnp.float32
    ).astype(jnp.bfloat16)
    mixed_gradient = jnp.where(live[:, None] > 0.5, mixed_gradient, jnp.zeros_like(mixed_gradient))
    mixed_gradient = mixed_gradient.reshape(
        token_total, KEY_VALUE_HEADS, QUERY_HEADS // KEY_VALUE_HEADS, HEAD_SIZE
    )
    softmaxed = probabilities(rotated_query, rotated_key, allowed)
    grad_probs = jnp.einsum(
        "tkgd,ukd->kgtu", mixed_gradient, reduced_value, preferred_element_type=jnp.float32
    )
    grad_value = jnp.einsum(
        "kgtu,tkgd->ukd",
        softmaxed.astype(jnp.bfloat16),
        mixed_gradient,
        preferred_element_type=jnp.float32,
    )
    grad_scores = (
        softmaxed * (grad_probs - jnp.sum(softmaxed * grad_probs, axis=-1, keepdims=True))
    ).astype(jnp.bfloat16)
    grad_query = jnp.einsum(
        "kgtu,ukd->tkgd", grad_scores, rotated_key, preferred_element_type=jnp.float32
    ) * HEAD_SIZE ** (-0.5)
    grad_key = jnp.einsum(
        "kgtu,tkgd->ukd", grad_scores, rotated_query, preferred_element_type=jnp.float32
    ) * HEAD_SIZE ** (-0.5)
    grad_query = unrotate(
        rounded(grad_query.reshape(token_total, QUERY_HEADS, HEAD_SIZE)), cosine_table, sine_values
    ).astype(jnp.bfloat16)
    grad_key = unrotate(rounded(grad_key), cosine_table, sine_values).astype(jnp.bfloat16)
    grad_proj = jnp.concatenate(
        [
            grad_query.reshape(token_total, query_width),
            grad_key.reshape(token_total, key_value_width),
            grad_value.astype(jnp.bfloat16).reshape(token_total, key_value_width),
        ],
        axis=1,
    )
    qkv_halves = weight_halves(attn_moved, grad_proj)
    grad_normed = lax.dot_general(
        grad_proj, qkv_full, (((1,), (1,)), ((), ())), preferred_element_type=jnp.float32
    )
    gain_one_grad = jnp.sum(grad_normed * normed, axis=0)
    grad_input = grad_h1 + norm_back(grad_normed * gain_one.astype(jnp.float32), normed, inverse)
    return (grad_input, qkv_halves, proj_halves, gain_one_grad)


def on_device(
    hidden_in,
    cotangent,
    seq_lengths,
    seq_owner,
    routes,
    query_key_value_weight,
    out_weight,
    router_weight,
    gain_attn,
    gain_mlp,
    expert_in,
    expert_out,
):
    layers = range(LAYER_COUNT)
    last = LAYER_COUNT - 1
    device = lax.axis_index(AXES)
    order = order_table()
    own_dense = [
        (
            query_key_value_weight[layer],
            out_weight[layer],
            router_weight[layer],
            gain_attn[layer],
            gain_mlp[layer],
        )
        for layer in layers
    ]
    lead = [own_dense[0][member].reshape(8, -1) for member in (0, 2, 3, 4)]
    fill = jnp.zeros((8, 128 - E - 2), jnp.bfloat16)
    lead_first = sent_by_chips(jnp.concatenate(lead + [fill], axis=1))
    lead_first, out_own, expert_in, expert_out = lax.optimization_barrier(
        (lead_first, own_dense[0][1], expert_in, expert_out)
    )
    lead_first = cut_weights(lead_first, (2048, E, 1, 1))
    out_first = sent_by_chips(out_own)
    dense = [(lead_first[0], out_first) + lead_first[1:], None]
    experts = [
        (gather_expert(expert_in[layer]), gather_expert(expert_out[layer])) for layer in layers
    ]
    position, live_row, allowed = seq_layout(seq_lengths, seq_owner, device)
    live = live_row.astype(jnp.float32)
    cosine_table, sine_values = rope_tables(position)
    routed, chosen = dispatch_table(routes, live_row)
    hidden = hidden_in.astype(jnp.float32)
    grad_hidden = cotangent.astype(jnp.float32)
    saved = []
    for layer in layers:
        attn_stash = attend_forward(
            hidden, dense[layer][0], dense[layer][3], live, allowed, cosine_table, sine_values
        )
        mixed_low = attn_stash[-1]
        hidden = hidden + jnp.dot(mixed_low, dense[layer][1], preferred_element_type=jnp.float32)
        rows, route_stash = route_rows(hidden, dense[layer], routed, chosen)
        if layer == 0:
            rows, experts, own_dense = lax.optimization_barrier((rows, experts, own_dense))
            dense[1] = cut_weights(sent_together(own_dense[1], AXES), DENSE_WIDTHS)
        rows_here = trade_rows(rows)
        moved = reorder(attn_stash[2], order), reorder(mixed_low, order)
        grad_rows = None
        if layer == last:
            slots = slot_gradients(grad_hidden, route_stash[-1])
            slots, rows_here = lax.optimization_barrier((slots, rows_here))
            grad_rows = trade_rows(slots)
        results, pre = feed_forward(rows_here, *experts[layer])
        if layer == last:
            results, grad_rows = lax.optimization_barrier((results, grad_rows))
        returned = trade_rows(results)
        hidden = hidden + jnp.dot(route_stash[-1], returned, preferred_element_type=jnp.float32)
        saved.append((attn_stash, moved, route_stash, rows_here, pre, returned, grad_rows))
    output_low = hidden.astype(jnp.bfloat16)
    layer_grads = [None] * LAYER_COUNT
    after = ()
    for layer in reversed(layers):
        attn_stash, moved, route_stash, rows_here, pre, returned, grad_rows = saved[layer]
        if grad_rows is None:
            slots = slot_gradients(grad_hidden, route_stash[-1])
            slots, after = lax.optimization_barrier((slots, after))
            grad_rows = trade_rows(slots)
        grad_in_rows, expert_grads = feed_backward(grad_rows, rows_here, pre, *experts[layer])
        grad_slots = trade_rows(grad_in_rows)
        router_grad, grad_routed = route_backward(
            grad_hidden, dense[layer], chosen, returned, route_stash
        )
        grad_slots, expert_grads = lax.optimization_barrier((grad_slots, expert_grads))
        expert_grads = [scatter_expert(g) for g in expert_grads]
        grad_h1, gain_two_grad = rows_backward(
            grad_hidden, dense[layer], chosen, grad_slots, grad_routed, route_stash
        )
        grad_hidden, qkv_halves, proj_halves, gain_one_grad = attend_backward(
            grad_h1, dense[layer], live, allowed, cosine_table, sine_values, attn_stash, *moved
        )
        small = small_halves(router_grad, gain_one_grad, gain_two_grad, order)
        if layer == last:
            after = expert_grads
            sums = [core_sum(halves) for halves in (qkv_halves, proj_halves, small)]
            done = chip_sum_aside(jnp.concatenate(sums, axis=1))
            proj_done, done = done[:, 2048:3072], jnp.concatenate(
                [done[:, :2048], done[:, 3072:]], axis=1
            )
        else:
            proj_done = chip_sum(core_sum(proj_halves))
            sums = [core_sum(halves) for halves in (qkv_halves, small)]
            done = chip_sum(jnp.concatenate(sums, axis=1))
        qkv_done, small_done = done[:, :2048], done[:, 2048:]
        layer_grads[layer] = (
            qkv_done,
            proj_done,
            small_done[:, :E],
            small_done[:, E],
            small_done[:, E + 1],
            expert_grads,
        )
    stacked = [
        jnp.stack([layer_grads[layer][member] for layer in layers]) for member in range(5)
    ]
    grads = [layer_grads[0][5], after]
    stacked.append(jnp.stack([jnp.concatenate(g[:2], axis=1) for g in grads]))
    stacked.append(jnp.stack([g[2] for g in grads]))
    return (output_low, grad_hidden) + tuple(stacked)


def solution(mesh):
    grid = Mesh(mesh.devices.reshape(4, 4, 2, 2, 2), AXES)
    placed = (
        P(AXES, None),
        P(AXES, None),
        P(),
        P(),
        P(AXES, None),
        P(None, AXES, None),
        P(None, AXES, None),
        P(None, AXES, None),
        P(None, AXES),
        P(None, AXES),
        P(None, AXES, None),
        P(None, AXES, None),
    )
    return jax.shard_map(
        on_device,
        mesh=grid,
        in_specs=placed,
        out_specs=(
            P(AXES, None),
            P(AXES, None),
            P(None, AXES, None),
            P(None, AXES, None),
            P(None, AXES, None),
            P(None, AXES),
            P(None, AXES),
            P(None, AXES, None),
            P(None, AXES, None),
        ),
        check_vma=False,
    )
```

```python
import math

import jax
import jax.numpy as jnp
from jax import lax
from jax.sharding import Mesh, PartitionSpec as P

MODEL_WIDTH = 1024
QUERY_HEADS = 16
KEY_VALUE_HEADS = 8
HEAD_SIZE = 64
E = 32
TOPK = 8
LAYER_COUNT = 2
SEQ_DEV = 4
TOK_DEV = 128
CAP = 36


EPSILON = 1e-06
ROPE_BASE = 10000.0
MASKED = -1e30

ROOM = 40
ROWS = E * ROOM
AXES = ("x", "y", "zh", "zl", "c")
EXPERT_AXES = ("x", "y", "zh")
CHIP_AXES = ("x", "y", "zh", "zl")
Z_AXES = ("zh", "zl")
GROUP_AXES = ("zl", "c")
DENSE_WIDTHS = (2048, 1024, E, 1, 1)
HALF = MODEL_WIDTH // 2
SWAP = [(0, 1), (1, 0)]


def sent_together(arrays, axis):
    both = jnp.concatenate([a.reshape(a.shape[0], -1) for a in arrays], axis=1)
    return lax.all_gather(both, axis, axis=0, tiled=True)


def sent_by_chips(own):
    core = lax.axis_index("c")
    copies = jnp.broadcast_to(own[None], (64,) + own.shape)
    mine = lax.all_to_all(copies, CHIP_AXES, split_axis=0, concat_axis=0, tiled=True)
    other = lax.ppermute(mine, "c", SWAP)
    pair = [jnp.where(core == 0, mine, other), jnp.where(core == 0, other, mine)]
    return jnp.stack(pair, axis=1).reshape(MODEL_WIDTH, -1)


def cut_weights(gathered, widths):
    at, pieces = 0, []
    for width in widths:
        pieces.append(gathered[:, at : at + width])
        at += width
    return tuple(pieces[:-2]) + (pieces[-2][:, 0], pieces[-1][:, 0])


def seq_layout(seq_lengths, seq_owner, device):
    owned_seq = seq_owner == device
    ranking = jnp.cumsum(owned_seq.astype(jnp.int32)) - 1
    counter = jnp.arange(SEQ_DEV, dtype=jnp.int32)
    picker = (owned_seq[None, :] & (ranking[None, :] == counter[:, None])).astype(jnp.int32)
    own_lengths = jnp.sum(picker * seq_lengths[None, :], axis=1)
    seq_ends = jnp.cumsum(own_lengths)
    slot_ids = jnp.arange(TOK_DEV, dtype=jnp.int32)
    segment = jnp.sum((slot_ids[:, None] >= seq_ends[None, :]).astype(jnp.int32), axis=1)
    seq_starts = seq_ends - own_lengths
    first_slot = jnp.sum(
        jnp.where(segment[:, None] == counter[None, :], seq_starts[None, :], 0), axis=1
    )
    position = slot_ids - first_slot
    allowed = (segment[:, None] == segment[None, :]) & (slot_ids[:, None] >= slot_ids[None, :])
    return (position, segment < SEQ_DEV, allowed)


def rope_tables(position):
    half_size = HEAD_SIZE // 2
    exponent = jnp.arange(half_size, dtype=jnp.float32) * (2.0 / HEAD_SIZE)
    frequency = jnp.exp(-math.log(ROPE_BASE) * exponent)
    angles = position.astype(jnp.float32)[:, None] * frequency[None, :]
    return (jnp.cos(angles), jnp.sin(angles))


def apply_rotation(values, cosine_table, sine_values):
    half_size = values.shape[-1] // 2
    first_half = values[..., :half_size]
    second_half = values[..., half_size:]
    cos_wide = cosine_table[:, None, :]
    sin_wide = sine_values[:, None, :]
    return jnp.concatenate(
        [
            first_half * cos_wide - second_half * sin_wide,
            second_half * cos_wide + first_half * sin_wide,
        ],
        axis=-1,
    )


def unrotate(grad_rot, cosine_table, sine_values):
    half_size = grad_rot.shape[-1] // 2
    first_half = grad_rot[..., :half_size]
    second_half = grad_rot[..., half_size:]
    cos_wide = cosine_table[:, None, :]
    sin_wide = sine_values[:, None, :]
    return jnp.concatenate(
        [
            first_half * cos_wide + second_half * sin_wide,
            second_half * cos_wide - first_half * sin_wide,
        ],
        axis=-1,
    )


def rounded(values):
    return lax.optimization_barrier(values.astype(jnp.bfloat16)).astype(jnp.float32)


def dispatch_table(route_block, live_row):
    experts = jnp.arange(E, dtype=jnp.int32)
    routed = jnp.any(route_block[:, :, None] == experts[None, None, :], axis=1)
    hits = (routed & live_row[:, None]).astype(jnp.bfloat16)
    slot_ids = jnp.arange(TOK_DEV, dtype=jnp.int32)
    before = (slot_ids[None, :] < slot_ids[:, None]).astype(jnp.bfloat16)
    rank = jnp.dot(before, hits, preferred_element_type=jnp.float32)
    code = jnp.where(hits > 0, rank, -1.0).astype(jnp.bfloat16)
    spread = spread_table()
    wide = jnp.dot(code, spread, preferred_element_type=jnp.float32)
    place = (jnp.arange(ROWS, dtype=jnp.int32) % ROOM).astype(jnp.float32)
    chosen = (wide == place[None, :]).astype(jnp.bfloat16)
    return routed, chosen


def spread_table():
    rows = jnp.arange(ROWS, dtype=jnp.int32) // ROOM
    return (jnp.arange(E, dtype=jnp.int32)[:, None] == rows[None, :]).astype(jnp.bfloat16)


def trade_rows(rows):
    return lax.all_to_all(
        rows.reshape(E, ROOM, MODEL_WIDTH), EXPERT_AXES, split_axis=0, concat_axis=0, tiled=True
    ).reshape(ROWS, MODEL_WIDTH)


def gather_expert(own_in, own_out):
    both = jnp.concatenate([own_in, own_out], axis=1)
    return lax.all_gather(both, GROUP_AXES, axis=0, tiled=True)


def scatter_expert(grads):
    both = jnp.concatenate(grads, axis=1).astype(jnp.bfloat16)
    return lax.psum_scatter(both, GROUP_AXES, scatter_dimension=0, tiled=True)


def order_table():
    at = jnp.arange(MODEL_WIDTH, dtype=jnp.int32)
    core = (at // HALF + lax.axis_index("c")) % 2
    depth, plane, row = at // 128 % 4, at // 8 % 16, at % 8
    source = (plane * 4 + depth) * 16 + core * 8 + row
    return (at[:, None] == source[None, :]).astype(jnp.bfloat16)


def reorder(values, order):
    return jnp.dot(values, order, preferred_element_type=jnp.float32).astype(jnp.bfloat16)


def weight_halves(left, right):
    pair = (((0,), (0,)), ((), ()))
    kept = lax.dot_general(left[:, :HALF], right, pair, preferred_element_type=jnp.float32)
    given = lax.dot_general(left[:, HALF:], right, pair, preferred_element_type=jnp.float32)
    return kept, given.astype(jnp.bfloat16)


def small_halves(router_grad, gain_one_grad, gain_two_grad, order):
    fill = jnp.zeros((MODEL_WIDTH, 128 - E - 2), jnp.float32)
    small = jnp.concatenate(
        [router_grad, gain_one_grad[:, None], gain_two_grad[:, None], fill], axis=1
    ).astype(jnp.bfloat16)
    moved = lax.dot_general(
        order, small, (((0,), (0,)), ((), ())), preferred_element_type=jnp.float32
    )
    return moved[:HALF], moved[HALF:].astype(jnp.bfloat16)


def core_sum(halves):
    kept, given = halves
    return (kept + lax.ppermute(given, "c", SWAP).astype(jnp.float32)).astype(jnp.bfloat16)


def chip_sum(parts):
    parts = parts.reshape(64, 8, -1)
    parts = lax.all_to_all(parts, Z_AXES + ("x", "y"), split_axis=0, concat_axis=0, tiled=True)
    return jnp.sum(parts.astype(jnp.float32), axis=0)


def chip_sum_aside(parts):
    parts = lax.psum_scatter(parts, Z_AXES, scatter_dimension=0, tiled=True)
    parts = lax.psum_scatter(parts, "x", scatter_dimension=0, tiled=True)
    return lax.psum_scatter(parts, "y", scatter_dimension=0, tiled=True).astype(jnp.float32)


def norm_back(grad_norm, normed, inverse):
    return inverse * (grad_norm - normed * jnp.mean(grad_norm * normed, axis=-1, keepdims=True))


def probabilities(rotated_query, rotated_key, allowed):
    scores = jnp.einsum(
        "tkgd,ukd->kgtu", rotated_query, rotated_key, preferred_element_type=jnp.float32
    ) * HEAD_SIZE ** (-0.5)
    scores = jnp.where(allowed[None, None], scores, MASKED)
    biggest = jnp.max(scores, axis=-1, keepdims=True)
    exp_scores = jnp.exp(scores - biggest)
    return exp_scores / jnp.sum(exp_scores, axis=-1, keepdims=True)


def attend_forward(hidden, qkv_full, gain_one, live, allowed, cosine_table, sine_values):
    token_total = hidden.shape[0]
    query_width = QUERY_HEADS * HEAD_SIZE
    key_value_width = KEY_VALUE_HEADS * HEAD_SIZE
    inverse = lax.rsqrt(jnp.mean(hidden * hidden, axis=-1, keepdims=True) + EPSILON)
    normed = hidden * inverse
    normed_low = (normed * gain_one.astype(jnp.float32)).astype(jnp.bfloat16)
    projected_rows = jnp.dot(normed_low, qkv_full, preferred_element_type=jnp.float32)
    rotated_query = apply_rotation(
        projected_rows[:, :query_width].reshape(token_total, QUERY_HEADS, HEAD_SIZE),
        cosine_table,
        sine_values,
    ).astype(jnp.bfloat16)
    rotated_query = rotated_query.reshape(
        token_total, KEY_VALUE_HEADS, QUERY_HEADS // KEY_VALUE_HEADS, HEAD_SIZE
    )
    rotated_key = apply_rotation(
        projected_rows[:, query_width : query_width + key_value_width].reshape(
            token_total, KEY_VALUE_HEADS, HEAD_SIZE
        ),
        cosine_table,
        sine_values,
    ).astype(jnp.bfloat16)
    reduced_value = (
        projected_rows[:, query_width + key_value_width :]
        .reshape(token_total, KEY_VALUE_HEADS, HEAD_SIZE)
        .astype(jnp.bfloat16)
    )
    softmaxed = probabilities(rotated_query, rotated_key, allowed)
    mixed = jnp.einsum(
        "kgtu,ukd->tkgd",
        softmaxed.astype(jnp.bfloat16),
        reduced_value,
        preferred_element_type=jnp.float32,
    )
    mixed_low = (mixed.reshape(token_total, query_width) * live[:, None]).astype(jnp.bfloat16)
    return inverse, normed, normed_low, rotated_query, rotated_key, reduced_value, mixed_low


def route_rows(hidden, weights, routed, chosen):
    qkv_full, out_full, router_full, gain_one, gain_two = weights
    inverse_two = lax.rsqrt(jnp.mean(hidden * hidden, axis=-1, keepdims=True) + EPSILON)
    normed_two = hidden * inverse_two
    routed_in = (normed_two * gain_two.astype(jnp.float32)).astype(jnp.bfloat16)
    rows = lax.dot_general(
        chosen, routed_in, (((0,), (0,)), ((), ())), preferred_element_type=jnp.float32
    ).astype(jnp.bfloat16)
    logits = jnp.dot(routed_in, router_full, preferred_element_type=jnp.float32)
    masked = jnp.where(routed, logits, MASKED)
    exp_chosen = jnp.where(routed, jnp.exp(masked - jnp.max(masked, axis=-1, keepdims=True)), 0.0)
    gate_prob = exp_chosen / jnp.sum(exp_chosen, axis=-1, keepdims=True)
    gate_wide = jnp.dot(
        gate_prob.astype(jnp.bfloat16), spread_table(), preferred_element_type=jnp.float32
    ).astype(jnp.bfloat16)
    return rows, (inverse_two, normed_two, routed_in, gate_prob, gate_wide * chosen)


def slot_gradients(grad_out, mixing):
    return lax.dot_general(
        mixing,
        grad_out.astype(jnp.bfloat16),
        (((0,), (0,)), ((), ())),
        preferred_element_type=jnp.float32,
    ).astype(jnp.bfloat16)


def feed_forward(rows_here, expert):
    expert_in_l, expert_out_l = expert[:, : 2 * MODEL_WIDTH], expert[:, 2 * MODEL_WIDTH :]
    gate_pre = lax.dot_general(
        rows_here,
        expert_in_l[:, :MODEL_WIDTH],
        (((1,), (1,)), ((), ())),
        preferred_element_type=jnp.float32,
    )
    up_pre = lax.dot_general(
        rows_here,
        expert_in_l[:, MODEL_WIDTH:],
        (((1,), (1,)), ((), ())),
        preferred_element_type=jnp.float32,
    )
    units = (jax.nn.silu(gate_pre) * up_pre).astype(jnp.bfloat16)
    results = jnp.dot(units, expert_out_l, preferred_element_type=jnp.float32).astype(jnp.bfloat16)
    return results, (gate_pre, up_pre)


def feed_backward(grad_rows, rows_here, pre, expert):
    expert_in_l, expert_out_l = expert[:, : 2 * MODEL_WIDTH], expert[:, 2 * MODEL_WIDTH :]
    gate_pre, up_pre = pre
    sigmoid_pre = jax.nn.sigmoid(gate_pre)
    activated = gate_pre * sigmoid_pre
    units = (activated * up_pre).astype(jnp.bfloat16)
    grad_units = lax.dot_general(
        grad_rows, expert_out_l, (((1,), (1,)), ((), ())), preferred_element_type=jnp.float32
    )
    grad_gate_pre = (
        grad_units * up_pre * (sigmoid_pre * (1.0 + gate_pre * (1.0 - sigmoid_pre)))
    ).astype(jnp.bfloat16)
    grad_up_pre = (grad_units * activated).astype(jnp.bfloat16)
    grad_in_rows = jnp.dot(
        grad_gate_pre, expert_in_l[:, :MODEL_WIDTH], preferred_element_type=jnp.float32
    )
    grad_in_rows = (
        grad_in_rows
        + jnp.dot(grad_up_pre, expert_in_l[:, MODEL_WIDTH:], preferred_element_type=jnp.float32)
    ).astype(jnp.bfloat16)
    out_grad = lax.dot_general(
        units, grad_rows, (((0,), (0,)), ((), ())), preferred_element_type=jnp.float32
    )
    gate_w_grad = lax.dot_general(
        grad_gate_pre, rows_here, (((0,), (0,)), ((), ())), preferred_element_type=jnp.float32
    )
    up_w_grad = lax.dot_general(
        grad_up_pre, rows_here, (((0,), (0,)), ((), ())), preferred_element_type=jnp.float32
    )
    return grad_in_rows, (gate_w_grad, up_w_grad, out_grad)


def route_backward(grad_out, weights, chosen, returned, stash):
    qkv_full, out_full, router_full, gain_one, gain_two = weights
    inverse_two, normed_two, routed_in, gate_prob, mixing = stash
    products = lax.dot_general(
        grad_out.astype(jnp.bfloat16),
        returned,
        (((1,), (1,)), ((), ())),
        preferred_element_type=jnp.float32,
    )
    grad_gate = lax.dot_general(
        products * chosen.astype(jnp.float32),
        spread_table().astype(jnp.float32),
        (((1,), (1,)), ((), ())),
        precision=lax.Precision.HIGHEST,
        preferred_element_type=jnp.float32,
    )
    grad_chosen = gate_prob * (grad_gate - jnp.sum(gate_prob * grad_gate, axis=-1, keepdims=True))
    grad_logits = grad_chosen.astype(jnp.bfloat16)
    router_grad = lax.dot_general(
        routed_in, grad_logits, (((0,), (0,)), ((), ())), preferred_element_type=jnp.float32
    )
    grad_routed = lax.dot_general(
        grad_logits, router_full, (((1,), (1,)), ((), ())), preferred_element_type=jnp.float32
    )
    return router_grad, grad_routed


def rows_backward(grad_out, weights, chosen, grad_slots, grad_routed, stash):
    qkv_full, out_full, router_full, gain_one, gain_two = weights
    inverse_two, normed_two, routed_in, gate_prob, mixing = stash
    grad_routed = grad_routed + jnp.dot(chosen, grad_slots, preferred_element_type=jnp.float32)
    gain_two_grad = jnp.sum(grad_routed * normed_two, axis=0)
    grad_h1 = grad_out + norm_back(
        grad_routed * gain_two.astype(jnp.float32), normed_two, inverse_two
    )
    return grad_h1, gain_two_grad


def attend_backward(
    grad_h1, weights, live, allowed, cosine_table, sine_values, attn_stash, attn_moved, mixed_moved
):
    qkv_full, out_full, router_full, gain_one, gain_two = weights
    inverse, normed, normed_low, rotated_query, rotated_key, reduced_value, mixed_low = attn_stash
    token_total = grad_h1.shape[0]
    query_width = QUERY_HEADS * HEAD_SIZE
    key_value_width = KEY_VALUE_HEADS * HEAD_SIZE
    grad_low = grad_h1.astype(jnp.bfloat16)
    proj_sum = core_sum(weight_halves(mixed_moved, grad_low))
    mixed_gradient = lax.dot_general(
        grad_low, out_full, (((1,), (1,)), ((), ())), preferred_element_type=jnp.float32
    ).astype(jnp.bfloat16)
    mixed_gradient, proj_sum = lax.optimization_barrier((mixed_gradient, proj_sum))
    mixed_gradient = jnp.where(live[:, None] > 0.5, mixed_gradient, jnp.zeros_like(mixed_gradient))
    mixed_gradient = mixed_gradient.reshape(
        token_total, KEY_VALUE_HEADS, QUERY_HEADS // KEY_VALUE_HEADS, HEAD_SIZE
    )
    softmaxed = probabilities(rotated_query, rotated_key, allowed)
    grad_probs = jnp.einsum(
        "tkgd,ukd->kgtu", mixed_gradient, reduced_value, preferred_element_type=jnp.float32
    )
    grad_value = jnp.einsum(
        "kgtu,tkgd->ukd",
        softmaxed.astype(jnp.bfloat16),
        mixed_gradient,
        preferred_element_type=jnp.float32,
    )
    grad_scores = (
        softmaxed * (grad_probs - jnp.sum(softmaxed * grad_probs, axis=-1, keepdims=True))
    ).astype(jnp.bfloat16)
    grad_query = jnp.einsum(
        "kgtu,ukd->tkgd", grad_scores, rotated_key, preferred_element_type=jnp.float32
    ) * HEAD_SIZE ** (-0.5)
    grad_key = jnp.einsum(
        "kgtu,tkgd->ukd", grad_scores, rotated_query, preferred_element_type=jnp.float32
    ) * HEAD_SIZE ** (-0.5)
    grad_query = unrotate(
        rounded(grad_query.reshape(token_total, QUERY_HEADS, HEAD_SIZE)), cosine_table, sine_values
    ).astype(jnp.bfloat16)
    grad_key = unrotate(rounded(grad_key), cosine_table, sine_values).astype(jnp.bfloat16)
    grad_proj = jnp.concatenate(
        [
            grad_query.reshape(token_total, query_width),
            grad_key.reshape(token_total, key_value_width),
            grad_value.astype(jnp.bfloat16).reshape(token_total, key_value_width),
        ],
        axis=1,
    )
    qkv_halves = weight_halves(attn_moved, grad_proj)
    grad_normed = lax.dot_general(
        grad_proj, qkv_full, (((1,), (1,)), ((), ())), preferred_element_type=jnp.float32
    )
    gain_one_grad = jnp.sum(grad_normed * normed, axis=0)
    grad_input = grad_h1 + norm_back(grad_normed * gain_one.astype(jnp.float32), normed, inverse)
    return (grad_input, qkv_halves, proj_sum, gain_one_grad)


def on_device(
    hidden_in,
    cotangent,
    seq_lengths,
    seq_owner,
    routes,
    query_key_value_weight,
    out_weight,
    router_weight,
    gain_attn,
    gain_mlp,
    expert_in,
    expert_out,
):
    layers = range(LAYER_COUNT)
    last = LAYER_COUNT - 1
    device = lax.axis_index(AXES)
    order = order_table()
    own_dense = [
        (
            query_key_value_weight[layer],
            out_weight[layer],
            router_weight[layer],
            gain_attn[layer],
            gain_mlp[layer],
        )
        for layer in layers
    ]
    lead = [own_dense[0][member].reshape(8, -1) for member in (0, 2, 3, 4)]
    fill = jnp.zeros((8, 128 - E - 2), jnp.bfloat16)
    lead_first = sent_by_chips(jnp.concatenate(lead + [fill], axis=1))
    lead_first, out_own, expert_in, expert_out = lax.optimization_barrier(
        (lead_first, own_dense[0][1], expert_in, expert_out)
    )
    lead_first = cut_weights(lead_first, (2048, E, 1, 1))
    out_first = sent_by_chips(out_own)
    dense = [(lead_first[0], out_first) + lead_first[1:], None]
    experts = [gather_expert(expert_in[0], expert_out[0]), None]
    position, live_row, allowed = seq_layout(seq_lengths, seq_owner, device)
    live = live_row.astype(jnp.float32)
    cosine_table, sine_values = rope_tables(position)
    routed, chosen = dispatch_table(routes, live_row)
    hidden = hidden_in.astype(jnp.float32)
    grad_hidden = cotangent.astype(jnp.float32)
    saved = []
    for layer in layers:
        attn_stash = attend_forward(
            hidden, dense[layer][0], dense[layer][3], live, allowed, cosine_table, sine_values
        )
        mixed_low = attn_stash[-1]
        hidden = hidden + jnp.dot(mixed_low, dense[layer][1], preferred_element_type=jnp.float32)
        rows, route_stash = route_rows(hidden, dense[layer], routed, chosen)
        if layer == 0:
            rows, own_dense = lax.optimization_barrier((rows, own_dense))
            gathered = sent_together(own_dense[1], AXES)
            gathered, expert_in, expert_out = lax.optimization_barrier(
                (gathered, expert_in, expert_out)
            )
            dense[1] = cut_weights(gathered, DENSE_WIDTHS)
            experts[1] = gather_expert(expert_in[1], expert_out[1])
        rows_here = trade_rows(rows)
        moved = reorder(attn_stash[2], order), reorder(mixed_low, order)
        grad_rows = None
        if layer == last:
            slots = slot_gradients(grad_hidden, route_stash[-1])
            slots, rows_here = lax.optimization_barrier((slots, rows_here))
            grad_rows = trade_rows(slots)
        results, pre = feed_forward(rows_here, experts[layer])
        if layer == last:
            results, grad_rows = lax.optimization_barrier((results, grad_rows))
        returned = trade_rows(results)
        hidden = hidden + jnp.dot(route_stash[-1], returned, preferred_element_type=jnp.float32)
        saved.append((attn_stash, moved, route_stash, rows_here, pre, returned, grad_rows))
    output_low = hidden.astype(jnp.bfloat16)
    expert_sums = [None] * LAYER_COUNT
    for layer in reversed(layers):
        attn_stash, moved, route_stash, rows_here, pre, returned, grad_rows = saved[layer]
        if grad_rows is None:
            slots = slot_gradients(grad_hidden, route_stash[-1])
            grad_rows, sums = lax.optimization_barrier((trade_rows(slots), sums))
            sums.append(jnp.zeros_like(sums[-1]))
            done_last = chip_sum_aside(jnp.concatenate(sums, axis=1))[:, :-128]
        grad_in_rows, expert_grads = feed_backward(grad_rows, rows_here, pre, experts[layer])
        grad_slots = trade_rows(grad_in_rows)
        router_grad, grad_routed = route_backward(
            grad_hidden, dense[layer], chosen, returned, route_stash
        )
        grad_slots, expert_grads = lax.optimization_barrier((grad_slots, expert_grads))
        expert_grads = scatter_expert(expert_grads)
        grad_h1, gain_two_grad = rows_backward(
            grad_hidden, dense[layer], chosen, grad_slots, grad_routed, route_stash
        )
        grad_hidden, qkv_halves, proj_sum, gain_one_grad = attend_backward(
            grad_h1, dense[layer], live, allowed, cosine_table, sine_values, attn_stash, *moved
        )
        small = small_halves(router_grad, gain_one_grad, gain_two_grad, order)
        if layer == last:
            sums = [core_sum(qkv_halves), proj_sum, core_sum(small)]
        else:
            proj_done = chip_sum(proj_sum)
            sums = [core_sum(halves) for halves in (qkv_halves, small)]
            done = chip_sum(jnp.concatenate(sums, axis=1))
        expert_sums[layer] = expert_grads
    first = [done[:, :2048], proj_done, done[:, 2048:]]
    second = [done_last[:, :2048], done_last[:, 2048:3072], done_last[:, 3072:]]
    qkv, proj, small = [jnp.stack(pair) for pair in zip(first, second)]
    both = jnp.stack(expert_sums).astype(jnp.float32)
    return (
        output_low,
        grad_hidden,
        qkv,
        proj,
        small[:, :, :E],
        small[:, :, E],
        small[:, :, E + 1],
        both[:, :, : 2 * MODEL_WIDTH],
        both[:, :, 2 * MODEL_WIDTH :],
    )


def solution(mesh):
    grid = Mesh(mesh.devices.reshape(4, 4, 2, 2, 2), AXES)
    placed = (
        P(AXES, None),
        P(AXES, None),
        P(),
        P(),
        P(AXES, None),
        P(None, AXES, None),
        P(None, AXES, None),
        P(None, AXES, None),
        P(None, AXES),
        P(None, AXES),
        P(None, AXES, None),
        P(None, AXES, None),
    )
    return jax.shard_map(
        on_device,
        mesh=grid,
        in_specs=placed,
        out_specs=(
            P(AXES, None),
            P(AXES, None),
            P(None, AXES, None),
            P(None, AXES, None),
            P(None, AXES, None),
            P(None, AXES),
            P(None, AXES),
            P(None, AXES, None),
            P(None, AXES, None),
        ),
        check_vma=False,
    )
```

```python
import math

import jax
import jax.numpy as jnp
from jax import lax
from jax.sharding import Mesh, PartitionSpec as P

MODEL_WIDTH = 1024
QUERY_HEADS = 16
KEY_VALUE_HEADS = 8
HEAD_SIZE = 64
E = 32
TOPK = 8
LAYER_COUNT = 2
SEQ_DEV = 4
TOK_DEV = 128
CAP = 36


EPSILON = 1e-06
ROPE_BASE = 10000.0
MASKED = -1e30

ROOM = 40
ROWS = E * ROOM
AXES = ("x", "y", "zh", "zl", "c")
EXPERT_AXES = ("x", "y", "zh")
CHIP_AXES = ("x", "y", "zh", "zl")
Z_AXES = ("zh", "zl")
GROUP_AXES = ("zl", "c")
DENSE_WIDTHS = (2048, 1024, E, 1, 1)
HALF = MODEL_WIDTH // 2
SWAP = [(0, 1), (1, 0)]


def sent_together(arrays, axis):
    both = jnp.concatenate([a.reshape(a.shape[0], -1) for a in arrays], axis=1)
    return lax.all_gather(both, axis, axis=0, tiled=True)


def sent_by_chips(own):
    core = lax.axis_index("c")
    copies = jnp.broadcast_to(own[None], (64,) + own.shape)
    mine = lax.all_to_all(copies, CHIP_AXES, split_axis=0, concat_axis=0, tiled=True)
    other = lax.ppermute(mine, "c", SWAP)
    pair = [jnp.where(core == 0, mine, other), jnp.where(core == 0, other, mine)]
    return jnp.stack(pair, axis=1).reshape(MODEL_WIDTH, -1)


def cut_weights(gathered, widths):
    at, pieces = 0, []
    for width in widths:
        pieces.append(gathered[:, at : at + width])
        at += width
    return tuple(pieces[:-2]) + (pieces[-2][:, 0], pieces[-1][:, 0])


def seq_layout(seq_lengths, seq_owner, device):
    owned_seq = seq_owner == device
    ranking = jnp.cumsum(owned_seq.astype(jnp.int32)) - 1
    counter = jnp.arange(SEQ_DEV, dtype=jnp.int32)
    picker = (owned_seq[None, :] & (ranking[None, :] == counter[:, None])).astype(jnp.int32)
    own_lengths = jnp.sum(picker * seq_lengths[None, :], axis=1)
    seq_ends = jnp.cumsum(own_lengths)
    slot_ids = jnp.arange(TOK_DEV, dtype=jnp.int32)
    segment = jnp.sum((slot_ids[:, None] >= seq_ends[None, :]).astype(jnp.int32), axis=1)
    seq_starts = seq_ends - own_lengths
    first_slot = jnp.sum(
        jnp.where(segment[:, None] == counter[None, :], seq_starts[None, :], 0), axis=1
    )
    position = slot_ids - first_slot
    allowed = (segment[:, None] == segment[None, :]) & (slot_ids[:, None] >= slot_ids[None, :])
    return (position, segment < SEQ_DEV, allowed)


def rope_tables(position):
    half_size = HEAD_SIZE // 2
    exponent = jnp.arange(half_size, dtype=jnp.float32) * (2.0 / HEAD_SIZE)
    frequency = jnp.exp(-math.log(ROPE_BASE) * exponent)
    angles = position.astype(jnp.float32)[:, None] * frequency[None, :]
    return (jnp.cos(angles), jnp.sin(angles))


def apply_rotation(values, cosine_table, sine_values):
    half_size = values.shape[-1] // 2
    first_half = values[..., :half_size]
    second_half = values[..., half_size:]
    cos_wide = cosine_table[:, None, :]
    sin_wide = sine_values[:, None, :]
    return jnp.concatenate(
        [
            first_half * cos_wide - second_half * sin_wide,
            second_half * cos_wide + first_half * sin_wide,
        ],
        axis=-1,
    )


def unrotate(grad_rot, cosine_table, sine_values):
    half_size = grad_rot.shape[-1] // 2
    first_half = grad_rot[..., :half_size]
    second_half = grad_rot[..., half_size:]
    cos_wide = cosine_table[:, None, :]
    sin_wide = sine_values[:, None, :]
    return jnp.concatenate(
        [
            first_half * cos_wide + second_half * sin_wide,
            second_half * cos_wide - first_half * sin_wide,
        ],
        axis=-1,
    )


def rounded(values):
    return lax.optimization_barrier(values.astype(jnp.bfloat16)).astype(jnp.float32)


def dispatch_table(route_block, live_row):
    experts = jnp.arange(E, dtype=jnp.int32)
    routed = jnp.any(route_block[:, :, None] == experts[None, None, :], axis=1)
    hits = (routed & live_row[:, None]).astype(jnp.bfloat16)
    slot_ids = jnp.arange(TOK_DEV, dtype=jnp.int32)
    before = (slot_ids[None, :] < slot_ids[:, None]).astype(jnp.bfloat16)
    rank = jnp.dot(before, hits, preferred_element_type=jnp.float32)
    code = jnp.where(hits > 0, rank, -1.0).astype(jnp.bfloat16)
    spread = spread_table()
    wide = jnp.dot(code, spread, preferred_element_type=jnp.float32)
    place = (jnp.arange(ROWS, dtype=jnp.int32) % ROOM).astype(jnp.float32)
    chosen = (wide == place[None, :]).astype(jnp.bfloat16)
    return routed, chosen


def spread_table():
    rows = jnp.arange(ROWS, dtype=jnp.int32) // ROOM
    return (jnp.arange(E, dtype=jnp.int32)[:, None] == rows[None, :]).astype(jnp.bfloat16)


def trade_rows(rows):
    return lax.all_to_all(
        rows.reshape(E, ROOM, MODEL_WIDTH), EXPERT_AXES, split_axis=0, concat_axis=0, tiled=True
    ).reshape(ROWS, MODEL_WIDTH)


def gather_expert(own_in, own_out):
    both = jnp.concatenate([own_in, own_out], axis=1)
    return lax.all_gather(both, GROUP_AXES, axis=0, tiled=True)


def scatter_expert(grads):
    both = jnp.concatenate(grads, axis=1).astype(jnp.bfloat16)
    return lax.psum_scatter(both, GROUP_AXES, scatter_dimension=0, tiled=True)


def order_table():
    at = jnp.arange(MODEL_WIDTH, dtype=jnp.int32)
    core = (at // HALF + lax.axis_index("c")) % 2
    depth, plane, row = at // 128 % 4, at // 8 % 16, at % 8
    source = (plane * 4 + depth) * 16 + core * 8 + row
    return (at[:, None] == source[None, :]).astype(jnp.bfloat16)


def reorder(values, order):
    return jnp.dot(values, order, preferred_element_type=jnp.float32).astype(jnp.bfloat16)


def weight_halves(left, right):
    pair = (((0,), (0,)), ((), ()))
    kept = lax.dot_general(left[:, :HALF], right, pair, preferred_element_type=jnp.float32)
    given = lax.dot_general(left[:, HALF:], right, pair, preferred_element_type=jnp.float32)
    return kept, given.astype(jnp.bfloat16)


def small_halves(router_grad, gain_one_grad, gain_two_grad, order):
    fill = jnp.zeros((MODEL_WIDTH, 128 - E - 2), jnp.float32)
    small = jnp.concatenate(
        [router_grad, gain_one_grad[:, None], gain_two_grad[:, None], fill], axis=1
    ).astype(jnp.bfloat16)
    moved = lax.dot_general(
        order, small, (((0,), (0,)), ((), ())), preferred_element_type=jnp.float32
    )
    return moved[:HALF], moved[HALF:].astype(jnp.bfloat16)


def core_sum(halves):
    kept, given = halves
    return (kept + lax.ppermute(given, "c", SWAP).astype(jnp.float32)).astype(jnp.bfloat16)


def chip_sum(parts):
    parts = parts.reshape(64, 8, -1)
    parts = lax.all_to_all(parts, Z_AXES + ("x", "y"), split_axis=0, concat_axis=0, tiled=True)
    return jnp.sum(parts.astype(jnp.float32), axis=0)


def norm_back(grad_norm, normed, inverse):
    return inverse * (grad_norm - normed * jnp.mean(grad_norm * normed, axis=-1, keepdims=True))


def probabilities(rotated_query, rotated_key, allowed):
    scores = jnp.einsum(
        "tkgd,ukd->kgtu", rotated_query, rotated_key, preferred_element_type=jnp.float32
    ) * HEAD_SIZE ** (-0.5)
    scores = jnp.where(allowed[None, None], scores, MASKED)
    biggest = jnp.max(scores, axis=-1, keepdims=True)
    exp_scores = jnp.exp(scores - biggest)
    return exp_scores / jnp.sum(exp_scores, axis=-1, keepdims=True)


def attend_forward(hidden, qkv_full, gain_one, live, allowed, cosine_table, sine_values):
    token_total = hidden.shape[0]
    query_width = QUERY_HEADS * HEAD_SIZE
    key_value_width = KEY_VALUE_HEADS * HEAD_SIZE
    inverse = lax.rsqrt(jnp.mean(hidden * hidden, axis=-1, keepdims=True) + EPSILON)
    normed = hidden * inverse
    normed_low = (normed * gain_one.astype(jnp.float32)).astype(jnp.bfloat16)
    projected_rows = jnp.dot(normed_low, qkv_full, preferred_element_type=jnp.float32)
    rotated_query = apply_rotation(
        projected_rows[:, :query_width].reshape(token_total, QUERY_HEADS, HEAD_SIZE),
        cosine_table,
        sine_values,
    ).astype(jnp.bfloat16)
    rotated_query = rotated_query.reshape(
        token_total, KEY_VALUE_HEADS, QUERY_HEADS // KEY_VALUE_HEADS, HEAD_SIZE
    )
    rotated_key = apply_rotation(
        projected_rows[:, query_width : query_width + key_value_width].reshape(
            token_total, KEY_VALUE_HEADS, HEAD_SIZE
        ),
        cosine_table,
        sine_values,
    ).astype(jnp.bfloat16)
    reduced_value = (
        projected_rows[:, query_width + key_value_width :]
        .reshape(token_total, KEY_VALUE_HEADS, HEAD_SIZE)
        .astype(jnp.bfloat16)
    )
    softmaxed = probabilities(rotated_query, rotated_key, allowed)
    mixed = jnp.einsum(
        "kgtu,ukd->tkgd",
        softmaxed.astype(jnp.bfloat16),
        reduced_value,
        preferred_element_type=jnp.float32,
    )
    mixed_low = (mixed.reshape(token_total, query_width) * live[:, None]).astype(jnp.bfloat16)
    return inverse, normed, normed_low, rotated_query, rotated_key, reduced_value, mixed_low


def route_rows(hidden, weights, routed, chosen):
    qkv_full, out_full, router_full, gain_one, gain_two = weights
    inverse_two = lax.rsqrt(jnp.mean(hidden * hidden, axis=-1, keepdims=True) + EPSILON)
    normed_two = hidden * inverse_two
    routed_in = (normed_two * gain_two.astype(jnp.float32)).astype(jnp.bfloat16)
    rows = lax.dot_general(
        chosen, routed_in, (((0,), (0,)), ((), ())), preferred_element_type=jnp.float32
    ).astype(jnp.bfloat16)
    logits = jnp.dot(routed_in, router_full, preferred_element_type=jnp.float32)
    masked = jnp.where(routed, logits, MASKED)
    exp_chosen = jnp.where(routed, jnp.exp(masked - jnp.max(masked, axis=-1, keepdims=True)), 0.0)
    gate_prob = exp_chosen / jnp.sum(exp_chosen, axis=-1, keepdims=True)
    gate_wide = jnp.dot(
        gate_prob.astype(jnp.bfloat16), spread_table(), preferred_element_type=jnp.float32
    ).astype(jnp.bfloat16)
    return rows, (inverse_two, normed_two, routed_in, gate_prob, gate_wide * chosen)


def slot_gradients(grad_out, mixing):
    return lax.dot_general(
        mixing,
        grad_out.astype(jnp.bfloat16),
        (((0,), (0,)), ((), ())),
        preferred_element_type=jnp.float32,
    ).astype(jnp.bfloat16)


def feed_forward(rows_here, expert):
    expert_in_l, expert_out_l = expert[:, : 2 * MODEL_WIDTH], expert[:, 2 * MODEL_WIDTH :]
    gate_pre = lax.dot_general(
        rows_here,
        expert_in_l[:, :MODEL_WIDTH],
        (((1,), (1,)), ((), ())),
        preferred_element_type=jnp.float32,
    )
    up_pre = lax.dot_general(
        rows_here,
        expert_in_l[:, MODEL_WIDTH:],
        (((1,), (1,)), ((), ())),
        preferred_element_type=jnp.float32,
    )
    units = (jax.nn.silu(gate_pre) * up_pre).astype(jnp.bfloat16)
    results = jnp.dot(units, expert_out_l, preferred_element_type=jnp.float32).astype(jnp.bfloat16)
    return results, (gate_pre, up_pre)


def feed_backward(grad_rows, rows_here, pre, expert):
    expert_in_l, expert_out_l = expert[:, : 2 * MODEL_WIDTH], expert[:, 2 * MODEL_WIDTH :]
    gate_pre, up_pre = pre
    sigmoid_pre = jax.nn.sigmoid(gate_pre)
    activated = gate_pre * sigmoid_pre
    units = (activated * up_pre).astype(jnp.bfloat16)
    grad_units = lax.dot_general(
        grad_rows, expert_out_l, (((1,), (1,)), ((), ())), preferred_element_type=jnp.float32
    )
    grad_gate_pre = (
        grad_units * up_pre * (sigmoid_pre * (1.0 + gate_pre * (1.0 - sigmoid_pre)))
    ).astype(jnp.bfloat16)
    grad_up_pre = (grad_units * activated).astype(jnp.bfloat16)
    grad_in_rows = jnp.dot(
        grad_gate_pre, expert_in_l[:, :MODEL_WIDTH], preferred_element_type=jnp.float32
    )
    grad_in_rows = (
        grad_in_rows
        + jnp.dot(grad_up_pre, expert_in_l[:, MODEL_WIDTH:], preferred_element_type=jnp.float32)
    ).astype(jnp.bfloat16)
    out_grad = lax.dot_general(
        units, grad_rows, (((0,), (0,)), ((), ())), preferred_element_type=jnp.float32
    )
    gate_w_grad = lax.dot_general(
        grad_gate_pre, rows_here, (((0,), (0,)), ((), ())), preferred_element_type=jnp.float32
    )
    up_w_grad = lax.dot_general(
        grad_up_pre, rows_here, (((0,), (0,)), ((), ())), preferred_element_type=jnp.float32
    )
    return grad_in_rows, (gate_w_grad, up_w_grad, out_grad)


def route_backward(grad_out, weights, chosen, returned, stash):
    qkv_full, out_full, router_full, gain_one, gain_two = weights
    inverse_two, normed_two, routed_in, gate_prob, mixing = stash
    products = lax.dot_general(
        grad_out.astype(jnp.bfloat16),
        returned,
        (((1,), (1,)), ((), ())),
        preferred_element_type=jnp.float32,
    )
    grad_gate = lax.dot_general(
        products * chosen.astype(jnp.float32),
        spread_table().astype(jnp.float32),
        (((1,), (1,)), ((), ())),
        precision=lax.Precision.HIGHEST,
        preferred_element_type=jnp.float32,
    )
    grad_chosen = gate_prob * (grad_gate - jnp.sum(gate_prob * grad_gate, axis=-1, keepdims=True))
    grad_logits = grad_chosen.astype(jnp.bfloat16)
    router_grad = lax.dot_general(
        routed_in, grad_logits, (((0,), (0,)), ((), ())), preferred_element_type=jnp.float32
    )
    grad_routed = lax.dot_general(
        grad_logits, router_full, (((1,), (1,)), ((), ())), preferred_element_type=jnp.float32
    )
    return router_grad, grad_routed


def rows_backward(grad_out, weights, chosen, grad_slots, grad_routed, stash):
    qkv_full, out_full, router_full, gain_one, gain_two = weights
    inverse_two, normed_two, routed_in, gate_prob, mixing = stash
    grad_routed = grad_routed + jnp.dot(chosen, grad_slots, preferred_element_type=jnp.float32)
    gain_two_grad = jnp.sum(grad_routed * normed_two, axis=0)
    grad_h1 = grad_out + norm_back(
        grad_routed * gain_two.astype(jnp.float32), normed_two, inverse_two
    )
    return grad_h1, gain_two_grad


def attend_backward(
    grad_h1, weights, live, allowed, cosine_table, sine_values, attn_stash, attn_moved, mixed_moved
):
    qkv_full, out_full, router_full, gain_one, gain_two = weights
    inverse, normed, normed_low, rotated_query, rotated_key, reduced_value, mixed_low = attn_stash
    token_total = grad_h1.shape[0]
    query_width = QUERY_HEADS * HEAD_SIZE
    key_value_width = KEY_VALUE_HEADS * HEAD_SIZE
    grad_low = grad_h1.astype(jnp.bfloat16)
    proj_sum = core_sum(weight_halves(mixed_moved, grad_low))
    mixed_gradient = lax.dot_general(
        grad_low, out_full, (((1,), (1,)), ((), ())), preferred_element_type=jnp.float32
    ).astype(jnp.bfloat16)
    mixed_gradient = jnp.where(live[:, None] > 0.5, mixed_gradient, jnp.zeros_like(mixed_gradient))
    mixed_gradient = mixed_gradient.reshape(
        token_total, KEY_VALUE_HEADS, QUERY_HEADS // KEY_VALUE_HEADS, HEAD_SIZE
    )
    softmaxed = probabilities(rotated_query, rotated_key, allowed)
    grad_probs = jnp.einsum(
        "tkgd,ukd->kgtu", mixed_gradient, reduced_value, preferred_element_type=jnp.float32
    )
    grad_value = jnp.einsum(
        "kgtu,tkgd->ukd",
        softmaxed.astype(jnp.bfloat16),
        mixed_gradient,
        preferred_element_type=jnp.float32,
    )
    grad_scores = (
        softmaxed * (grad_probs - jnp.sum(softmaxed * grad_probs, axis=-1, keepdims=True))
    ).astype(jnp.bfloat16)
    grad_query = jnp.einsum(
        "kgtu,ukd->tkgd", grad_scores, rotated_key, preferred_element_type=jnp.float32
    ) * HEAD_SIZE ** (-0.5)
    grad_key = jnp.einsum(
        "kgtu,tkgd->ukd", grad_scores, rotated_query, preferred_element_type=jnp.float32
    ) * HEAD_SIZE ** (-0.5)
    grad_query = unrotate(
        rounded(grad_query.reshape(token_total, QUERY_HEADS, HEAD_SIZE)), cosine_table, sine_values
    ).astype(jnp.bfloat16)
    grad_key = unrotate(rounded(grad_key), cosine_table, sine_values).astype(jnp.bfloat16)
    grad_proj = jnp.concatenate(
        [
            grad_query.reshape(token_total, query_width),
            grad_key.reshape(token_total, key_value_width),
            grad_value.astype(jnp.bfloat16).reshape(token_total, key_value_width),
        ],
        axis=1,
    )
    qkv_halves = weight_halves(attn_moved, grad_proj)
    grad_normed = lax.dot_general(
        grad_proj, qkv_full, (((1,), (1,)), ((), ())), preferred_element_type=jnp.float32
    )
    gain_one_grad = jnp.sum(grad_normed * normed, axis=0)
    grad_input = grad_h1 + norm_back(grad_normed * gain_one.astype(jnp.float32), normed, inverse)
    return (grad_input, qkv_halves, proj_sum, gain_one_grad)


def on_device(
    hidden_in,
    cotangent,
    seq_lengths,
    seq_owner,
    routes,
    query_key_value_weight,
    out_weight,
    router_weight,
    gain_attn,
    gain_mlp,
    expert_in,
    expert_out,
):
    layers = range(LAYER_COUNT)
    last = LAYER_COUNT - 1
    device = lax.axis_index(AXES)
    order = order_table()
    own_dense = [
        (
            query_key_value_weight[layer],
            out_weight[layer],
            router_weight[layer],
            gain_attn[layer],
            gain_mlp[layer],
        )
        for layer in layers
    ]
    lead = [part.reshape(8, -1) for part in own_dense[0]]
    fill = jnp.zeros((8, 128 - E - 2), jnp.bfloat16)
    lead = sent_by_chips(jnp.concatenate(lead + [fill], axis=1))
    dense = [cut_weights(lead, DENSE_WIDTHS), None]
    experts = [gather_expert(expert_in[0], expert_out[0]), None]
    experts[0], own_dense = lax.optimization_barrier((experts[0], own_dense))
    gathered = sent_together(own_dense[1], AXES)
    gathered, expert_in, expert_out = lax.optimization_barrier((gathered, expert_in, expert_out))
    dense[1] = cut_weights(gathered, DENSE_WIDTHS)
    experts[1] = gather_expert(expert_in[1], expert_out[1])
    position, live_row, allowed = seq_layout(seq_lengths, seq_owner, device)
    live = live_row.astype(jnp.float32)
    cosine_table, sine_values = rope_tables(position)
    routed, chosen = dispatch_table(routes, live_row)
    hidden = hidden_in.astype(jnp.float32)
    grad_hidden = cotangent.astype(jnp.float32)
    saved = []
    for layer in layers:
        attn_stash = attend_forward(
            hidden, dense[layer][0], dense[layer][3], live, allowed, cosine_table, sine_values
        )
        mixed_low = attn_stash[-1]
        hidden = hidden + jnp.dot(mixed_low, dense[layer][1], preferred_element_type=jnp.float32)
        rows, route_stash = route_rows(hidden, dense[layer], routed, chosen)
        rows_here = trade_rows(rows)
        moved = reorder(attn_stash[2], order), reorder(mixed_low, order)
        grad_rows = None
        if layer == last:
            slots = slot_gradients(grad_hidden, route_stash[-1])
            slots, rows_here = lax.optimization_barrier((slots, rows_here))
            grad_rows = trade_rows(slots)
        results, pre = feed_forward(rows_here, experts[layer])
        if layer == last:
            results, grad_rows = lax.optimization_barrier((results, grad_rows))
        returned = trade_rows(results)
        hidden = hidden + jnp.dot(route_stash[-1], returned, preferred_element_type=jnp.float32)
        saved.append((attn_stash, moved, route_stash, rows_here, pre, returned, grad_rows))
    output_low = hidden.astype(jnp.bfloat16)
    expert_sums = [None] * LAYER_COUNT
    for layer in reversed(layers):
        attn_stash, moved, route_stash, rows_here, pre, returned, grad_rows = saved[layer]
        if grad_rows is None:
            slots = slot_gradients(grad_hidden, route_stash[-1])
            grad_rows, sums = lax.optimization_barrier((trade_rows(slots), sums))
            joined = jnp.concatenate(sums, axis=1)
        grad_in_rows, expert_grads = feed_backward(grad_rows, rows_here, pre, experts[layer])
        grad_slots = trade_rows(grad_in_rows)
        router_grad, grad_routed = route_backward(
            grad_hidden, dense[layer], chosen, returned, route_stash
        )
        expert_sums[layer] = scatter_expert(expert_grads)
        if layer != last:
            grad_slots, joined = lax.optimization_barrier((grad_slots, joined))
            done_last = chip_sum(joined)
        grad_h1, gain_two_grad = rows_backward(
            grad_hidden, dense[layer], chosen, grad_slots, grad_routed, route_stash
        )
        grad_hidden, qkv_halves, proj_sum, gain_one_grad = attend_backward(
            grad_h1, dense[layer], live, allowed, cosine_table, sine_values, attn_stash, *moved
        )
        small = small_halves(router_grad, gain_one_grad, gain_two_grad, order)
        sums = [core_sum(qkv_halves), proj_sum, core_sum(small)]
    done = chip_sum(jnp.concatenate(sums, axis=1))
    first = [done[:, :2048], done[:, 2048:3072], done[:, 3072:]]
    second = [done_last[:, :2048], done_last[:, 2048:3072], done_last[:, 3072:]]
    qkv, proj, small = [jnp.stack(pair) for pair in zip(first, second)]
    both = jnp.stack(expert_sums).astype(jnp.float32)
    return (
        output_low,
        grad_hidden,
        qkv,
        proj,
        small[:, :, :E],
        small[:, :, E],
        small[:, :, E + 1],
        both[:, :, : 2 * MODEL_WIDTH],
        both[:, :, 2 * MODEL_WIDTH :],
    )


def solution(mesh):
    grid = Mesh(mesh.devices.reshape(4, 4, 2, 2, 2), AXES)
    placed = (
        P(AXES, None),
        P(AXES, None),
        P(),
        P(),
        P(AXES, None),
        P(None, AXES, None),
        P(None, AXES, None),
        P(None, AXES, None),
        P(None, AXES),
        P(None, AXES),
        P(None, AXES, None),
        P(None, AXES, None),
    )
    return jax.shard_map(
        on_device,
        mesh=grid,
        in_specs=placed,
        out_specs=(
            P(AXES, None),
            P(AXES, None),
            P(None, AXES, None),
            P(None, AXES, None),
            P(None, AXES, None),
            P(None, AXES),
            P(None, AXES),
            P(None, AXES, None),
            P(None, AXES, None),
        ),
        check_vma=False,
    )
```

```python
import math

import jax
import jax.numpy as jnp
from jax import lax
from jax.sharding import Mesh, PartitionSpec as P

MODEL_WIDTH = 1024
QUERY_HEADS = 16
KEY_VALUE_HEADS = 8
HEAD_SIZE = 64
E = 32
TOPK = 8
LAYER_COUNT = 2
SEQ_DEV = 4
TOK_DEV = 128
CAP = 36


EPSILON = 1e-06
ROPE_BASE = 10000.0
MASKED = -1e30

ROOM = 40
ROWS = E * ROOM
AXES = ("x", "y", "zh", "zl", "c")
EXPERT_AXES = ("x", "y", "zh")
CHIP_AXES = ("x", "y", "zh", "zl")
Z_AXES = ("zh", "zl")
DENSE_WIDTHS = (2048, 1024, E, 1, 1)
HALF = MODEL_WIDTH // 2
SWAP = [(0, 1), (1, 0)]


def sent_together(arrays, axis):
    both = jnp.concatenate([a.reshape(a.shape[0], -1) for a in arrays], axis=1)
    return lax.all_gather(both, axis, axis=0, tiled=True)


def sent_by_chips(own, beside):
    core = lax.axis_index("c")
    copies = jnp.broadcast_to(own[None], (64,) + own.shape)
    mine = lax.all_to_all(copies, CHIP_AXES, split_axis=0, concat_axis=0, tiled=True)
    mine, beside = lax.optimization_barrier((mine, beside))
    other = lax.ppermute(mine, "c", SWAP)
    pair = [jnp.where(core == 0, mine, other), jnp.where(core == 0, other, mine)]
    return jnp.stack(pair, axis=1).reshape(MODEL_WIDTH, -1), beside


def cut_weights(gathered, widths):
    at, pieces = 0, []
    for width in widths:
        pieces.append(gathered[:, at : at + width])
        at += width
    return tuple(pieces[:-2]) + (pieces[-2][:, 0], pieces[-1][:, 0])


def seq_layout(seq_lengths, seq_owner, device):
    owned_seq = seq_owner == device
    ranking = jnp.cumsum(owned_seq.astype(jnp.int32)) - 1
    counter = jnp.arange(SEQ_DEV, dtype=jnp.int32)
    picker = (owned_seq[None, :] & (ranking[None, :] == counter[:, None])).astype(jnp.int32)
    own_lengths = jnp.sum(picker * seq_lengths[None, :], axis=1)
    seq_ends = jnp.cumsum(own_lengths)
    slot_ids = jnp.arange(TOK_DEV, dtype=jnp.int32)
    segment = jnp.sum((slot_ids[:, None] >= seq_ends[None, :]).astype(jnp.int32), axis=1)
    seq_starts = seq_ends - own_lengths
    first_slot = jnp.sum(
        jnp.where(segment[:, None] == counter[None, :], seq_starts[None, :], 0), axis=1
    )
    position = slot_ids - first_slot
    allowed = (segment[:, None] == segment[None, :]) & (slot_ids[:, None] >= slot_ids[None, :])
    return (position, segment < SEQ_DEV, allowed)


def rope_tables(position):
    half_size = HEAD_SIZE // 2
    exponent = jnp.arange(half_size, dtype=jnp.float32) * (2.0 / HEAD_SIZE)
    frequency = jnp.exp(-math.log(ROPE_BASE) * exponent)
    angles = position.astype(jnp.float32)[:, None] * frequency[None, :]
    return (jnp.cos(angles), jnp.sin(angles))


def apply_rotation(values, cosine_table, sine_values):
    half_size = values.shape[-1] // 2
    first_half = values[..., :half_size]
    second_half = values[..., half_size:]
    cos_wide = cosine_table[:, None, :]
    sin_wide = sine_values[:, None, :]
    return jnp.concatenate(
        [
            first_half * cos_wide - second_half * sin_wide,
            second_half * cos_wide + first_half * sin_wide,
        ],
        axis=-1,
    )


def unrotate(grad_rot, cosine_table, sine_values):
    half_size = grad_rot.shape[-1] // 2
    first_half = grad_rot[..., :half_size]
    second_half = grad_rot[..., half_size:]
    cos_wide = cosine_table[:, None, :]
    sin_wide = sine_values[:, None, :]
    return jnp.concatenate(
        [
            first_half * cos_wide + second_half * sin_wide,
            second_half * cos_wide - first_half * sin_wide,
        ],
        axis=-1,
    )


def rounded(values):
    return lax.optimization_barrier(values.astype(jnp.bfloat16)).astype(jnp.float32)


def dispatch_table(route_block, live_row):
    experts = jnp.arange(E, dtype=jnp.int32)
    routed = jnp.any(route_block[:, :, None] == experts[None, None, :], axis=1)
    hits = (routed & live_row[:, None]).astype(jnp.bfloat16)
    slot_ids = jnp.arange(TOK_DEV, dtype=jnp.int32)
    before = (slot_ids[None, :] < slot_ids[:, None]).astype(jnp.bfloat16)
    rank = jnp.dot(before, hits, preferred_element_type=jnp.float32)
    code = jnp.where(hits > 0, rank, -1.0).astype(jnp.bfloat16)
    spread = spread_table()
    wide = jnp.dot(code, spread, preferred_element_type=jnp.float32)
    place = (jnp.arange(ROWS, dtype=jnp.int32) % ROOM).astype(jnp.float32)
    chosen = (wide == place[None, :]).astype(jnp.bfloat16)
    return routed, chosen


def spread_table():
    rows = jnp.arange(ROWS, dtype=jnp.int32) // ROOM
    return (jnp.arange(E, dtype=jnp.int32)[:, None] == rows[None, :]).astype(jnp.bfloat16)


def trade_rows(rows):
    return lax.all_to_all(
        rows.reshape(E, ROOM, MODEL_WIDTH), EXPERT_AXES, split_axis=0, concat_axis=0, tiled=True
    ).reshape(ROWS, MODEL_WIDTH)


def gather_expert(own_in, own_out):
    both = jnp.concatenate([own_in, own_out], axis=1)
    both = lax.all_gather(both, "zl", axis=0, tiled=True)
    return lax.all_gather(both, "c", axis=0, tiled=True)


def scatter_expert(grads):
    both = jnp.concatenate(grads, axis=1).astype(jnp.bfloat16)
    both = lax.psum_scatter(both, "c", scatter_dimension=0, tiled=True)
    return lax.psum_scatter(both, "zl", scatter_dimension=0, tiled=True)


def order_table():
    at = jnp.arange(MODEL_WIDTH, dtype=jnp.int32)
    core = (at // HALF + lax.axis_index("c")) % 2
    depth, plane, row = at // 128 % 4, at // 8 % 16, at % 8
    source = (plane * 4 + depth) * 16 + core * 8 + row
    return (at[:, None] == source[None, :]).astype(jnp.bfloat16)


def reorder(values, order):
    return jnp.dot(values, order, preferred_element_type=jnp.float32).astype(jnp.bfloat16)


def weight_halves(left, right):
    pair = (((0,), (0,)), ((), ()))
    kept = lax.dot_general(left[:, :HALF], right, pair, preferred_element_type=jnp.float32)
    given = lax.dot_general(left[:, HALF:], right, pair, preferred_element_type=jnp.float32)
    return kept, given.astype(jnp.bfloat16)


def small_halves(router_grad, gain_one_grad, gain_two_grad, order):
    fill = jnp.zeros((MODEL_WIDTH, 128 - E - 2), jnp.float32)
    small = jnp.concatenate(
        [router_grad, gain_one_grad[:, None], gain_two_grad[:, None], fill], axis=1
    ).astype(jnp.bfloat16)
    moved = lax.dot_general(
        order, small, (((0,), (0,)), ((), ())), preferred_element_type=jnp.float32
    )
    return moved[:HALF], moved[HALF:].astype(jnp.bfloat16)


def core_sum(halves):
    kept, given = halves
    return (kept + lax.ppermute(given, "c", SWAP).astype(jnp.float32)).astype(jnp.bfloat16)


def chip_sum(parts, axes):
    parts = parts.reshape(-1, 8, parts.shape[1])
    parts = lax.all_to_all(parts, axes, split_axis=0, concat_axis=0, tiled=True)
    return jnp.sum(parts.astype(jnp.float32), axis=0)


def norm_back(grad_norm, normed, inverse):
    return inverse * (grad_norm - normed * jnp.mean(grad_norm * normed, axis=-1, keepdims=True))


def probabilities(rotated_query, rotated_key, allowed):
    scores = jnp.einsum(
        "tkgd,ukd->kgtu", rotated_query, rotated_key, preferred_element_type=jnp.float32
    ) * HEAD_SIZE ** (-0.5)
    scores = jnp.where(allowed[None, None], scores, MASKED)
    biggest = jnp.max(scores, axis=-1, keepdims=True)
    exp_scores = jnp.exp(scores - biggest)
    return exp_scores / jnp.sum(exp_scores, axis=-1, keepdims=True)


def attend_forward(hidden, qkv_full, gain_one, live, allowed, cosine_table, sine_values):
    token_total = hidden.shape[0]
    query_width = QUERY_HEADS * HEAD_SIZE
    key_value_width = KEY_VALUE_HEADS * HEAD_SIZE
    inverse = lax.rsqrt(jnp.mean(hidden * hidden, axis=-1, keepdims=True) + EPSILON)
    normed = hidden * inverse
    normed_low = (normed * gain_one.astype(jnp.float32)).astype(jnp.bfloat16)
    projected_rows = jnp.dot(normed_low, qkv_full, preferred_element_type=jnp.float32)
    rotated_query = apply_rotation(
        projected_rows[:, :query_width].reshape(token_total, QUERY_HEADS, HEAD_SIZE),
        cosine_table,
        sine_values,
    ).astype(jnp.bfloat16)
    rotated_query = rotated_query.reshape(
        token_total, KEY_VALUE_HEADS, QUERY_HEADS // KEY_VALUE_HEADS, HEAD_SIZE
    )
    rotated_key = apply_rotation(
        projected_rows[:, query_width : query_width + key_value_width].reshape(
            token_total, KEY_VALUE_HEADS, HEAD_SIZE
        ),
        cosine_table,
        sine_values,
    ).astype(jnp.bfloat16)
    reduced_value = (
        projected_rows[:, query_width + key_value_width :]
        .reshape(token_total, KEY_VALUE_HEADS, HEAD_SIZE)
        .astype(jnp.bfloat16)
    )
    softmaxed = probabilities(rotated_query, rotated_key, allowed)
    mixed = jnp.einsum(
        "kgtu,ukd->tkgd",
        softmaxed.astype(jnp.bfloat16),
        reduced_value,
        preferred_element_type=jnp.float32,
    )
    mixed_low = (mixed.reshape(token_total, query_width) * live[:, None]).astype(jnp.bfloat16)
    return inverse, normed, normed_low, rotated_query, rotated_key, reduced_value, mixed_low


def route_rows(hidden, weights, routed, chosen):
    qkv_full, out_full, router_full, gain_one, gain_two = weights
    inverse_two = lax.rsqrt(jnp.mean(hidden * hidden, axis=-1, keepdims=True) + EPSILON)
    normed_two = hidden * inverse_two
    routed_in = (normed_two * gain_two.astype(jnp.float32)).astype(jnp.bfloat16)
    rows = lax.dot_general(
        chosen, routed_in, (((0,), (0,)), ((), ())), preferred_element_type=jnp.float32
    ).astype(jnp.bfloat16)
    logits = jnp.dot(routed_in, router_full, preferred_element_type=jnp.float32)
    masked = jnp.where(routed, logits, MASKED)
    exp_chosen = jnp.where(routed, jnp.exp(masked - jnp.max(masked, axis=-1, keepdims=True)), 0.0)
    gate_prob = exp_chosen / jnp.sum(exp_chosen, axis=-1, keepdims=True)
    gate_wide = jnp.dot(
        gate_prob.astype(jnp.bfloat16), spread_table(), preferred_element_type=jnp.float32
    ).astype(jnp.bfloat16)
    return rows, (inverse_two, normed_two, routed_in, gate_prob, gate_wide * chosen)


def slot_gradients(grad_out, mixing):
    return lax.dot_general(
        mixing,
        grad_out.astype(jnp.bfloat16),
        (((0,), (0,)), ((), ())),
        preferred_element_type=jnp.float32,
    ).astype(jnp.bfloat16)


def feed_forward(rows_here, expert):
    expert_in_l, expert_out_l = expert[:, : 2 * MODEL_WIDTH], expert[:, 2 * MODEL_WIDTH :]
    gate_pre = lax.dot_general(
        rows_here,
        expert_in_l[:, :MODEL_WIDTH],
        (((1,), (1,)), ((), ())),
        preferred_element_type=jnp.float32,
    )
    up_pre = lax.dot_general(
        rows_here,
        expert_in_l[:, MODEL_WIDTH:],
        (((1,), (1,)), ((), ())),
        preferred_element_type=jnp.float32,
    )
    units = (jax.nn.silu(gate_pre) * up_pre).astype(jnp.bfloat16)
    results = jnp.dot(units, expert_out_l, preferred_element_type=jnp.float32).astype(jnp.bfloat16)
    return results, (gate_pre, up_pre)


def feed_backward(grad_rows, rows_here, pre, expert):
    expert_in_l, expert_out_l = expert[:, : 2 * MODEL_WIDTH], expert[:, 2 * MODEL_WIDTH :]
    gate_pre, up_pre = pre
    sigmoid_pre = jax.nn.sigmoid(gate_pre)
    activated = gate_pre * sigmoid_pre
    units = (activated * up_pre).astype(jnp.bfloat16)
    grad_units = lax.dot_general(
        grad_rows, expert_out_l, (((1,), (1,)), ((), ())), preferred_element_type=jnp.float32
    )
    grad_gate_pre = (
        grad_units * up_pre * (sigmoid_pre * (1.0 + gate_pre * (1.0 - sigmoid_pre)))
    ).astype(jnp.bfloat16)
    grad_up_pre = (grad_units * activated).astype(jnp.bfloat16)
    grad_in_rows = jnp.dot(
        grad_gate_pre, expert_in_l[:, :MODEL_WIDTH], preferred_element_type=jnp.float32
    )
    grad_in_rows = (
        grad_in_rows
        + jnp.dot(grad_up_pre, expert_in_l[:, MODEL_WIDTH:], preferred_element_type=jnp.float32)
    ).astype(jnp.bfloat16)
    out_grad = lax.dot_general(
        units, grad_rows, (((0,), (0,)), ((), ())), preferred_element_type=jnp.float32
    )
    gate_w_grad = lax.dot_general(
        grad_gate_pre, rows_here, (((0,), (0,)), ((), ())), preferred_element_type=jnp.float32
    )
    up_w_grad = lax.dot_general(
        grad_up_pre, rows_here, (((0,), (0,)), ((), ())), preferred_element_type=jnp.float32
    )
    return grad_in_rows, (gate_w_grad, up_w_grad, out_grad)


def route_backward(grad_out, weights, chosen, returned, stash):
    qkv_full, out_full, router_full, gain_one, gain_two = weights
    inverse_two, normed_two, routed_in, gate_prob, mixing = stash
    products = lax.dot_general(
        grad_out.astype(jnp.bfloat16),
        returned,
        (((1,), (1,)), ((), ())),
        preferred_element_type=jnp.float32,
    )
    grad_gate = lax.dot_general(
        products * chosen.astype(jnp.float32),
        spread_table().astype(jnp.float32),
        (((1,), (1,)), ((), ())),
        precision=lax.Precision.HIGHEST,
        preferred_element_type=jnp.float32,
    )
    grad_chosen = gate_prob * (grad_gate - jnp.sum(gate_prob * grad_gate, axis=-1, keepdims=True))
    grad_logits = grad_chosen.astype(jnp.bfloat16)
    router_grad = lax.dot_general(
        routed_in, grad_logits, (((0,), (0,)), ((), ())), preferred_element_type=jnp.float32
    )
    grad_routed = lax.dot_general(
        grad_logits, router_full, (((1,), (1,)), ((), ())), preferred_element_type=jnp.float32
    )
    return router_grad, grad_routed


def rows_backward(grad_out, weights, chosen, grad_slots, grad_routed, stash):
    qkv_full, out_full, router_full, gain_one, gain_two = weights
    inverse_two, normed_two, routed_in, gate_prob, mixing = stash
    grad_routed = grad_routed + jnp.dot(chosen, grad_slots, preferred_element_type=jnp.float32)
    gain_two_grad = jnp.sum(grad_routed * normed_two, axis=0)
    grad_h1 = grad_out + norm_back(
        grad_routed * gain_two.astype(jnp.float32), normed_two, inverse_two
    )
    return grad_h1, gain_two_grad


def attend_backward(
    grad_h1, weights, live, allowed, cosine_table, sine_values, attn_stash, attn_moved, mixed_moved
):
    qkv_full, out_full, router_full, gain_one, gain_two = weights
    inverse, normed, normed_low, rotated_query, rotated_key, reduced_value, mixed_low = attn_stash
    token_total = grad_h1.shape[0]
    query_width = QUERY_HEADS * HEAD_SIZE
    key_value_width = KEY_VALUE_HEADS * HEAD_SIZE
    grad_low = grad_h1.astype(jnp.bfloat16)
    proj_sum = core_sum(weight_halves(mixed_moved, grad_low))
    mixed_gradient = lax.dot_general(
        grad_low, out_full, (((1,), (1,)), ((), ())), preferred_element_type=jnp.float32
    ).astype(jnp.bfloat16)
    mixed_gradient = jnp.where(live[:, None] > 0.5, mixed_gradient, jnp.zeros_like(mixed_gradient))
    mixed_gradient = mixed_gradient.reshape(
        token_total, KEY_VALUE_HEADS, QUERY_HEADS // KEY_VALUE_HEADS, HEAD_SIZE
    )
    softmaxed = probabilities(rotated_query, rotated_key, allowed)
    grad_probs = jnp.einsum(
        "tkgd,ukd->kgtu", mixed_gradient, reduced_value, preferred_element_type=jnp.float32
    )
    grad_value = jnp.einsum(
        "kgtu,tkgd->ukd",
        softmaxed.astype(jnp.bfloat16),
        mixed_gradient,
        preferred_element_type=jnp.float32,
    )
    grad_scores = (
        softmaxed * (grad_probs - jnp.sum(softmaxed * grad_probs, axis=-1, keepdims=True))
    ).astype(jnp.bfloat16)
    grad_query = jnp.einsum(
        "kgtu,ukd->tkgd", grad_scores, rotated_key, preferred_element_type=jnp.float32
    ) * HEAD_SIZE ** (-0.5)
    grad_key = jnp.einsum(
        "kgtu,tkgd->ukd", grad_scores, rotated_query, preferred_element_type=jnp.float32
    ) * HEAD_SIZE ** (-0.5)
    grad_query = unrotate(
        rounded(grad_query.reshape(token_total, QUERY_HEADS, HEAD_SIZE)), cosine_table, sine_values
    ).astype(jnp.bfloat16)
    grad_key = unrotate(rounded(grad_key), cosine_table, sine_values).astype(jnp.bfloat16)
    grad_proj = jnp.concatenate(
        [
            grad_query.reshape(token_total, query_width),
            grad_key.reshape(token_total, key_value_width),
            grad_value.astype(jnp.bfloat16).reshape(token_total, key_value_width),
        ],
        axis=1,
    )
    qkv_halves = weight_halves(attn_moved, grad_proj)
    grad_normed = lax.dot_general(
        grad_proj, qkv_full, (((1,), (1,)), ((), ())), preferred_element_type=jnp.float32
    )
    gain_one_grad = jnp.sum(grad_normed * normed, axis=0)
    grad_input = grad_h1 + norm_back(grad_normed * gain_one.astype(jnp.float32), normed, inverse)
    return (grad_input, qkv_halves, proj_sum, gain_one_grad)


def on_device(
    hidden_in,
    cotangent,
    seq_lengths,
    seq_owner,
    routes,
    query_key_value_weight,
    out_weight,
    router_weight,
    gain_attn,
    gain_mlp,
    expert_in,
    expert_out,
):
    layers = range(LAYER_COUNT)
    last = LAYER_COUNT - 1
    device = lax.axis_index(AXES)
    order = order_table()
    own_dense = [
        (
            query_key_value_weight[layer],
            out_weight[layer],
            router_weight[layer],
            gain_attn[layer],
            gain_mlp[layer],
        )
        for layer in layers
    ]
    lead = [part.reshape(8, -1) for part in own_dense[0]]
    fill = jnp.zeros((8, 128 - E - 2), jnp.bfloat16)
    position, live_row, allowed = seq_layout(seq_lengths, seq_owner, device)
    live = live_row.astype(jnp.float32)
    cosine_table, sine_values = rope_tables(position)
    routed, chosen = dispatch_table(routes, live_row)
    beside = order, live, allowed, cosine_table, sine_values, routed, chosen
    lead, beside = sent_by_chips(jnp.concatenate(lead + [fill], axis=1), beside)
    order, live, allowed, cosine_table, sine_values, routed, chosen = beside
    dense = [cut_weights(lead, DENSE_WIDTHS), None]
    experts = [gather_expert(expert_in[0], expert_out[0]), None]
    experts[0], own_dense = lax.optimization_barrier((experts[0], own_dense))
    gathered = sent_together(own_dense[1], AXES)
    gathered, expert_in, expert_out = lax.optimization_barrier((gathered, expert_in, expert_out))
    dense[1] = cut_weights(gathered, DENSE_WIDTHS)
    experts[1] = gather_expert(expert_in[1], expert_out[1])
    hidden = hidden_in.astype(jnp.float32)
    grad_hidden = cotangent.astype(jnp.float32)
    saved = []
    for layer in layers:
        attn_stash = attend_forward(
            hidden, dense[layer][0], dense[layer][3], live, allowed, cosine_table, sine_values
        )
        mixed_low = attn_stash[-1]
        hidden = hidden + jnp.dot(mixed_low, dense[layer][1], preferred_element_type=jnp.float32)
        rows, route_stash = route_rows(hidden, dense[layer], routed, chosen)
        rows_here = trade_rows(rows)
        moved = reorder(attn_stash[2], order), reorder(mixed_low, order)
        grad_rows = None
        if layer == last:
            slots = slot_gradients(grad_hidden, route_stash[-1])
            slots, rows_here = lax.optimization_barrier((slots, rows_here))
            grad_rows = trade_rows(slots)
        results, pre = feed_forward(rows_here, experts[layer])
        if layer == last:
            results, grad_rows = lax.optimization_barrier((results, grad_rows))
        returned = trade_rows(results)
        hidden = hidden + jnp.dot(route_stash[-1], returned, preferred_element_type=jnp.float32)
        saved.append((attn_stash, moved, route_stash, rows_here, pre, returned, grad_rows))
    output_low = hidden.astype(jnp.bfloat16)
    expert_sums = [None] * LAYER_COUNT
    for layer in reversed(layers):
        attn_stash, moved, route_stash, rows_here, pre, returned, grad_rows = saved[layer]
        if grad_rows is None:
            slots = slot_gradients(grad_hidden, route_stash[-1])
            grad_rows, sums = lax.optimization_barrier((trade_rows(slots), sums))
            joined = jnp.concatenate(sums, axis=1)
            joined = lax.psum_scatter(joined, Z_AXES, scatter_dimension=0, tiled=True)
        grad_in_rows, expert_grads = feed_backward(grad_rows, rows_here, pre, experts[layer])
        grad_slots = trade_rows(grad_in_rows)
        router_grad, grad_routed = route_backward(
            grad_hidden, dense[layer], chosen, returned, route_stash
        )
        expert_sums[layer] = scatter_expert(expert_grads)
        if layer != last:
            grad_slots, joined = lax.optimization_barrier((grad_slots, joined))
            done_last = chip_sum(joined, ("x", "y"))
        grad_h1, gain_two_grad = rows_backward(
            grad_hidden, dense[layer], chosen, grad_slots, grad_routed, route_stash
        )
        grad_hidden, qkv_halves, proj_sum, gain_one_grad = attend_backward(
            grad_h1, dense[layer], live, allowed, cosine_table, sine_values, attn_stash, *moved
        )
        small = small_halves(router_grad, gain_one_grad, gain_two_grad, order)
        sums = [core_sum(qkv_halves), proj_sum, core_sum(small)]
    proj_done = chip_sum(sums.pop(1), Z_AXES + ("x", "y"))
    done = chip_sum(jnp.concatenate(sums, axis=1), Z_AXES + ("x", "y"))
    first = [done[:, :2048], proj_done, done[:, 2048:]]
    second = [done_last[:, :2048], done_last[:, 2048:3072], done_last[:, 3072:]]
    qkv, proj, small = [jnp.stack(pair) for pair in zip(first, second)]
    both = jnp.stack(expert_sums).astype(jnp.float32)
    return (
        output_low,
        grad_hidden,
        qkv,
        proj,
        small[:, :, :E],
        small[:, :, E],
        small[:, :, E + 1],
        both[:, :, : 2 * MODEL_WIDTH],
        both[:, :, 2 * MODEL_WIDTH :],
    )


def solution(mesh):
    grid = Mesh(mesh.devices.reshape(4, 4, 2, 2, 2), AXES)
    placed = (
        P(AXES, None),
        P(AXES, None),
        P(),
        P(),
        P(AXES, None),
        P(None, AXES, None),
        P(None, AXES, None),
        P(None, AXES, None),
        P(None, AXES),
        P(None, AXES),
        P(None, AXES, None),
        P(None, AXES, None),
    )
    return jax.shard_map(
        on_device,
        mesh=grid,
        in_specs=placed,
        out_specs=(
            P(AXES, None),
            P(AXES, None),
            P(None, AXES, None),
            P(None, AXES, None),
            P(None, AXES, None),
            P(None, AXES),
            P(None, AXES),
            P(None, AXES, None),
            P(None, AXES, None),
        ),
        check_vma=False,
    )
```

```python
import math

import jax
import jax.numpy as jnp
from jax import lax
from jax.sharding import Mesh, PartitionSpec as P

MODEL_WIDTH = 1024
QUERY_HEADS = 16
KEY_VALUE_HEADS = 8
HEAD_SIZE = 64
E = 32
TOPK = 8
LAYER_COUNT = 2
SEQ_DEV = 4
TOK_DEV = 128
CAP = 36


EPSILON = 1e-06
ROPE_BASE = 10000.0
MASKED = -1e30

ROOM = 40
ROWS = E * ROOM
AXES = ("x", "y", "zh", "zl", "c")
EXPERT_AXES = ("x", "y", "zh")
CHIP_AXES = ("x", "y", "zh", "zl")
Z_AXES = ("zh", "zl")
DENSE_WIDTHS = (2048, 1024, E, 1, 1)
HALF = MODEL_WIDTH // 2
SWAP = [(0, 1), (1, 0)]


def sent_together(arrays, axis):
    both = jnp.concatenate([a.reshape(a.shape[0], -1) for a in arrays], axis=1)
    return lax.all_gather(both, axis, axis=0, tiled=True)


def sent_by_chips(own, beside):
    core = lax.axis_index("c")
    copies = jnp.broadcast_to(own[None], (64,) + own.shape)
    mine = lax.all_to_all(copies, CHIP_AXES, split_axis=0, concat_axis=0, tiled=True)
    mine, beside = lax.optimization_barrier((mine, beside))
    other = lax.ppermute(mine, "c", SWAP)
    pair = [jnp.where(core == 0, mine, other), jnp.where(core == 0, other, mine)]
    return jnp.stack(pair, axis=1).reshape(MODEL_WIDTH, -1), beside


def cut_weights(gathered, widths):
    at, pieces = 0, []
    for width in widths:
        pieces.append(gathered[:, at : at + width])
        at += width
    return tuple(pieces[:-2]) + (pieces[-2][:, 0], pieces[-1][:, 0])


def seq_layout(seq_lengths, seq_owner, device):
    owned_seq = seq_owner == device
    ranking = jnp.cumsum(owned_seq.astype(jnp.int32)) - 1
    counter = jnp.arange(SEQ_DEV, dtype=jnp.int32)
    picker = (owned_seq[None, :] & (ranking[None, :] == counter[:, None])).astype(jnp.int32)
    own_lengths = jnp.sum(picker * seq_lengths[None, :], axis=1)
    seq_ends = jnp.cumsum(own_lengths)
    slot_ids = jnp.arange(TOK_DEV, dtype=jnp.int32)
    segment = jnp.sum((slot_ids[:, None] >= seq_ends[None, :]).astype(jnp.int32), axis=1)
    seq_starts = seq_ends - own_lengths
    first_slot = jnp.sum(
        jnp.where(segment[:, None] == counter[None, :], seq_starts[None, :], 0), axis=1
    )
    position = slot_ids - first_slot
    allowed = (segment[:, None] == segment[None, :]) & (slot_ids[:, None] >= slot_ids[None, :])
    return (position, segment < SEQ_DEV, allowed)


def rope_tables(position):
    half_size = HEAD_SIZE // 2
    exponent = jnp.arange(half_size, dtype=jnp.float32) * (2.0 / HEAD_SIZE)
    frequency = jnp.exp(-math.log(ROPE_BASE) * exponent)
    angles = position.astype(jnp.float32)[:, None] * frequency[None, :]
    return (jnp.cos(angles), jnp.sin(angles))


def apply_rotation(values, cosine_table, sine_values):
    half_size = values.shape[-1] // 2
    first_half = values[..., :half_size]
    second_half = values[..., half_size:]
    cos_wide = cosine_table[:, None, :]
    sin_wide = sine_values[:, None, :]
    return jnp.concatenate(
        [
            first_half * cos_wide - second_half * sin_wide,
            second_half * cos_wide + first_half * sin_wide,
        ],
        axis=-1,
    )


def unrotate(grad_rot, cosine_table, sine_values):
    half_size = grad_rot.shape[-1] // 2
    first_half = grad_rot[..., :half_size]
    second_half = grad_rot[..., half_size:]
    cos_wide = cosine_table[:, None, :]
    sin_wide = sine_values[:, None, :]
    return jnp.concatenate(
        [
            first_half * cos_wide + second_half * sin_wide,
            second_half * cos_wide - first_half * sin_wide,
        ],
        axis=-1,
    )


def rounded(values):
    return lax.optimization_barrier(values.astype(jnp.bfloat16)).astype(jnp.float32)


def dispatch_table(route_block, live_row):
    experts = jnp.arange(E, dtype=jnp.int32)
    routed = jnp.any(route_block[:, :, None] == experts[None, None, :], axis=1)
    hits = (routed & live_row[:, None]).astype(jnp.bfloat16)
    slot_ids = jnp.arange(TOK_DEV, dtype=jnp.int32)
    before = (slot_ids[None, :] < slot_ids[:, None]).astype(jnp.bfloat16)
    rank = jnp.dot(before, hits, preferred_element_type=jnp.float32)
    code = jnp.where(hits > 0, rank, -1.0).astype(jnp.bfloat16)
    spread = spread_table()
    wide = jnp.dot(code, spread, preferred_element_type=jnp.float32)
    place = (jnp.arange(ROWS, dtype=jnp.int32) % ROOM).astype(jnp.float32)
    chosen = (wide == place[None, :]).astype(jnp.bfloat16)
    return routed, chosen


def spread_table():
    rows = jnp.arange(ROWS, dtype=jnp.int32) // ROOM
    return (jnp.arange(E, dtype=jnp.int32)[:, None] == rows[None, :]).astype(jnp.bfloat16)


def trade_rows(rows):
    return lax.all_to_all(
        rows.reshape(E, ROOM, MODEL_WIDTH), EXPERT_AXES, split_axis=0, concat_axis=0, tiled=True
    ).reshape(ROWS, MODEL_WIDTH)


def gather_expert(own_in, own_out):
    own = jnp.concatenate([own_in, own_out], axis=1)
    pair = jnp.concatenate([own, lax.ppermute(own, "zl", SWAP)], axis=0)
    return jnp.concatenate([pair, lax.ppermute(pair, "c", SWAP)], axis=0)


def expert_core_sum(pairs):
    dims = (((0,), (0,)), ((), ()))
    half = pairs[0][0].shape[1] // 2
    kept = [
        lax.dot_general(left[:, :half], right, dims, preferred_element_type=jnp.float32)
        for left, right in pairs
    ]
    given = [
        lax.dot_general(left[:, half:], right, dims, preferred_element_type=jnp.float32)
        for left, right in pairs
    ]
    given = jnp.concatenate([g.astype(jnp.bfloat16) for g in given], axis=1)
    return jnp.concatenate(kept, axis=1) + lax.ppermute(given, "c", SWAP).astype(jnp.float32)


def expert_chip_sum(kept):
    half = kept.shape[0] // 2
    other = lax.ppermute(kept[half:].astype(jnp.bfloat16), "zl", SWAP)
    return kept[:half] + other.astype(jnp.float32)


def order_table():
    at = jnp.arange(MODEL_WIDTH, dtype=jnp.int32)
    core = (at // HALF + lax.axis_index("c")) % 2
    depth, plane, row = at // 128 % 4, at // 8 % 16, at % 8
    source = (plane * 4 + depth) * 16 + core * 8 + row
    return (at[:, None] == source[None, :]).astype(jnp.bfloat16)


def reorder(values, order):
    return jnp.dot(values, order, preferred_element_type=jnp.float32).astype(jnp.bfloat16)


def weight_halves(left, right):
    pair = (((0,), (0,)), ((), ()))
    kept = lax.dot_general(left[:, :HALF], right, pair, preferred_element_type=jnp.float32)
    given = lax.dot_general(left[:, HALF:], right, pair, preferred_element_type=jnp.float32)
    return kept, given.astype(jnp.bfloat16)


def small_halves(router_grad, gain_one_grad, gain_two_grad, order):
    fill = jnp.zeros((MODEL_WIDTH, 128 - E - 2), jnp.float32)
    small = jnp.concatenate(
        [router_grad, gain_one_grad[:, None], gain_two_grad[:, None], fill], axis=1
    ).astype(jnp.bfloat16)
    moved = lax.dot_general(
        order, small, (((0,), (0,)), ((), ())), preferred_element_type=jnp.float32
    )
    return moved[:HALF], moved[HALF:].astype(jnp.bfloat16)


def core_sum(halves):
    kept, given = halves
    return (kept + lax.ppermute(given, "c", SWAP).astype(jnp.float32)).astype(jnp.bfloat16)


def chip_sum(parts, axes):
    parts = parts.reshape(-1, 8, parts.shape[1])
    parts = lax.all_to_all(parts, axes, split_axis=0, concat_axis=0, tiled=True)
    return jnp.sum(parts.astype(jnp.float32), axis=0)


def norm_back(grad_norm, normed, inverse):
    return inverse * (grad_norm - normed * jnp.mean(grad_norm * normed, axis=-1, keepdims=True))


def probabilities(rotated_query, rotated_key, allowed):
    scores = jnp.einsum(
        "tkgd,ukd->kgtu", rotated_query, rotated_key, preferred_element_type=jnp.float32
    ) * HEAD_SIZE ** (-0.5)
    scores = jnp.where(allowed[None, None], scores, MASKED)
    biggest = jnp.max(scores, axis=-1, keepdims=True)
    exp_scores = jnp.exp(scores - biggest)
    return exp_scores / jnp.sum(exp_scores, axis=-1, keepdims=True)


def attend_forward(hidden, qkv_full, gain_one, live, allowed, cosine_table, sine_values):
    token_total = hidden.shape[0]
    query_width = QUERY_HEADS * HEAD_SIZE
    key_value_width = KEY_VALUE_HEADS * HEAD_SIZE
    inverse = lax.rsqrt(jnp.mean(hidden * hidden, axis=-1, keepdims=True) + EPSILON)
    normed = hidden * inverse
    normed_low = (normed * gain_one.astype(jnp.float32)).astype(jnp.bfloat16)
    projected_rows = jnp.dot(normed_low, qkv_full, preferred_element_type=jnp.float32)
    rotated_query = apply_rotation(
        projected_rows[:, :query_width].reshape(token_total, QUERY_HEADS, HEAD_SIZE),
        cosine_table,
        sine_values,
    ).astype(jnp.bfloat16)
    rotated_query = rotated_query.reshape(
        token_total, KEY_VALUE_HEADS, QUERY_HEADS // KEY_VALUE_HEADS, HEAD_SIZE
    )
    rotated_key = apply_rotation(
        projected_rows[:, query_width : query_width + key_value_width].reshape(
            token_total, KEY_VALUE_HEADS, HEAD_SIZE
        ),
        cosine_table,
        sine_values,
    ).astype(jnp.bfloat16)
    reduced_value = (
        projected_rows[:, query_width + key_value_width :]
        .reshape(token_total, KEY_VALUE_HEADS, HEAD_SIZE)
        .astype(jnp.bfloat16)
    )
    softmaxed = probabilities(rotated_query, rotated_key, allowed)
    mixed = jnp.einsum(
        "kgtu,ukd->tkgd",
        softmaxed.astype(jnp.bfloat16),
        reduced_value,
        preferred_element_type=jnp.float32,
    )
    mixed_low = (mixed.reshape(token_total, query_width) * live[:, None]).astype(jnp.bfloat16)
    return inverse, normed, normed_low, rotated_query, rotated_key, reduced_value, mixed_low


def route_rows(hidden, weights, routed, chosen):
    qkv_full, out_full, router_full, gain_one, gain_two = weights
    inverse_two = lax.rsqrt(jnp.mean(hidden * hidden, axis=-1, keepdims=True) + EPSILON)
    normed_two = hidden * inverse_two
    routed_in = (normed_two * gain_two.astype(jnp.float32)).astype(jnp.bfloat16)
    rows = lax.dot_general(
        chosen, routed_in, (((0,), (0,)), ((), ())), preferred_element_type=jnp.float32
    ).astype(jnp.bfloat16)
    logits = jnp.dot(routed_in, router_full, preferred_element_type=jnp.float32)
    masked = jnp.where(routed, logits, MASKED)
    exp_chosen = jnp.where(routed, jnp.exp(masked - jnp.max(masked, axis=-1, keepdims=True)), 0.0)
    gate_prob = exp_chosen / jnp.sum(exp_chosen, axis=-1, keepdims=True)
    gate_wide = jnp.dot(
        gate_prob.astype(jnp.bfloat16), spread_table(), preferred_element_type=jnp.float32
    ).astype(jnp.bfloat16)
    return rows, (inverse_two, normed_two, routed_in, gate_prob, gate_wide * chosen)


def slot_gradients(grad_out, mixing):
    return lax.dot_general(
        mixing,
        grad_out.astype(jnp.bfloat16),
        (((0,), (0,)), ((), ())),
        preferred_element_type=jnp.float32,
    ).astype(jnp.bfloat16)


def feed_forward(rows_here, expert):
    expert_in_l, expert_out_l = expert[:, : 2 * MODEL_WIDTH], expert[:, 2 * MODEL_WIDTH :]
    gate_pre = lax.dot_general(
        rows_here,
        expert_in_l[:, :MODEL_WIDTH],
        (((1,), (1,)), ((), ())),
        preferred_element_type=jnp.float32,
    )
    up_pre = lax.dot_general(
        rows_here,
        expert_in_l[:, MODEL_WIDTH:],
        (((1,), (1,)), ((), ())),
        preferred_element_type=jnp.float32,
    )
    units = (jax.nn.silu(gate_pre) * up_pre).astype(jnp.bfloat16)
    results = jnp.dot(units, expert_out_l, preferred_element_type=jnp.float32).astype(jnp.bfloat16)
    return results, (gate_pre, up_pre)


def feed_backward(grad_rows, rows_here, pre, expert):
    expert_in_l, expert_out_l = expert[:, : 2 * MODEL_WIDTH], expert[:, 2 * MODEL_WIDTH :]
    gate_pre, up_pre = pre
    sigmoid_pre = jax.nn.sigmoid(gate_pre)
    activated = gate_pre * sigmoid_pre
    units = (activated * up_pre).astype(jnp.bfloat16)
    grad_units = lax.dot_general(
        grad_rows, expert_out_l, (((1,), (1,)), ((), ())), preferred_element_type=jnp.float32
    )
    grad_gate_pre = (
        grad_units * up_pre * (sigmoid_pre * (1.0 + gate_pre * (1.0 - sigmoid_pre)))
    ).astype(jnp.bfloat16)
    grad_up_pre = (grad_units * activated).astype(jnp.bfloat16)
    grad_in_rows = jnp.dot(
        grad_gate_pre, expert_in_l[:, :MODEL_WIDTH], preferred_element_type=jnp.float32
    )
    grad_in_rows = (
        grad_in_rows
        + jnp.dot(grad_up_pre, expert_in_l[:, MODEL_WIDTH:], preferred_element_type=jnp.float32)
    ).astype(jnp.bfloat16)
    pairs = ((grad_gate_pre, rows_here), (grad_up_pre, rows_here), (units, grad_rows))
    return grad_in_rows, pairs


def route_backward(grad_out, weights, chosen, returned, stash):
    qkv_full, out_full, router_full, gain_one, gain_two = weights
    inverse_two, normed_two, routed_in, gate_prob, mixing = stash
    products = lax.dot_general(
        grad_out.astype(jnp.bfloat16),
        returned,
        (((1,), (1,)), ((), ())),
        preferred_element_type=jnp.float32,
    )
    grad_gate = lax.dot_general(
        products * chosen.astype(jnp.float32),
        spread_table().astype(jnp.float32),
        (((1,), (1,)), ((), ())),
        precision=lax.Precision.HIGHEST,
        preferred_element_type=jnp.float32,
    )
    grad_chosen = gate_prob * (grad_gate - jnp.sum(gate_prob * grad_gate, axis=-1, keepdims=True))
    grad_logits = grad_chosen.astype(jnp.bfloat16)
    router_grad = lax.dot_general(
        routed_in, grad_logits, (((0,), (0,)), ((), ())), preferred_element_type=jnp.float32
    )
    grad_routed = lax.dot_general(
        grad_logits, router_full, (((1,), (1,)), ((), ())), preferred_element_type=jnp.float32
    )
    return router_grad, grad_routed


def rows_backward(grad_out, weights, chosen, grad_slots, grad_routed, stash):
    qkv_full, out_full, router_full, gain_one, gain_two = weights
    inverse_two, normed_two, routed_in, gate_prob, mixing = stash
    grad_routed = grad_routed + jnp.dot(chosen, grad_slots, preferred_element_type=jnp.float32)
    gain_two_grad = jnp.sum(grad_routed * normed_two, axis=0)
    grad_h1 = grad_out + norm_back(
        grad_routed * gain_two.astype(jnp.float32), normed_two, inverse_two
    )
    return grad_h1, gain_two_grad


def attend_backward(
    grad_h1, weights, live, allowed, cosine_table, sine_values, attn_stash, attn_moved, mixed_moved
):
    qkv_full, out_full, router_full, gain_one, gain_two = weights
    inverse, normed, normed_low, rotated_query, rotated_key, reduced_value, mixed_low = attn_stash
    token_total = grad_h1.shape[0]
    query_width = QUERY_HEADS * HEAD_SIZE
    key_value_width = KEY_VALUE_HEADS * HEAD_SIZE
    grad_low = grad_h1.astype(jnp.bfloat16)
    proj_sum = core_sum(weight_halves(mixed_moved, grad_low))
    mixed_gradient = lax.dot_general(
        grad_low, out_full, (((1,), (1,)), ((), ())), preferred_element_type=jnp.float32
    ).astype(jnp.bfloat16)
    mixed_gradient = jnp.where(live[:, None] > 0.5, mixed_gradient, jnp.zeros_like(mixed_gradient))
    mixed_gradient = mixed_gradient.reshape(
        token_total, KEY_VALUE_HEADS, QUERY_HEADS // KEY_VALUE_HEADS, HEAD_SIZE
    )
    softmaxed = probabilities(rotated_query, rotated_key, allowed)
    grad_probs = jnp.einsum(
        "tkgd,ukd->kgtu", mixed_gradient, reduced_value, preferred_element_type=jnp.float32
    )
    grad_value = jnp.einsum(
        "kgtu,tkgd->ukd",
        softmaxed.astype(jnp.bfloat16),
        mixed_gradient,
        preferred_element_type=jnp.float32,
    )
    grad_scores = (
        softmaxed * (grad_probs - jnp.sum(softmaxed * grad_probs, axis=-1, keepdims=True))
    ).astype(jnp.bfloat16)
    grad_query = jnp.einsum(
        "kgtu,ukd->tkgd", grad_scores, rotated_key, preferred_element_type=jnp.float32
    ) * HEAD_SIZE ** (-0.5)
    grad_key = jnp.einsum(
        "kgtu,tkgd->ukd", grad_scores, rotated_query, preferred_element_type=jnp.float32
    ) * HEAD_SIZE ** (-0.5)
    grad_query = unrotate(
        rounded(grad_query.reshape(token_total, QUERY_HEADS, HEAD_SIZE)), cosine_table, sine_values
    ).astype(jnp.bfloat16)
    grad_key = unrotate(rounded(grad_key), cosine_table, sine_values).astype(jnp.bfloat16)
    grad_proj = jnp.concatenate(
        [
            grad_query.reshape(token_total, query_width),
            grad_key.reshape(token_total, key_value_width),
            grad_value.astype(jnp.bfloat16).reshape(token_total, key_value_width),
        ],
        axis=1,
    )
    qkv_halves = weight_halves(attn_moved, grad_proj)
    grad_normed = lax.dot_general(
        grad_proj, qkv_full, (((1,), (1,)), ((), ())), preferred_element_type=jnp.float32
    )
    gain_one_grad = jnp.sum(grad_normed * normed, axis=0)
    grad_input = grad_h1 + norm_back(grad_normed * gain_one.astype(jnp.float32), normed, inverse)
    return (grad_input, qkv_halves, proj_sum, gain_one_grad)


def on_device(
    hidden_in,
    cotangent,
    seq_lengths,
    seq_owner,
    routes,
    query_key_value_weight,
    out_weight,
    router_weight,
    gain_attn,
    gain_mlp,
    expert_in,
    expert_out,
):
    layers = range(LAYER_COUNT)
    last = LAYER_COUNT - 1
    device = lax.axis_index(AXES)
    order = order_table()
    own_dense = [
        (
            query_key_value_weight[layer],
            out_weight[layer],
            router_weight[layer],
            gain_attn[layer],
            gain_mlp[layer],
        )
        for layer in layers
    ]
    lead = [part.reshape(8, -1) for part in own_dense[0]]
    fill = jnp.zeros((8, 128 - E - 2), jnp.bfloat16)
    position, live_row, allowed = seq_layout(seq_lengths, seq_owner, device)
    live = live_row.astype(jnp.float32)
    cosine_table, sine_values = rope_tables(position)
    routed, chosen = dispatch_table(routes, live_row)
    experts = [gather_expert(expert_in[0], expert_out[0]), None]
    beside = order, live, allowed, cosine_table, sine_values, routed, chosen, experts[0]
    lead, beside = sent_by_chips(jnp.concatenate(lead + [fill], axis=1), beside)
    order, live, allowed, cosine_table, sine_values, routed, chosen, experts[0] = beside
    lead, own_dense = lax.optimization_barrier((lead, own_dense))
    dense = [cut_weights(lead, DENSE_WIDTHS), None]
    dense[1] = cut_weights(sent_together(own_dense[1], AXES), DENSE_WIDTHS)
    hidden = hidden_in.astype(jnp.float32)
    grad_hidden = cotangent.astype(jnp.float32)
    saved = []
    for layer in layers:
        attn_stash = attend_forward(
            hidden, dense[layer][0], dense[layer][3], live, allowed, cosine_table, sine_values
        )
        mixed_low = attn_stash[-1]
        hidden = hidden + jnp.dot(mixed_low, dense[layer][1], preferred_element_type=jnp.float32)
        rows, route_stash = route_rows(hidden, dense[layer], routed, chosen)
        if layer == 0:
            rows, expert_in, expert_out = lax.optimization_barrier((rows, expert_in, expert_out))
            experts[1] = gather_expert(expert_in[1], expert_out[1])
        rows_here = trade_rows(rows)
        moved = reorder(attn_stash[2], order), reorder(mixed_low, order)
        grad_rows = None
        if layer == last:
            slots = slot_gradients(grad_hidden, route_stash[-1])
            slots, rows_here = lax.optimization_barrier((slots, rows_here))
            grad_rows = trade_rows(slots)
        results, pre = feed_forward(rows_here, experts[layer])
        if layer == last:
            results, grad_rows = lax.optimization_barrier((results, grad_rows))
        returned = trade_rows(results)
        if layer == 0:
            returned, experts[1] = lax.optimization_barrier((returned, experts[1]))
        hidden = hidden + jnp.dot(route_stash[-1], returned, preferred_element_type=jnp.float32)
        saved.append((attn_stash, moved, route_stash, rows_here, pre, returned, grad_rows))
    output_low = hidden.astype(jnp.bfloat16)
    expert_sums = [None] * LAYER_COUNT
    for layer in reversed(layers):
        attn_stash, moved, route_stash, rows_here, pre, returned, grad_rows = saved[layer]
        if grad_rows is None:
            slots = slot_gradients(grad_hidden, route_stash[-1])
            slots, proj_last = lax.optimization_barrier((slots, proj_last))
            grad_rows = trade_rows(slots)
            grad_rows, sums, expert_sums[last] = lax.optimization_barrier(
                (grad_rows, sums, expert_sums[last])
            )
            joined = jnp.concatenate(sums, axis=1)
        grad_in_rows, pairs = feed_backward(grad_rows, rows_here, pre, experts[layer])
        grad_in_rows, pairs = lax.optimization_barrier((grad_in_rows, pairs))
        grad_slots = trade_rows(grad_in_rows)
        expert_kept = expert_core_sum(pairs)
        router_grad, grad_routed = route_backward(
            grad_hidden, dense[layer], chosen, returned, route_stash
        )
        grad_slots, expert_kept = lax.optimization_barrier((grad_slots, expert_kept))
        expert_sums[layer] = expert_chip_sum(expert_kept)
        if layer != last:
            grad_slots, joined = lax.optimization_barrier((grad_slots, joined))
            done_last = chip_sum(joined, Z_AXES + ("x", "y"))
        grad_h1, gain_two_grad = rows_backward(
            grad_hidden, dense[layer], chosen, grad_slots, grad_routed, route_stash
        )
        grad_hidden, qkv_halves, proj_sum, gain_one_grad = attend_backward(
            grad_h1, dense[layer], live, allowed, cosine_table, sine_values, attn_stash, *moved
        )
        small = small_halves(router_grad, gain_one_grad, gain_two_grad, order)
        if layer == last:
            proj_last = chip_sum(proj_sum, Z_AXES + ("x", "y"))
            sums = [core_sum(qkv_halves), core_sum(small)]
        else:
            sums = [core_sum(qkv_halves), proj_sum, core_sum(small)]
            done = chip_sum(jnp.concatenate(sums, axis=1), Z_AXES + ("x", "y"))
    first = [done[:, :2048], done[:, 2048:3072], done[:, 3072:]]
    second = [done_last[:, :2048], proj_last, done_last[:, 2048:]]
    qkv, proj, small = [jnp.stack(pair) for pair in zip(first, second)]
    both = jnp.stack(expert_sums)
    return (
        output_low,
        grad_hidden,
        qkv,
        proj,
        small[:, :, :E],
        small[:, :, E],
        small[:, :, E + 1],
        both[:, :, : 2 * MODEL_WIDTH],
        both[:, :, 2 * MODEL_WIDTH :],
    )


def solution(mesh):
    grid = Mesh(mesh.devices.reshape(4, 4, 2, 2, 2), AXES)
    placed = (
        P(AXES, None),
        P(AXES, None),
        P(),
        P(),
        P(AXES, None),
        P(None, AXES, None),
        P(None, AXES, None),
        P(None, AXES, None),
        P(None, AXES),
        P(None, AXES),
        P(None, AXES, None),
        P(None, AXES, None),
    )
    return jax.shard_map(
        on_device,
        mesh=grid,
        in_specs=placed,
        out_specs=(
            P(AXES, None),
            P(AXES, None),
            P(None, AXES, None),
            P(None, AXES, None),
            P(None, AXES, None),
            P(None, AXES),
            P(None, AXES),
            P(None, AXES, None),
            P(None, AXES, None),
        ),
        check_vma=False,
    )
```

```python
import math

import jax
import jax.numpy as jnp
from jax import lax
from jax.sharding import Mesh, PartitionSpec as P

MODEL_WIDTH = 1024
QUERY_HEADS = 16
KEY_VALUE_HEADS = 8
HEAD_SIZE = 64
E = 32
TOPK = 8
LAYER_COUNT = 2
SEQ_DEV = 4
TOK_DEV = 128
CAP = 36


EPSILON = 1e-06
ROPE_BASE = 10000.0
MASKED = -1e30

ROOM = 40
ROWS = E * ROOM
AXES = ("x", "y", "zh", "zl", "c")
EXPERT_AXES = ("x", "y", "zh")
CHIP_AXES = ("x", "y", "zh", "zl")
Z_AXES = ("zh", "zl")
GROUP_AXES = ("zl", "c")
DENSE_WIDTHS = (2048, 1024, E, 1, 1)
HALF = MODEL_WIDTH // 2
SWAP = [(0, 1), (1, 0)]


def sent_together(arrays, axis):
    both = jnp.concatenate([a.reshape(a.shape[0], -1) for a in arrays], axis=1)
    return lax.all_gather(both, axis, axis=0, tiled=True)


def sent_by_chips(own, beside):
    core = lax.axis_index("c")
    copies = jnp.broadcast_to(own[None], (64,) + own.shape)
    mine = lax.all_to_all(copies, CHIP_AXES, split_axis=0, concat_axis=0, tiled=True)
    mine, beside = lax.optimization_barrier((mine, beside))
    other = lax.ppermute(mine, "c", SWAP)
    pair = [jnp.where(core == 0, mine, other), jnp.where(core == 0, other, mine)]
    return jnp.stack(pair, axis=1).reshape(MODEL_WIDTH, -1), beside


def cut_weights(gathered, widths):
    at, pieces = 0, []
    for width in widths:
        pieces.append(gathered[:, at : at + width])
        at += width
    return tuple(pieces[:-2]) + (pieces[-2][:, 0], pieces[-1][:, 0])


def seq_layout(seq_lengths, seq_owner, device):
    owned_seq = seq_owner == device
    ranking = jnp.cumsum(owned_seq.astype(jnp.int32)) - 1
    counter = jnp.arange(SEQ_DEV, dtype=jnp.int32)
    picker = (owned_seq[None, :] & (ranking[None, :] == counter[:, None])).astype(jnp.int32)
    own_lengths = jnp.sum(picker * seq_lengths[None, :], axis=1)
    seq_ends = jnp.cumsum(own_lengths)
    slot_ids = jnp.arange(TOK_DEV, dtype=jnp.int32)
    segment = jnp.sum((slot_ids[:, None] >= seq_ends[None, :]).astype(jnp.int32), axis=1)
    seq_starts = seq_ends - own_lengths
    first_slot = jnp.sum(
        jnp.where(segment[:, None] == counter[None, :], seq_starts[None, :], 0), axis=1
    )
    position = slot_ids - first_slot
    allowed = (segment[:, None] == segment[None, :]) & (slot_ids[:, None] >= slot_ids[None, :])
    return (position, segment < SEQ_DEV, allowed)


def rope_tables(position):
    half_size = HEAD_SIZE // 2
    exponent = jnp.arange(half_size, dtype=jnp.float32) * (2.0 / HEAD_SIZE)
    frequency = jnp.exp(-math.log(ROPE_BASE) * exponent)
    angles = position.astype(jnp.float32)[:, None] * frequency[None, :]
    return (jnp.cos(angles), jnp.sin(angles))


def apply_rotation(values, cosine_table, sine_values):
    half_size = values.shape[-1] // 2
    first_half = values[..., :half_size]
    second_half = values[..., half_size:]
    cos_wide = cosine_table[:, None, :]
    sin_wide = sine_values[:, None, :]
    return jnp.concatenate(
        [
            first_half * cos_wide - second_half * sin_wide,
            second_half * cos_wide + first_half * sin_wide,
        ],
        axis=-1,
    )


def unrotate(grad_rot, cosine_table, sine_values):
    half_size = grad_rot.shape[-1] // 2
    first_half = grad_rot[..., :half_size]
    second_half = grad_rot[..., half_size:]
    cos_wide = cosine_table[:, None, :]
    sin_wide = sine_values[:, None, :]
    return jnp.concatenate(
        [
            first_half * cos_wide + second_half * sin_wide,
            second_half * cos_wide - first_half * sin_wide,
        ],
        axis=-1,
    )


def rounded(values):
    return lax.optimization_barrier(values.astype(jnp.bfloat16)).astype(jnp.float32)


def dispatch_table(route_block, live_row):
    experts = jnp.arange(E, dtype=jnp.int32)
    routed = jnp.any(route_block[:, :, None] == experts[None, None, :], axis=1)
    hits = (routed & live_row[:, None]).astype(jnp.bfloat16)
    slot_ids = jnp.arange(TOK_DEV, dtype=jnp.int32)
    before = (slot_ids[None, :] < slot_ids[:, None]).astype(jnp.bfloat16)
    rank = jnp.dot(before, hits, preferred_element_type=jnp.float32)
    code = jnp.where(hits > 0, rank, -1.0).astype(jnp.bfloat16)
    spread = spread_table()
    wide = jnp.dot(code, spread, preferred_element_type=jnp.float32)
    place = (jnp.arange(ROWS, dtype=jnp.int32) % ROOM).astype(jnp.float32)
    chosen = (wide == place[None, :]).astype(jnp.bfloat16)
    return routed, chosen


def spread_table():
    rows = jnp.arange(ROWS, dtype=jnp.int32) // ROOM
    return (jnp.arange(E, dtype=jnp.int32)[:, None] == rows[None, :]).astype(jnp.bfloat16)


def trade_rows(rows):
    return lax.all_to_all(
        rows.reshape(E, ROOM, MODEL_WIDTH), EXPERT_AXES, split_axis=0, concat_axis=0, tiled=True
    ).reshape(ROWS, MODEL_WIDTH)


def gather_chip(own):
    other = lax.ppermute(own, "zl", SWAP)
    first = lax.axis_index("zl") == 0
    return jnp.stack([jnp.where(first, own, other), jnp.where(first, other, own)])


def gather_core(pair):
    other = lax.ppermute(pair, "c", SWAP)
    first = lax.axis_index("c") == 0
    both = [jnp.where(first, pair, other), jnp.where(first, other, pair)]
    return jnp.stack(both, axis=1).reshape(-1, pair.shape[2])


def scatter_expert(grads):
    both = jnp.concatenate(grads, axis=1).astype(jnp.bfloat16)
    return lax.psum_scatter(both, GROUP_AXES, scatter_dimension=0, tiled=True)


def order_table():
    at = jnp.arange(MODEL_WIDTH, dtype=jnp.int32)
    core = (at // HALF + lax.axis_index("c")) % 2
    depth, plane, row = at // 128 % 4, at // 8 % 16, at % 8
    source = (plane * 4 + depth) * 16 + core * 8 + row
    return (at[:, None] == source[None, :]).astype(jnp.bfloat16)


def reorder(values, order):
    return jnp.dot(values, order, preferred_element_type=jnp.float32).astype(jnp.bfloat16)


def weight_halves(left, right):
    pair = (((0,), (0,)), ((), ()))
    kept = lax.dot_general(left[:, :HALF], right, pair, preferred_element_type=jnp.float32)
    given = lax.dot_general(left[:, HALF:], right, pair, preferred_element_type=jnp.float32)
    return kept, given.astype(jnp.bfloat16)


def small_halves(router_grad, gain_one_grad, gain_two_grad, order):
    fill = jnp.zeros((MODEL_WIDTH, 128 - E - 2), jnp.float32)
    small = jnp.concatenate(
        [router_grad, gain_one_grad[:, None], gain_two_grad[:, None], fill], axis=1
    ).astype(jnp.bfloat16)
    moved = lax.dot_general(
        order, small, (((0,), (0,)), ((), ())), preferred_element_type=jnp.float32
    )
    return moved[:HALF], moved[HALF:].astype(jnp.bfloat16)


def core_sum(halves):
    kept, given = halves
    return (kept + lax.ppermute(given, "c", SWAP).astype(jnp.float32)).astype(jnp.bfloat16)


def chip_sum(parts):
    parts = parts.reshape(64, 8, -1)
    parts = lax.all_to_all(parts, Z_AXES + ("x", "y"), split_axis=0, concat_axis=0, tiled=True)
    return jnp.sum(parts.astype(jnp.float32), axis=0)


def norm_back(grad_norm, normed, inverse):
    return inverse * (grad_norm - normed * jnp.mean(grad_norm * normed, axis=-1, keepdims=True))


def probabilities(rotated_query, rotated_key, allowed):
    scores = jnp.einsum(
        "tkgd,ukd->kgtu", rotated_query, rotated_key, preferred_element_type=jnp.float32
    ) * HEAD_SIZE ** (-0.5)
    scores = jnp.where(allowed[None, None], scores, MASKED)
    biggest = jnp.max(scores, axis=-1, keepdims=True)
    exp_scores = jnp.exp(scores - biggest)
    return exp_scores / jnp.sum(exp_scores, axis=-1, keepdims=True)


def attend_forward(hidden, qkv_full, gain_one, live, allowed, cosine_table, sine_values):
    token_total = hidden.shape[0]
    query_width = QUERY_HEADS * HEAD_SIZE
    key_value_width = KEY_VALUE_HEADS * HEAD_SIZE
    inverse = lax.rsqrt(jnp.mean(hidden * hidden, axis=-1, keepdims=True) + EPSILON)
    normed = hidden * inverse
    normed_low = (normed * gain_one.astype(jnp.float32)).astype(jnp.bfloat16)
    projected_rows = jnp.dot(normed_low, qkv_full, preferred_element_type=jnp.float32)
    rotated_query = apply_rotation(
        projected_rows[:, :query_width].reshape(token_total, QUERY_HEADS, HEAD_SIZE),
        cosine_table,
        sine_values,
    ).astype(jnp.bfloat16)
    rotated_query = rotated_query.reshape(
        token_total, KEY_VALUE_HEADS, QUERY_HEADS // KEY_VALUE_HEADS, HEAD_SIZE
    )
    rotated_key = apply_rotation(
        projected_rows[:, query_width : query_width + key_value_width].reshape(
            token_total, KEY_VALUE_HEADS, HEAD_SIZE
        ),
        cosine_table,
        sine_values,
    ).astype(jnp.bfloat16)
    reduced_value = (
        projected_rows[:, query_width + key_value_width :]
        .reshape(token_total, KEY_VALUE_HEADS, HEAD_SIZE)
        .astype(jnp.bfloat16)
    )
    softmaxed = probabilities(rotated_query, rotated_key, allowed)
    mixed = jnp.einsum(
        "kgtu,ukd->tkgd",
        softmaxed.astype(jnp.bfloat16),
        reduced_value,
        preferred_element_type=jnp.float32,
    )
    mixed_low = (mixed.reshape(token_total, query_width) * live[:, None]).astype(jnp.bfloat16)
    return inverse, normed, normed_low, rotated_query, rotated_key, reduced_value, mixed_low


def route_rows(hidden, weights, routed, chosen):
    qkv_full, out_full, router_full, gain_one, gain_two = weights
    inverse_two = lax.rsqrt(jnp.mean(hidden * hidden, axis=-1, keepdims=True) + EPSILON)
    normed_two = hidden * inverse_two
    routed_in = (normed_two * gain_two.astype(jnp.float32)).astype(jnp.bfloat16)
    rows = lax.dot_general(
        chosen, routed_in, (((0,), (0,)), ((), ())), preferred_element_type=jnp.float32
    ).astype(jnp.bfloat16)
    logits = jnp.dot(routed_in, router_full, preferred_element_type=jnp.float32)
    masked = jnp.where(routed, logits, MASKED)
    exp_chosen = jnp.where(routed, jnp.exp(masked - jnp.max(masked, axis=-1, keepdims=True)), 0.0)
    gate_prob = exp_chosen / jnp.sum(exp_chosen, axis=-1, keepdims=True)
    gate_wide = jnp.dot(
        gate_prob.astype(jnp.bfloat16), spread_table(), preferred_element_type=jnp.float32
    ).astype(jnp.bfloat16)
    return rows, (inverse_two, normed_two, routed_in, gate_prob, gate_wide * chosen)


def slot_gradients(grad_out, mixing):
    return lax.dot_general(
        mixing,
        grad_out.astype(jnp.bfloat16),
        (((0,), (0,)), ((), ())),
        preferred_element_type=jnp.float32,
    ).astype(jnp.bfloat16)


def feed_forward(rows_here, expert):
    expert_in_l, expert_out_l = expert[:, : 2 * MODEL_WIDTH], expert[:, 2 * MODEL_WIDTH :]
    gate_pre = lax.dot_general(
        rows_here,
        expert_in_l[:, :MODEL_WIDTH],
        (((1,), (1,)), ((), ())),
        preferred_element_type=jnp.float32,
    )
    up_pre = lax.dot_general(
        rows_here,
        expert_in_l[:, MODEL_WIDTH:],
        (((1,), (1,)), ((), ())),
        preferred_element_type=jnp.float32,
    )
    units = (jax.nn.silu(gate_pre) * up_pre).astype(jnp.bfloat16)
    results = jnp.dot(units, expert_out_l, preferred_element_type=jnp.float32).astype(jnp.bfloat16)
    return results, (gate_pre, up_pre)


def feed_backward(grad_rows, rows_here, pre, expert):
    expert_in_l, expert_out_l = expert[:, : 2 * MODEL_WIDTH], expert[:, 2 * MODEL_WIDTH :]
    gate_pre, up_pre = pre
    sigmoid_pre = jax.nn.sigmoid(gate_pre)
    activated = gate_pre * sigmoid_pre
    units = (activated * up_pre).astype(jnp.bfloat16)
    grad_units = lax.dot_general(
        grad_rows, expert_out_l, (((1,), (1,)), ((), ())), preferred_element_type=jnp.float32
    )
    grad_gate_pre = (
        grad_units * up_pre * (sigmoid_pre * (1.0 + gate_pre * (1.0 - sigmoid_pre)))
    ).astype(jnp.bfloat16)
    grad_up_pre = (grad_units * activated).astype(jnp.bfloat16)
    grad_in_rows = jnp.dot(
        grad_gate_pre, expert_in_l[:, :MODEL_WIDTH], preferred_element_type=jnp.float32
    )
    grad_in_rows = (
        grad_in_rows
        + jnp.dot(grad_up_pre, expert_in_l[:, MODEL_WIDTH:], preferred_element_type=jnp.float32)
    ).astype(jnp.bfloat16)
    out_grad = lax.dot_general(
        units, grad_rows, (((0,), (0,)), ((), ())), preferred_element_type=jnp.float32
    )
    gate_w_grad = lax.dot_general(
        grad_gate_pre, rows_here, (((0,), (0,)), ((), ())), preferred_element_type=jnp.float32
    )
    up_w_grad = lax.dot_general(
        grad_up_pre, rows_here, (((0,), (0,)), ((), ())), preferred_element_type=jnp.float32
    )
    return grad_in_rows, (gate_w_grad, up_w_grad, out_grad)


def route_backward(grad_out, weights, chosen, returned, stash):
    qkv_full, out_full, router_full, gain_one, gain_two = weights
    inverse_two, normed_two, routed_in, gate_prob, mixing = stash
    products = lax.dot_general(
        grad_out.astype(jnp.bfloat16),
        returned,
        (((1,), (1,)), ((), ())),
        preferred_element_type=jnp.float32,
    )
    grad_gate = lax.dot_general(
        products * chosen.astype(jnp.float32),
        spread_table().astype(jnp.float32),
        (((1,), (1,)), ((), ())),
        precision=lax.Precision.HIGHEST,
        preferred_element_type=jnp.float32,
    )
    grad_chosen = gate_prob * (grad_gate - jnp.sum(gate_prob * grad_gate, axis=-1, keepdims=True))
    grad_logits = grad_chosen.astype(jnp.bfloat16)
    router_grad = lax.dot_general(
        routed_in, grad_logits, (((0,), (0,)), ((), ())), preferred_element_type=jnp.float32
    )
    grad_routed = lax.dot_general(
        grad_logits, router_full, (((1,), (1,)), ((), ())), preferred_element_type=jnp.float32
    )
    return router_grad, grad_routed


def rows_backward(grad_out, weights, chosen, grad_slots, grad_routed, stash):
    qkv_full, out_full, router_full, gain_one, gain_two = weights
    inverse_two, normed_two, routed_in, gate_prob, mixing = stash
    grad_routed = grad_routed + jnp.dot(chosen, grad_slots, preferred_element_type=jnp.float32)
    gain_two_grad = jnp.sum(grad_routed * normed_two, axis=0)
    grad_h1 = grad_out + norm_back(
        grad_routed * gain_two.astype(jnp.float32), normed_two, inverse_two
    )
    return grad_h1, gain_two_grad


def attend_backward(
    grad_h1, weights, live, allowed, cosine_table, sine_values, attn_stash, attn_moved, mixed_moved
):
    qkv_full, out_full, router_full, gain_one, gain_two = weights
    inverse, normed, normed_low, rotated_query, rotated_key, reduced_value, mixed_low = attn_stash
    token_total = grad_h1.shape[0]
    query_width = QUERY_HEADS * HEAD_SIZE
    key_value_width = KEY_VALUE_HEADS * HEAD_SIZE
    grad_low = grad_h1.astype(jnp.bfloat16)
    proj_sum = core_sum(weight_halves(mixed_moved, grad_low))
    mixed_gradient = lax.dot_general(
        grad_low, out_full, (((1,), (1,)), ((), ())), preferred_element_type=jnp.float32
    ).astype(jnp.bfloat16)
    mixed_gradient = jnp.where(live[:, None] > 0.5, mixed_gradient, jnp.zeros_like(mixed_gradient))
    mixed_gradient = mixed_gradient.reshape(
        token_total, KEY_VALUE_HEADS, QUERY_HEADS // KEY_VALUE_HEADS, HEAD_SIZE
    )
    softmaxed = probabilities(rotated_query, rotated_key, allowed)
    grad_probs = jnp.einsum(
        "tkgd,ukd->kgtu", mixed_gradient, reduced_value, preferred_element_type=jnp.float32
    )
    grad_value = jnp.einsum(
        "kgtu,tkgd->ukd",
        softmaxed.astype(jnp.bfloat16),
        mixed_gradient,
        preferred_element_type=jnp.float32,
    )
    grad_scores = (
        softmaxed * (grad_probs - jnp.sum(softmaxed * grad_probs, axis=-1, keepdims=True))
    ).astype(jnp.bfloat16)
    grad_query = jnp.einsum(
        "kgtu,ukd->tkgd", grad_scores, rotated_key, preferred_element_type=jnp.float32
    ) * HEAD_SIZE ** (-0.5)
    grad_key = jnp.einsum(
        "kgtu,tkgd->ukd", grad_scores, rotated_query, preferred_element_type=jnp.float32
    ) * HEAD_SIZE ** (-0.5)
    grad_query = unrotate(
        rounded(grad_query.reshape(token_total, QUERY_HEADS, HEAD_SIZE)), cosine_table, sine_values
    ).astype(jnp.bfloat16)
    grad_key = unrotate(rounded(grad_key), cosine_table, sine_values).astype(jnp.bfloat16)
    grad_proj = jnp.concatenate(
        [
            grad_query.reshape(token_total, query_width),
            grad_key.reshape(token_total, key_value_width),
            grad_value.astype(jnp.bfloat16).reshape(token_total, key_value_width),
        ],
        axis=1,
    )
    qkv_halves = weight_halves(attn_moved, grad_proj)
    grad_normed = lax.dot_general(
        grad_proj, qkv_full, (((1,), (1,)), ((), ())), preferred_element_type=jnp.float32
    )
    gain_one_grad = jnp.sum(grad_normed * normed, axis=0)
    grad_input = grad_h1 + norm_back(grad_normed * gain_one.astype(jnp.float32), normed, inverse)
    return (grad_input, qkv_halves, proj_sum, gain_one_grad)


def on_device(
    hidden_in,
    cotangent,
    seq_lengths,
    seq_owner,
    routes,
    query_key_value_weight,
    out_weight,
    router_weight,
    gain_attn,
    gain_mlp,
    expert_in,
    expert_out,
):
    layers = range(LAYER_COUNT)
    last = LAYER_COUNT - 1
    device = lax.axis_index(AXES)
    order = order_table()
    own_dense = [
        (
            query_key_value_weight[layer],
            out_weight[layer],
            router_weight[layer],
            gain_attn[layer],
            gain_mlp[layer],
        )
        for layer in layers
    ]
    lead = [part.reshape(8, -1) for part in own_dense[0]]
    fill = jnp.zeros((8, 128 - E - 2), jnp.bfloat16)
    position, live_row, allowed = seq_layout(seq_lengths, seq_owner, device)
    live = live_row.astype(jnp.float32)
    cosine_table, sine_values = rope_tables(position)
    routed, chosen = dispatch_table(routes, live_row)
    own_experts = [
        jnp.concatenate([expert_in[layer], expert_out[layer]], axis=1) for layer in layers
    ]
    beside = order, live, allowed, cosine_table, sine_values, routed, chosen, own_experts
    lead, beside = sent_by_chips(jnp.concatenate(lead + [fill], axis=1), beside)
    order, live, allowed, cosine_table, sine_values, routed, chosen, own_experts = beside
    chip_experts = gather_chip(own_experts[0])
    lead, own_dense = lax.optimization_barrier((lead, own_dense))
    dense = [cut_weights(lead, DENSE_WIDTHS), None]
    dense[1] = cut_weights(sent_together(own_dense[1], AXES), DENSE_WIDTHS)
    hidden = hidden_in.astype(jnp.float32)
    grad_hidden = cotangent.astype(jnp.float32)
    saved, experts = [], []
    for layer in layers:
        attn_stash = attend_forward(
            hidden, dense[layer][0], dense[layer][3], live, allowed, cosine_table, sine_values
        )
        mixed_low = attn_stash[-1]
        hidden = hidden + jnp.dot(mixed_low, dense[layer][1], preferred_element_type=jnp.float32)
        rows, route_stash = route_rows(hidden, dense[layer], routed, chosen)
        rows, chip_experts = lax.optimization_barrier((rows, chip_experts))
        rows_here = trade_rows(rows)
        expert = gather_core(chip_experts)
        moved = reorder(attn_stash[2], order), reorder(mixed_low, order)
        grad_rows = None
        if layer == last:
            slots = slot_gradients(grad_hidden, route_stash[-1])
            slots, rows_here = lax.optimization_barrier((slots, rows_here))
            grad_rows = trade_rows(slots)
        else:
            rows_here, expert = lax.optimization_barrier((rows_here, expert))
        experts.append(expert)
        results, pre = feed_forward(rows_here, expert)
        if layer == last:
            results, grad_rows = lax.optimization_barrier((results, grad_rows))
        returned = trade_rows(results)
        if layer != last:
            returned, own_expert = lax.optimization_barrier((returned, own_experts[layer + 1]))
            chip_experts = gather_chip(own_expert)
        hidden = hidden + jnp.dot(route_stash[-1], returned, preferred_element_type=jnp.float32)
        saved.append((attn_stash, moved, route_stash, rows_here, pre, returned, grad_rows))
    output_low = hidden.astype(jnp.bfloat16)
    expert_sums = [None] * LAYER_COUNT
    for layer in reversed(layers):
        attn_stash, moved, route_stash, rows_here, pre, returned, grad_rows = saved[layer]
        if grad_rows is None:
            slots = slot_gradients(grad_hidden, route_stash[-1])
            grad_rows, sums = lax.optimization_barrier((trade_rows(slots), sums))
            joined = [jnp.concatenate([sums[0], sums[2]], axis=1), sums[1]]
        grad_in_rows, expert_grads = feed_backward(grad_rows, rows_here, pre, experts[layer])
        grad_slots = trade_rows(grad_in_rows)
        router_grad, grad_routed = route_backward(
            grad_hidden, dense[layer], chosen, returned, route_stash
        )
        expert_sums[layer] = scatter_expert(expert_grads)
        if layer != last:
            grad_slots, joined = lax.optimization_barrier((grad_slots, joined))
            done_last = chip_sum(joined[0]), chip_sum(joined[1])
        grad_h1, gain_two_grad = rows_backward(
            grad_hidden, dense[layer], chosen, grad_slots, grad_routed, route_stash
        )
        grad_hidden, qkv_halves, proj_sum, gain_one_grad = attend_backward(
            grad_h1, dense[layer], live, allowed, cosine_table, sine_values, attn_stash, *moved
        )
        small = small_halves(router_grad, gain_one_grad, gain_two_grad, order)
        sums = [core_sum(qkv_halves), proj_sum, core_sum(small)]
    proj_done = chip_sum(sums.pop(1))
    done = chip_sum(jnp.concatenate(sums, axis=1))
    first = [done[:, :2048], proj_done, done[:, 2048:]]
    second = [done_last[0][:, :2048], done_last[1], done_last[0][:, 2048:]]
    qkv, proj, small = [jnp.stack(pair) for pair in zip(first, second)]
    both = jnp.stack(expert_sums).astype(jnp.float32)
    return (
        output_low,
        grad_hidden,
        qkv,
        proj,
        small[:, :, :E],
        small[:, :, E],
        small[:, :, E + 1],
        both[:, :, : 2 * MODEL_WIDTH],
        both[:, :, 2 * MODEL_WIDTH :],
    )


def solution(mesh):
    grid = Mesh(mesh.devices.reshape(4, 4, 2, 2, 2), AXES)
    placed = (
        P(AXES, None),
        P(AXES, None),
        P(),
        P(),
        P(AXES, None),
        P(None, AXES, None),
        P(None, AXES, None),
        P(None, AXES, None),
        P(None, AXES),
        P(None, AXES),
        P(None, AXES, None),
        P(None, AXES, None),
    )
    return jax.shard_map(
        on_device,
        mesh=grid,
        in_specs=placed,
        out_specs=(
            P(AXES, None),
            P(AXES, None),
            P(None, AXES, None),
            P(None, AXES, None),
            P(None, AXES, None),
            P(None, AXES),
            P(None, AXES),
            P(None, AXES, None),
            P(None, AXES, None),
        ),
        check_vma=False,
    )
```

```python
import math

import jax
import jax.numpy as jnp
from jax import lax
from jax.sharding import Mesh, PartitionSpec as P

MODEL_WIDTH = 1024
QUERY_HEADS = 16
KEY_VALUE_HEADS = 8
HEAD_SIZE = 64
E = 32
TOPK = 8
LAYER_COUNT = 2
SEQ_DEV = 4
TOK_DEV = 128
CAP = 36


EPSILON = 1e-06
ROPE_BASE = 10000.0
MASKED = -1e30

ROOM = 40
ROWS = E * ROOM
AXES = ("x", "y", "zh", "zl", "c")
EXPERT_AXES = ("x", "y", "zh")
CHIP_AXES = ("x", "y", "zh", "zl")
Z_AXES = ("zh", "zl")
GROUP_AXES = ("zl", "c")
DENSE_WIDTHS = (2048, 1024, E, 1, 1)
HALF = MODEL_WIDTH // 2
SWAP = [(0, 1), (1, 0)]


def sent_together(arrays, axis):
    both = jnp.concatenate([a.reshape(a.shape[0], -1) for a in arrays], axis=1)
    return lax.all_gather(both, axis, axis=0, tiled=True)


def sent_by_chips(own, beside):
    core = lax.axis_index("c")
    copies = jnp.broadcast_to(own[None], (64,) + own.shape)
    mine = lax.all_to_all(copies, CHIP_AXES, split_axis=0, concat_axis=0, tiled=True)
    mine, beside = lax.optimization_barrier((mine, beside))
    other = lax.ppermute(mine, "c", SWAP)
    pair = [jnp.where(core == 0, mine, other), jnp.where(core == 0, other, mine)]
    return jnp.stack(pair, axis=1).reshape(MODEL_WIDTH, -1), beside


def cut_weights(gathered, widths):
    at, pieces = 0, []
    for width in widths:
        pieces.append(gathered[:, at : at + width])
        at += width
    return tuple(pieces[:-2]) + (pieces[-2][:, 0], pieces[-1][:, 0])


def seq_layout(seq_lengths, seq_owner, device):
    owned_seq = seq_owner == device
    ranking = jnp.cumsum(owned_seq.astype(jnp.int32)) - 1
    counter = jnp.arange(SEQ_DEV, dtype=jnp.int32)
    picker = (owned_seq[None, :] & (ranking[None, :] == counter[:, None])).astype(jnp.int32)
    own_lengths = jnp.sum(picker * seq_lengths[None, :], axis=1)
    seq_ends = jnp.cumsum(own_lengths)
    slot_ids = jnp.arange(TOK_DEV, dtype=jnp.int32)
    segment = jnp.sum((slot_ids[:, None] >= seq_ends[None, :]).astype(jnp.int32), axis=1)
    seq_starts = seq_ends - own_lengths
    first_slot = jnp.sum(
        jnp.where(segment[:, None] == counter[None, :], seq_starts[None, :], 0), axis=1
    )
    position = slot_ids - first_slot
    allowed = (segment[:, None] == segment[None, :]) & (slot_ids[:, None] >= slot_ids[None, :])
    return (position, segment < SEQ_DEV, allowed)


def rope_tables(position):
    half_size = HEAD_SIZE // 2
    exponent = jnp.arange(half_size, dtype=jnp.float32) * (2.0 / HEAD_SIZE)
    frequency = jnp.exp(-math.log(ROPE_BASE) * exponent)
    angles = position.astype(jnp.float32)[:, None] * frequency[None, :]
    return (jnp.cos(angles), jnp.sin(angles))


def apply_rotation(values, cosine_table, sine_values):
    half_size = values.shape[-1] // 2
    first_half = values[..., :half_size]
    second_half = values[..., half_size:]
    cos_wide = cosine_table[:, None, :]
    sin_wide = sine_values[:, None, :]
    return jnp.concatenate(
        [
            first_half * cos_wide - second_half * sin_wide,
            second_half * cos_wide + first_half * sin_wide,
        ],
        axis=-1,
    )


def unrotate(grad_rot, cosine_table, sine_values):
    half_size = grad_rot.shape[-1] // 2
    first_half = grad_rot[..., :half_size]
    second_half = grad_rot[..., half_size:]
    cos_wide = cosine_table[:, None, :]
    sin_wide = sine_values[:, None, :]
    return jnp.concatenate(
        [
            first_half * cos_wide + second_half * sin_wide,
            second_half * cos_wide - first_half * sin_wide,
        ],
        axis=-1,
    )


def rounded(values):
    return lax.optimization_barrier(values.astype(jnp.bfloat16)).astype(jnp.float32)


def dispatch_table(route_block, live_row):
    experts = jnp.arange(E, dtype=jnp.int32)
    routed = jnp.any(route_block[:, :, None] == experts[None, None, :], axis=1)
    hits = (routed & live_row[:, None]).astype(jnp.bfloat16)
    slot_ids = jnp.arange(TOK_DEV, dtype=jnp.int32)
    before = (slot_ids[None, :] < slot_ids[:, None]).astype(jnp.bfloat16)
    rank = jnp.dot(before, hits, preferred_element_type=jnp.float32)
    code = jnp.where(hits > 0, rank, -1.0).astype(jnp.bfloat16)
    spread = spread_table()
    wide = jnp.dot(code, spread, preferred_element_type=jnp.float32)
    place = (jnp.arange(ROWS, dtype=jnp.int32) % ROOM).astype(jnp.float32)
    chosen = (wide == place[None, :]).astype(jnp.bfloat16)
    return routed, chosen


def spread_table():
    rows = jnp.arange(ROWS, dtype=jnp.int32) // ROOM
    return (jnp.arange(E, dtype=jnp.int32)[:, None] == rows[None, :]).astype(jnp.bfloat16)


def trade_rows(rows):
    return lax.all_to_all(
        rows.reshape(E, ROOM, MODEL_WIDTH), EXPERT_AXES, split_axis=0, concat_axis=0, tiled=True
    ).reshape(ROWS, MODEL_WIDTH)


def join_chip(own, other):
    first = lax.axis_index("zl") == 0
    return jnp.stack([jnp.where(first, own, other), jnp.where(first, other, own)])


def gather_core(pair):
    other = lax.ppermute(pair, "c", SWAP)
    first = lax.axis_index("c") == 0
    both = [jnp.where(first, pair, other), jnp.where(first, other, pair)]
    return jnp.stack(both, axis=1).reshape(-1, pair.shape[2])


def scatter_expert(grads):
    both = jnp.concatenate(grads, axis=1).astype(jnp.bfloat16)
    return lax.psum_scatter(both, GROUP_AXES, scatter_dimension=0, tiled=True)


def order_table():
    at = jnp.arange(MODEL_WIDTH, dtype=jnp.int32)
    core = (at // HALF + lax.axis_index("c")) % 2
    depth, plane, row = at // 128 % 4, at // 8 % 16, at % 8
    source = (plane * 4 + depth) * 16 + core * 8 + row
    return (at[:, None] == source[None, :]).astype(jnp.bfloat16)


def reorder(values, order):
    return jnp.dot(values, order, preferred_element_type=jnp.float32).astype(jnp.bfloat16)


def weight_halves(left, right):
    pair = (((0,), (0,)), ((), ()))
    kept = lax.dot_general(left[:, :HALF], right, pair, preferred_element_type=jnp.float32)
    given = lax.dot_general(left[:, HALF:], right, pair, preferred_element_type=jnp.float32)
    return kept, given.astype(jnp.bfloat16)


def small_halves(router_grad, gain_one_grad, gain_two_grad, order):
    fill = jnp.zeros((MODEL_WIDTH, 128 - E - 2), jnp.float32)
    small = jnp.concatenate(
        [router_grad, gain_one_grad[:, None], gain_two_grad[:, None], fill], axis=1
    ).astype(jnp.bfloat16)
    moved = lax.dot_general(
        order, small, (((0,), (0,)), ((), ())), preferred_element_type=jnp.float32
    )
    return moved[:HALF], moved[HALF:].astype(jnp.bfloat16)


def core_sum(halves):
    kept, given = halves
    return (kept + lax.ppermute(given, "c", SWAP).astype(jnp.float32)).astype(jnp.bfloat16)


def chip_sum(parts):
    parts = parts.reshape(64, 8, -1)
    parts = lax.all_to_all(parts, Z_AXES + ("x", "y"), split_axis=0, concat_axis=0, tiled=True)
    return jnp.sum(parts.astype(jnp.float32), axis=0)


def norm_back(grad_norm, normed, inverse):
    return inverse * (grad_norm - normed * jnp.mean(grad_norm * normed, axis=-1, keepdims=True))


def probabilities(rotated_query, rotated_key, allowed):
    scores = jnp.einsum(
        "tkgd,ukd->kgtu", rotated_query, rotated_key, preferred_element_type=jnp.float32
    ) * HEAD_SIZE ** (-0.5)
    scores = jnp.where(allowed[None, None], scores, MASKED)
    biggest = jnp.max(scores, axis=-1, keepdims=True)
    exp_scores = jnp.exp(scores - biggest)
    return exp_scores / jnp.sum(exp_scores, axis=-1, keepdims=True)


def attend_forward(hidden, qkv_full, gain_one, live, allowed, cosine_table, sine_values):
    token_total = hidden.shape[0]
    query_width = QUERY_HEADS * HEAD_SIZE
    key_value_width = KEY_VALUE_HEADS * HEAD_SIZE
    inverse = lax.rsqrt(jnp.mean(hidden * hidden, axis=-1, keepdims=True) + EPSILON)
    normed = hidden * inverse
    normed_low = (normed * gain_one.astype(jnp.float32)).astype(jnp.bfloat16)
    projected_rows = jnp.dot(normed_low, qkv_full, preferred_element_type=jnp.float32)
    rotated_query = apply_rotation(
        projected_rows[:, :query_width].reshape(token_total, QUERY_HEADS, HEAD_SIZE),
        cosine_table,
        sine_values,
    ).astype(jnp.bfloat16)
    rotated_query = rotated_query.reshape(
        token_total, KEY_VALUE_HEADS, QUERY_HEADS // KEY_VALUE_HEADS, HEAD_SIZE
    )
    rotated_key = apply_rotation(
        projected_rows[:, query_width : query_width + key_value_width].reshape(
            token_total, KEY_VALUE_HEADS, HEAD_SIZE
        ),
        cosine_table,
        sine_values,
    ).astype(jnp.bfloat16)
    reduced_value = (
        projected_rows[:, query_width + key_value_width :]
        .reshape(token_total, KEY_VALUE_HEADS, HEAD_SIZE)
        .astype(jnp.bfloat16)
    )
    softmaxed = probabilities(rotated_query, rotated_key, allowed)
    mixed = jnp.einsum(
        "kgtu,ukd->tkgd",
        softmaxed.astype(jnp.bfloat16),
        reduced_value,
        preferred_element_type=jnp.float32,
    )
    mixed_low = (mixed.reshape(token_total, query_width) * live[:, None]).astype(jnp.bfloat16)
    return inverse, normed, normed_low, rotated_query, rotated_key, reduced_value, mixed_low


def route_rows(hidden, weights, routed, chosen):
    qkv_full, out_full, router_full, gain_one, gain_two = weights
    inverse_two = lax.rsqrt(jnp.mean(hidden * hidden, axis=-1, keepdims=True) + EPSILON)
    normed_two = hidden * inverse_two
    routed_in = (normed_two * gain_two.astype(jnp.float32)).astype(jnp.bfloat16)
    rows = lax.dot_general(
        chosen, routed_in, (((0,), (0,)), ((), ())), preferred_element_type=jnp.float32
    ).astype(jnp.bfloat16)
    logits = jnp.dot(routed_in, router_full, preferred_element_type=jnp.float32)
    masked = jnp.where(routed, logits, MASKED)
    exp_chosen = jnp.where(routed, jnp.exp(masked - jnp.max(masked, axis=-1, keepdims=True)), 0.0)
    gate_prob = exp_chosen / jnp.sum(exp_chosen, axis=-1, keepdims=True)
    gate_wide = jnp.dot(
        gate_prob.astype(jnp.bfloat16), spread_table(), preferred_element_type=jnp.float32
    ).astype(jnp.bfloat16)
    return rows, (inverse_two, normed_two, routed_in, gate_prob, gate_wide * chosen)


def slot_gradients(grad_out, mixing):
    return lax.dot_general(
        mixing,
        grad_out.astype(jnp.bfloat16),
        (((0,), (0,)), ((), ())),
        preferred_element_type=jnp.float32,
    ).astype(jnp.bfloat16)


def feed_forward(rows_here, expert):
    expert_in_l, expert_out_l = expert[:, : 2 * MODEL_WIDTH], expert[:, 2 * MODEL_WIDTH :]
    gate_pre = lax.dot_general(
        rows_here,
        expert_in_l[:, :MODEL_WIDTH],
        (((1,), (1,)), ((), ())),
        preferred_element_type=jnp.float32,
    )
    up_pre = lax.dot_general(
        rows_here,
        expert_in_l[:, MODEL_WIDTH:],
        (((1,), (1,)), ((), ())),
        preferred_element_type=jnp.float32,
    )
    units = (jax.nn.silu(gate_pre) * up_pre).astype(jnp.bfloat16)
    results = jnp.dot(units, expert_out_l, preferred_element_type=jnp.float32).astype(jnp.bfloat16)
    return results, (gate_pre, up_pre)


def feed_backward(grad_rows, rows_here, pre, expert):
    expert_in_l, expert_out_l = expert[:, : 2 * MODEL_WIDTH], expert[:, 2 * MODEL_WIDTH :]
    gate_pre, up_pre = pre
    sigmoid_pre = jax.nn.sigmoid(gate_pre)
    activated = gate_pre * sigmoid_pre
    units = (activated * up_pre).astype(jnp.bfloat16)
    grad_units = lax.dot_general(
        grad_rows, expert_out_l, (((1,), (1,)), ((), ())), preferred_element_type=jnp.float32
    )
    grad_gate_pre = (
        grad_units * up_pre * (sigmoid_pre * (1.0 + gate_pre * (1.0 - sigmoid_pre)))
    ).astype(jnp.bfloat16)
    grad_up_pre = (grad_units * activated).astype(jnp.bfloat16)
    grad_in_rows = jnp.dot(
        grad_gate_pre, expert_in_l[:, :MODEL_WIDTH], preferred_element_type=jnp.float32
    )
    grad_in_rows = (
        grad_in_rows
        + jnp.dot(grad_up_pre, expert_in_l[:, MODEL_WIDTH:], preferred_element_type=jnp.float32)
    ).astype(jnp.bfloat16)
    out_grad = lax.dot_general(
        units, grad_rows, (((0,), (0,)), ((), ())), preferred_element_type=jnp.float32
    )
    gate_w_grad = lax.dot_general(
        grad_gate_pre, rows_here, (((0,), (0,)), ((), ())), preferred_element_type=jnp.float32
    )
    up_w_grad = lax.dot_general(
        grad_up_pre, rows_here, (((0,), (0,)), ((), ())), preferred_element_type=jnp.float32
    )
    return grad_in_rows, (gate_w_grad, up_w_grad, out_grad)


def route_backward(grad_out, weights, chosen, returned, stash):
    qkv_full, out_full, router_full, gain_one, gain_two = weights
    inverse_two, normed_two, routed_in, gate_prob, mixing = stash
    products = lax.dot_general(
        grad_out.astype(jnp.bfloat16),
        returned,
        (((1,), (1,)), ((), ())),
        preferred_element_type=jnp.float32,
    )
    grad_gate = lax.dot_general(
        products * chosen.astype(jnp.float32),
        spread_table().astype(jnp.float32),
        (((1,), (1,)), ((), ())),
        precision=lax.Precision.HIGHEST,
        preferred_element_type=jnp.float32,
    )
    grad_chosen = gate_prob * (grad_gate - jnp.sum(gate_prob * grad_gate, axis=-1, keepdims=True))
    grad_logits = grad_chosen.astype(jnp.bfloat16)
    router_grad = lax.dot_general(
        routed_in, grad_logits, (((0,), (0,)), ((), ())), preferred_element_type=jnp.float32
    )
    grad_routed = lax.dot_general(
        grad_logits, router_full, (((1,), (1,)), ((), ())), preferred_element_type=jnp.float32
    )
    return router_grad, grad_routed


def rows_backward(grad_out, weights, chosen, grad_slots, grad_routed, stash):
    qkv_full, out_full, router_full, gain_one, gain_two = weights
    inverse_two, normed_two, routed_in, gate_prob, mixing = stash
    grad_routed = grad_routed + jnp.dot(chosen, grad_slots, preferred_element_type=jnp.float32)
    gain_two_grad = jnp.sum(grad_routed * normed_two, axis=0)
    grad_h1 = grad_out + norm_back(
        grad_routed * gain_two.astype(jnp.float32), normed_two, inverse_two
    )
    return grad_h1, gain_two_grad


def attend_backward(
    grad_h1, weights, live, allowed, cosine_table, sine_values, attn_stash, attn_moved, mixed_moved
):
    qkv_full, out_full, router_full, gain_one, gain_two = weights
    inverse, normed, normed_low, rotated_query, rotated_key, reduced_value, mixed_low = attn_stash
    token_total = grad_h1.shape[0]
    query_width = QUERY_HEADS * HEAD_SIZE
    key_value_width = KEY_VALUE_HEADS * HEAD_SIZE
    grad_low = grad_h1.astype(jnp.bfloat16)
    proj_sum = core_sum(weight_halves(mixed_moved, grad_low))
    mixed_gradient = lax.dot_general(
        grad_low, out_full, (((1,), (1,)), ((), ())), preferred_element_type=jnp.float32
    ).astype(jnp.bfloat16)
    mixed_gradient = jnp.where(live[:, None] > 0.5, mixed_gradient, jnp.zeros_like(mixed_gradient))
    mixed_gradient = mixed_gradient.reshape(
        token_total, KEY_VALUE_HEADS, QUERY_HEADS // KEY_VALUE_HEADS, HEAD_SIZE
    )
    softmaxed = probabilities(rotated_query, rotated_key, allowed)
    grad_probs = jnp.einsum(
        "tkgd,ukd->kgtu", mixed_gradient, reduced_value, preferred_element_type=jnp.float32
    )
    grad_value = jnp.einsum(
        "kgtu,tkgd->ukd",
        softmaxed.astype(jnp.bfloat16),
        mixed_gradient,
        preferred_element_type=jnp.float32,
    )
    grad_scores = (
        softmaxed * (grad_probs - jnp.sum(softmaxed * grad_probs, axis=-1, keepdims=True))
    ).astype(jnp.bfloat16)
    grad_query = jnp.einsum(
        "kgtu,ukd->tkgd", grad_scores, rotated_key, preferred_element_type=jnp.float32
    ) * HEAD_SIZE ** (-0.5)
    grad_key = jnp.einsum(
        "kgtu,tkgd->ukd", grad_scores, rotated_query, preferred_element_type=jnp.float32
    ) * HEAD_SIZE ** (-0.5)
    grad_query = unrotate(
        rounded(grad_query.reshape(token_total, QUERY_HEADS, HEAD_SIZE)), cosine_table, sine_values
    ).astype(jnp.bfloat16)
    grad_key = unrotate(rounded(grad_key), cosine_table, sine_values).astype(jnp.bfloat16)
    grad_proj = jnp.concatenate(
        [
            grad_query.reshape(token_total, query_width),
            grad_key.reshape(token_total, key_value_width),
            grad_value.astype(jnp.bfloat16).reshape(token_total, key_value_width),
        ],
        axis=1,
    )
    qkv_halves = weight_halves(attn_moved, grad_proj)
    grad_normed = lax.dot_general(
        grad_proj, qkv_full, (((1,), (1,)), ((), ())), preferred_element_type=jnp.float32
    )
    gain_one_grad = jnp.sum(grad_normed * normed, axis=0)
    grad_input = grad_h1 + norm_back(grad_normed * gain_one.astype(jnp.float32), normed, inverse)
    return (grad_input, qkv_halves, proj_sum, gain_one_grad)


def on_device(
    hidden_in,
    cotangent,
    seq_lengths,
    seq_owner,
    routes,
    query_key_value_weight,
    out_weight,
    router_weight,
    gain_attn,
    gain_mlp,
    expert_in,
    expert_out,
):
    layers = range(LAYER_COUNT)
    last = LAYER_COUNT - 1
    device = lax.axis_index(AXES)
    order = order_table()
    own_dense = [
        (
            query_key_value_weight[layer],
            out_weight[layer],
            router_weight[layer],
            gain_attn[layer],
            gain_mlp[layer],
        )
        for layer in layers
    ]
    lead = [part.reshape(8, -1) for part in own_dense[0]]
    fill = jnp.zeros((8, 128 - E - 2), jnp.bfloat16)
    position, live_row, allowed = seq_layout(seq_lengths, seq_owner, device)
    routed, chosen = dispatch_table(routes, live_row)
    own_experts = [
        jnp.concatenate([expert_in[layer], expert_out[layer]], axis=1) for layer in layers
    ]
    beside = order, position, live_row, routed, chosen, own_experts
    lead, beside = sent_by_chips(jnp.concatenate(lead + [fill], axis=1), beside)
    order, position, live_row, routed, chosen, own_experts = beside
    live = live_row.astype(jnp.float32)
    cosine_table, sine_values = rope_tables(position)
    other_expert = lax.ppermute(own_experts[0], "zl", SWAP)
    lead, own_dense = lax.optimization_barrier((lead, own_dense))
    dense = [cut_weights(lead, DENSE_WIDTHS), None]
    dense[1] = cut_weights(sent_together(own_dense[1], AXES), DENSE_WIDTHS)
    hidden = hidden_in.astype(jnp.float32)
    grad_hidden = cotangent.astype(jnp.float32)
    saved, experts = [], []
    for layer in layers:
        attn_stash = attend_forward(
            hidden, dense[layer][0], dense[layer][3], live, allowed, cosine_table, sine_values
        )
        mixed_low = attn_stash[-1]
        hidden = hidden + jnp.dot(mixed_low, dense[layer][1], preferred_element_type=jnp.float32)
        rows, route_stash = route_rows(hidden, dense[layer], routed, chosen)
        rows, other_expert = lax.optimization_barrier((rows, other_expert))
        rows_here = trade_rows(rows)
        expert = gather_core(join_chip(own_experts[layer], other_expert))
        moved = reorder(attn_stash[2], order), reorder(mixed_low, order)
        grad_rows = None
        if layer == last:
            slots = slot_gradients(grad_hidden, route_stash[-1])
            slots, rows_here = lax.optimization_barrier((slots, rows_here))
            grad_rows = trade_rows(slots)
        experts.append(expert)
        results, pre = feed_forward(rows_here, expert)
        if layer == last:
            results, grad_rows = lax.optimization_barrier((results, grad_rows))
        returned = trade_rows(results)
        if layer != last:
            returned, own_expert = lax.optimization_barrier((returned, own_experts[layer + 1]))
            other_expert = lax.ppermute(own_expert, "zl", SWAP)
        hidden = hidden + jnp.dot(route_stash[-1], returned, preferred_element_type=jnp.float32)
        saved.append((attn_stash, moved, route_stash, rows_here, pre, returned, grad_rows))
    output_low = hidden.astype(jnp.bfloat16)
    expert_sums = [None] * LAYER_COUNT
    for layer in reversed(layers):
        attn_stash, moved, route_stash, rows_here, pre, returned, grad_rows = saved[layer]
        if grad_rows is None:
            slots = slot_gradients(grad_hidden, route_stash[-1])
            grad_rows, sums = lax.optimization_barrier((trade_rows(slots), sums))
            joined = jnp.concatenate(sums, axis=1)
        grad_in_rows, expert_grads = feed_backward(grad_rows, rows_here, pre, experts[layer])
        grad_slots = trade_rows(grad_in_rows)
        router_grad, grad_routed = route_backward(
            grad_hidden, dense[layer], chosen, returned, route_stash
        )
        expert_sums[layer] = scatter_expert(expert_grads)
        if layer != last:
            grad_slots, joined = lax.optimization_barrier((grad_slots, joined))
            done_last = chip_sum(joined)
        grad_h1, gain_two_grad = rows_backward(
            grad_hidden, dense[layer], chosen, grad_slots, grad_routed, route_stash
        )
        grad_hidden, qkv_halves, proj_sum, gain_one_grad = attend_backward(
            grad_h1, dense[layer], live, allowed, cosine_table, sine_values, attn_stash, *moved
        )
        small = small_halves(router_grad, gain_one_grad, gain_two_grad, order)
        sums = [core_sum(qkv_halves), proj_sum, core_sum(small)]
    done = chip_sum(jnp.concatenate(sums, axis=1))
    first, second = [(d[:, :2048], d[:, 2048:3072], d[:, 3072:]) for d in (done, done_last)]
    qkv, proj, small = [jnp.stack(pair) for pair in zip(first, second)]
    both = jnp.stack(expert_sums).astype(jnp.float32)
    return (
        output_low,
        grad_hidden,
        qkv,
        proj,
        small[:, :, :E],
        small[:, :, E],
        small[:, :, E + 1],
        both[:, :, : 2 * MODEL_WIDTH],
        both[:, :, 2 * MODEL_WIDTH :],
    )


def solution(mesh):
    grid = Mesh(mesh.devices.reshape(4, 4, 2, 2, 2), AXES)
    placed = (
        P(AXES, None),
        P(AXES, None),
        P(),
        P(),
        P(AXES, None),
        P(None, AXES, None),
        P(None, AXES, None),
        P(None, AXES, None),
        P(None, AXES),
        P(None, AXES),
        P(None, AXES, None),
        P(None, AXES, None),
    )
    return jax.shard_map(
        on_device,
        mesh=grid,
        in_specs=placed,
        out_specs=(
            P(AXES, None),
            P(AXES, None),
            P(None, AXES, None),
            P(None, AXES, None),
            P(None, AXES, None),
            P(None, AXES),
            P(None, AXES),
            P(None, AXES, None),
            P(None, AXES, None),
        ),
        check_vma=False,
    )
```

```python
import math

import jax
import jax.numpy as jnp
from jax import lax
from jax.experimental import pallas as pl
from jax.experimental.pallas import tpu as pltpu
from jax.sharding import Mesh, PartitionSpec as P

MODEL_WIDTH = 1024
QUERY_HEADS = 16
KEY_VALUE_HEADS = 8
HEAD_SIZE = 64
E = 32
TOPK = 8
LAYER_COUNT = 2
SEQ_DEV = 4
TOK_DEV = 128
CAP = 36


EPSILON = 1e-06
ROPE_BASE = 10000.0
MASKED = -1e30

ROOM = 40
ROWS = E * ROOM
ROW_BLOCK = 256
AXES = ("x", "y", "zh", "zl", "c")
EXPERT_AXES = ("x", "y", "zh")
CHIP_AXES = ("x", "y", "zh", "zl")
Z_AXES = ("zh", "zl")
GROUP_AXES = ("zl", "c")
DENSE_WIDTHS = (2048, 1024, E, 1, 1)
HALF = MODEL_WIDTH // 2
SWAP = [(0, 1), (1, 0)]


def sent_together(arrays, axis):
    both = jnp.concatenate([a.reshape(a.shape[0], -1) for a in arrays], axis=1)
    return lax.all_gather(both, axis, axis=0, tiled=True)


def sent_by_chips(own, beside):
    core = lax.axis_index("c")
    copies = jnp.broadcast_to(own[None], (64,) + own.shape)
    mine = lax.all_to_all(copies, CHIP_AXES, split_axis=0, concat_axis=0, tiled=True)
    mine, beside = lax.optimization_barrier((mine, beside))
    other = lax.ppermute(mine, "c", SWAP)
    pair = [jnp.where(core == 0, mine, other), jnp.where(core == 0, other, mine)]
    return jnp.stack(pair, axis=1).reshape(MODEL_WIDTH, -1), beside


def cut_weights(gathered, widths):
    at, pieces = 0, []
    for width in widths:
        pieces.append(gathered[:, at : at + width])
        at += width
    return tuple(pieces[:-2]) + (pieces[-2][:, 0], pieces[-1][:, 0])


def seq_layout(seq_lengths, seq_owner, device):
    owned_seq = seq_owner == device
    ranking = jnp.cumsum(owned_seq.astype(jnp.int32)) - 1
    counter = jnp.arange(SEQ_DEV, dtype=jnp.int32)
    picker = (owned_seq[None, :] & (ranking[None, :] == counter[:, None])).astype(jnp.int32)
    own_lengths = jnp.sum(picker * seq_lengths[None, :], axis=1)
    seq_ends = jnp.cumsum(own_lengths)
    slot_ids = jnp.arange(TOK_DEV, dtype=jnp.int32)
    segment = jnp.sum((slot_ids[:, None] >= seq_ends[None, :]).astype(jnp.int32), axis=1)
    seq_starts = seq_ends - own_lengths
    first_slot = jnp.sum(
        jnp.where(segment[:, None] == counter[None, :], seq_starts[None, :], 0), axis=1
    )
    position = slot_ids - first_slot
    allowed = (segment[:, None] == segment[None, :]) & (slot_ids[:, None] >= slot_ids[None, :])
    return (position, segment < SEQ_DEV, allowed)


def rope_tables(position):
    half_size = HEAD_SIZE // 2
    exponent = jnp.arange(half_size, dtype=jnp.float32) * (2.0 / HEAD_SIZE)
    frequency = jnp.exp(-math.log(ROPE_BASE) * exponent)
    angles = position.astype(jnp.float32)[:, None] * frequency[None, :]
    return (jnp.cos(angles), jnp.sin(angles))


def apply_rotation(values, cosine_table, sine_values):
    half_size = values.shape[-1] // 2
    first_half = values[..., :half_size]
    second_half = values[..., half_size:]
    cos_wide = cosine_table[:, None, :]
    sin_wide = sine_values[:, None, :]
    return jnp.concatenate(
        [
            first_half * cos_wide - second_half * sin_wide,
            second_half * cos_wide + first_half * sin_wide,
        ],
        axis=-1,
    )


def unrotate(grad_rot, cosine_table, sine_values):
    half_size = grad_rot.shape[-1] // 2
    first_half = grad_rot[..., :half_size]
    second_half = grad_rot[..., half_size:]
    cos_wide = cosine_table[:, None, :]
    sin_wide = sine_values[:, None, :]
    return jnp.concatenate(
        [
            first_half * cos_wide + second_half * sin_wide,
            second_half * cos_wide - first_half * sin_wide,
        ],
        axis=-1,
    )


def rounded(values):
    return lax.optimization_barrier(values.astype(jnp.bfloat16)).astype(jnp.float32)


def dispatch_table(route_block, live_row):
    experts = jnp.arange(E, dtype=jnp.int32)
    routed = jnp.any(route_block[:, :, None] == experts[None, None, :], axis=1)
    hits = (routed & live_row[:, None]).astype(jnp.bfloat16)
    slot_ids = jnp.arange(TOK_DEV, dtype=jnp.int32)
    before = (slot_ids[None, :] < slot_ids[:, None]).astype(jnp.bfloat16)
    rank = jnp.dot(before, hits, preferred_element_type=jnp.float32)
    code = jnp.where(hits > 0, rank, -1.0).astype(jnp.bfloat16)
    spread = spread_table()
    wide = jnp.dot(code, spread, preferred_element_type=jnp.float32)
    place = (jnp.arange(ROWS, dtype=jnp.int32) % ROOM).astype(jnp.float32)
    chosen = (wide == place[None, :]).astype(jnp.bfloat16)
    return routed, chosen


def spread_table():
    rows = jnp.arange(ROWS, dtype=jnp.int32) // ROOM
    return (jnp.arange(E, dtype=jnp.int32)[:, None] == rows[None, :]).astype(jnp.bfloat16)


def trade_rows(rows):
    return lax.all_to_all(
        rows.reshape(E, ROOM, MODEL_WIDTH), EXPERT_AXES, split_axis=0, concat_axis=0, tiled=True
    ).reshape(ROWS, MODEL_WIDTH)


def join_chip(own, other):
    first = lax.axis_index("zl") == 0
    return jnp.stack([jnp.where(first, own, other), jnp.where(first, other, own)])


def gather_core(pair):
    other = lax.ppermute(pair, "c", SWAP)
    first = lax.axis_index("c") == 0
    both = [jnp.where(first, pair, other), jnp.where(first, other, pair)]
    return jnp.stack(both, axis=1).reshape(-1, pair.shape[2])


def scatter_expert(grads):
    both = jnp.concatenate(grads, axis=1).astype(jnp.bfloat16)
    return lax.psum_scatter(both, GROUP_AXES, scatter_dimension=0, tiled=True)


def order_table():
    at = jnp.arange(MODEL_WIDTH, dtype=jnp.int32)
    core = (at // HALF + lax.axis_index("c")) % 2
    depth, plane, row = at // 128 % 4, at // 8 % 16, at % 8
    source = (plane * 4 + depth) * 16 + core * 8 + row
    return (at[:, None] == source[None, :]).astype(jnp.bfloat16)


def reorder(values, order):
    return jnp.dot(values, order, preferred_element_type=jnp.float32).astype(jnp.bfloat16)


def weight_halves(left, right):
    pair = (((0,), (0,)), ((), ()))
    kept = lax.dot_general(left[:, :HALF], right, pair, preferred_element_type=jnp.float32)
    given = lax.dot_general(left[:, HALF:], right, pair, preferred_element_type=jnp.float32)
    return kept, given.astype(jnp.bfloat16)


def small_halves(router_grad, gain_one_grad, gain_two_grad, order):
    fill = jnp.zeros((MODEL_WIDTH, 128 - E - 2), jnp.float32)
    small = jnp.concatenate(
        [router_grad, gain_one_grad[:, None], gain_two_grad[:, None], fill], axis=1
    ).astype(jnp.bfloat16)
    moved = lax.dot_general(
        order, small, (((0,), (0,)), ((), ())), preferred_element_type=jnp.float32
    )
    return moved[:HALF], moved[HALF:].astype(jnp.bfloat16)


def core_sum(halves):
    kept, given = halves
    return (kept + lax.ppermute(given, "c", SWAP).astype(jnp.float32)).astype(jnp.bfloat16)


def chip_sum(parts):
    parts = parts.reshape(64, 8, -1)
    parts = lax.all_to_all(parts, Z_AXES + ("x", "y"), split_axis=0, concat_axis=0, tiled=True)
    return jnp.sum(parts.astype(jnp.float32), axis=0)


def norm_back(grad_norm, normed, inverse):
    return inverse * (grad_norm - normed * jnp.mean(grad_norm * normed, axis=-1, keepdims=True))


def probabilities(rotated_query, rotated_key, allowed):
    scores = jnp.einsum(
        "tkgd,ukd->kgtu", rotated_query, rotated_key, preferred_element_type=jnp.float32
    ) * HEAD_SIZE ** (-0.5)
    scores = jnp.where(allowed[None, None], scores, MASKED)
    biggest = jnp.max(scores, axis=-1, keepdims=True)
    exp_scores = jnp.exp(scores - biggest)
    return exp_scores / jnp.sum(exp_scores, axis=-1, keepdims=True)


def attend_forward(hidden, qkv_full, gain_one, live, allowed, cosine_table, sine_values):
    token_total = hidden.shape[0]
    query_width = QUERY_HEADS * HEAD_SIZE
    key_value_width = KEY_VALUE_HEADS * HEAD_SIZE
    inverse = lax.rsqrt(jnp.mean(hidden * hidden, axis=-1, keepdims=True) + EPSILON)
    normed = hidden * inverse
    normed_low = (normed * gain_one.astype(jnp.float32)).astype(jnp.bfloat16)
    projected_rows = jnp.dot(normed_low, qkv_full, preferred_element_type=jnp.float32)
    rotated_query = apply_rotation(
        projected_rows[:, :query_width].reshape(token_total, QUERY_HEADS, HEAD_SIZE),
        cosine_table,
        sine_values,
    ).astype(jnp.bfloat16)
    rotated_query = rotated_query.reshape(
        token_total, KEY_VALUE_HEADS, QUERY_HEADS // KEY_VALUE_HEADS, HEAD_SIZE
    )
    rotated_key = apply_rotation(
        projected_rows[:, query_width : query_width + key_value_width].reshape(
            token_total, KEY_VALUE_HEADS, HEAD_SIZE
        ),
        cosine_table,
        sine_values,
    ).astype(jnp.bfloat16)
    reduced_value = (
        projected_rows[:, query_width + key_value_width :]
        .reshape(token_total, KEY_VALUE_HEADS, HEAD_SIZE)
        .astype(jnp.bfloat16)
    )
    softmaxed = probabilities(rotated_query, rotated_key, allowed)
    mixed = jnp.einsum(
        "kgtu,ukd->tkgd",
        softmaxed.astype(jnp.bfloat16),
        reduced_value,
        preferred_element_type=jnp.float32,
    )
    mixed_low = (mixed.reshape(token_total, query_width) * live[:, None]).astype(jnp.bfloat16)
    return inverse, normed, normed_low, rotated_query, rotated_key, reduced_value, mixed_low


def route_rows(hidden, weights, routed, chosen):
    qkv_full, out_full, router_full, gain_one, gain_two = weights
    inverse_two = lax.rsqrt(jnp.mean(hidden * hidden, axis=-1, keepdims=True) + EPSILON)
    normed_two = hidden * inverse_two
    routed_in = (normed_two * gain_two.astype(jnp.float32)).astype(jnp.bfloat16)
    rows = lax.dot_general(
        chosen, routed_in, (((0,), (0,)), ((), ())), preferred_element_type=jnp.float32
    ).astype(jnp.bfloat16)
    logits = jnp.dot(routed_in, router_full, preferred_element_type=jnp.float32)
    masked = jnp.where(routed, logits, MASKED)
    exp_chosen = jnp.where(routed, jnp.exp(masked - jnp.max(masked, axis=-1, keepdims=True)), 0.0)
    gate_prob = exp_chosen / jnp.sum(exp_chosen, axis=-1, keepdims=True)
    gate_wide = jnp.dot(
        gate_prob.astype(jnp.bfloat16), spread_table(), preferred_element_type=jnp.float32
    ).astype(jnp.bfloat16)
    return rows, (inverse_two, normed_two, routed_in, gate_prob, gate_wide * chosen)


def slot_gradients(grad_out, mixing):
    return lax.dot_general(
        mixing,
        grad_out.astype(jnp.bfloat16),
        (((0,), (0,)), ((), ())),
        preferred_element_type=jnp.float32,
    ).astype(jnp.bfloat16)


ACROSS = (((1,), (1,)), ((), ()))


def forward_kernel(rows_ref, expert_ref, results_ref, gate_ref, up_ref):
    rows = rows_ref[...]
    gate_pre = lax.dot_general(
        rows, expert_ref[:, :MODEL_WIDTH], ACROSS, preferred_element_type=jnp.float32
    )
    up_pre = lax.dot_general(
        rows,
        expert_ref[:, MODEL_WIDTH : 2 * MODEL_WIDTH],
        ACROSS,
        preferred_element_type=jnp.float32,
    )
    gate_ref[...] = gate_pre
    up_ref[...] = up_pre
    units = (gate_pre / (1.0 + jnp.exp(-gate_pre)) * up_pre).astype(jnp.bfloat16)
    results_ref[...] = jnp.dot(
        units, expert_ref[:, 2 * MODEL_WIDTH :], preferred_element_type=jnp.float32
    ).astype(jnp.bfloat16)


def backward_kernel(
    grad_ref, gate_ref, up_ref, expert_ref, rows_ref, grad_gate_ref, grad_up_ref, units_ref
):
    gate_pre, up_pre = gate_ref[...], up_ref[...]
    sigmoid_pre = 1.0 / (1.0 + jnp.exp(-gate_pre))
    activated = gate_pre * sigmoid_pre
    units_ref[...] = (activated * up_pre).astype(jnp.bfloat16)
    grad_units = lax.dot_general(
        grad_ref[...],
        expert_ref[:, 2 * MODEL_WIDTH :],
        ACROSS,
        preferred_element_type=jnp.float32,
    )
    grad_gate = (
        grad_units * up_pre * (sigmoid_pre * (1.0 + gate_pre * (1.0 - sigmoid_pre)))
    ).astype(jnp.bfloat16)
    grad_up = (grad_units * activated).astype(jnp.bfloat16)
    grad_gate_ref[...] = grad_gate
    grad_up_ref[...] = grad_up
    grad_rows = jnp.dot(
        grad_gate, expert_ref[:, :MODEL_WIDTH], preferred_element_type=jnp.float32
    ) + jnp.dot(
        grad_up,
        expert_ref[:, MODEL_WIDTH : 2 * MODEL_WIDTH],
        preferred_element_type=jnp.float32,
    )
    rows_ref[...] = grad_rows.astype(jnp.bfloat16)


def row_blocks(kernel, ins, expert_at, outs):
    def blocked(width):
        return pl.BlockSpec((ROW_BLOCK, width), lambda i: (i, 0))

    specs = [
        pl.BlockSpec(a.shape, lambda i: (0, 0)) if at == expert_at else blocked(a.shape[1])
        for at, a in enumerate(ins)
    ]
    flops = 2 * ROWS * 3 * MODEL_WIDTH * ins[expert_at].shape[0]
    moved = sum(a.size * a.dtype.itemsize for a in ins)
    return pl.pallas_call(
        kernel,
        grid=(ROWS // ROW_BLOCK,),
        in_specs=specs,
        out_specs=[blocked(width) for width, _ in outs],
        out_shape=[jax.ShapeDtypeStruct((ROWS, width), kind) for width, kind in outs],
        compiler_params=pltpu.CompilerParams(vmem_limit_bytes=40 * 1024 * 1024),
        cost_estimate=pl.CostEstimate(flops=flops, bytes_accessed=2 * moved, transcendentals=0),
    )(*ins)


def feed_forward(rows_here, expert):
    hidden_units = expert.shape[0]
    outs = (
        (MODEL_WIDTH, jnp.bfloat16),
        (hidden_units, jnp.float32),
        (hidden_units, jnp.float32),
    )
    results, gate_pre, up_pre = row_blocks(forward_kernel, (rows_here, expert), 1, outs)
    return results, (gate_pre, up_pre)


def feed_backward(grad_rows, rows_here, pre, expert):
    hidden_units = expert.shape[0]
    outs = ((MODEL_WIDTH, jnp.bfloat16),) + ((hidden_units, jnp.bfloat16),) * 3
    grad_in_rows, grad_gate_pre, grad_up_pre, units = row_blocks(
        backward_kernel, (grad_rows, *pre, expert), 3, outs
    )
    pair = (((0,), (0,)), ((), ()))
    gate_w_grad, up_w_grad, out_grad = [
        lax.dot_general(left, right, pair, preferred_element_type=jnp.float32)
        for left, right in (
            (grad_gate_pre, rows_here),
            (grad_up_pre, rows_here),
            (units, grad_rows),
        )
    ]
    return grad_in_rows, (gate_w_grad, up_w_grad, out_grad)


def route_backward(grad_out, weights, chosen, returned, stash):
    qkv_full, out_full, router_full, gain_one, gain_two = weights
    inverse_two, normed_two, routed_in, gate_prob, mixing = stash
    products = lax.dot_general(
        grad_out.astype(jnp.bfloat16),
        returned,
        (((1,), (1,)), ((), ())),
        preferred_element_type=jnp.float32,
    )
    grad_gate = lax.dot_general(
        products * chosen.astype(jnp.float32),
        spread_table().astype(jnp.float32),
        (((1,), (1,)), ((), ())),
        precision=lax.Precision.HIGHEST,
        preferred_element_type=jnp.float32,
    )
    grad_chosen = gate_prob * (grad_gate - jnp.sum(gate_prob * grad_gate, axis=-1, keepdims=True))
    grad_logits = grad_chosen.astype(jnp.bfloat16)
    router_grad = lax.dot_general(
        routed_in, grad_logits, (((0,), (0,)), ((), ())), preferred_element_type=jnp.float32
    )
    grad_routed = lax.dot_general(
        grad_logits, router_full, (((1,), (1,)), ((), ())), preferred_element_type=jnp.float32
    )
    return router_grad, grad_routed


def rows_backward(grad_out, weights, chosen, grad_slots, grad_routed, stash):
    qkv_full, out_full, router_full, gain_one, gain_two = weights
    inverse_two, normed_two, routed_in, gate_prob, mixing = stash
    grad_routed = grad_routed + jnp.dot(chosen, grad_slots, preferred_element_type=jnp.float32)
    gain_two_grad = jnp.sum(grad_routed * normed_two, axis=0)
    grad_h1 = grad_out + norm_back(
        grad_routed * gain_two.astype(jnp.float32), normed_two, inverse_two
    )
    return grad_h1, gain_two_grad


def attend_backward(
    grad_h1, weights, live, allowed, cosine_table, sine_values, attn_stash, attn_moved, mixed_moved
):
    qkv_full, out_full, router_full, gain_one, gain_two = weights
    inverse, normed, normed_low, rotated_query, rotated_key, reduced_value, mixed_low = attn_stash
    token_total = grad_h1.shape[0]
    query_width = QUERY_HEADS * HEAD_SIZE
    key_value_width = KEY_VALUE_HEADS * HEAD_SIZE
    grad_low = grad_h1.astype(jnp.bfloat16)
    proj_sum = core_sum(weight_halves(mixed_moved, grad_low))
    mixed_gradient = lax.dot_general(
        grad_low, out_full, (((1,), (1,)), ((), ())), preferred_element_type=jnp.float32
    ).astype(jnp.bfloat16)
    mixed_gradient = jnp.where(live[:, None] > 0.5, mixed_gradient, jnp.zeros_like(mixed_gradient))
    mixed_gradient = mixed_gradient.reshape(
        token_total, KEY_VALUE_HEADS, QUERY_HEADS // KEY_VALUE_HEADS, HEAD_SIZE
    )
    softmaxed = probabilities(rotated_query, rotated_key, allowed)
    grad_probs = jnp.einsum(
        "tkgd,ukd->kgtu", mixed_gradient, reduced_value, preferred_element_type=jnp.float32
    )
    grad_value = jnp.einsum(
        "kgtu,tkgd->ukd",
        softmaxed.astype(jnp.bfloat16),
        mixed_gradient,
        preferred_element_type=jnp.float32,
    )
    grad_scores = (
        softmaxed * (grad_probs - jnp.sum(softmaxed * grad_probs, axis=-1, keepdims=True))
    ).astype(jnp.bfloat16)
    grad_query = jnp.einsum(
        "kgtu,ukd->tkgd", grad_scores, rotated_key, preferred_element_type=jnp.float32
    ) * HEAD_SIZE ** (-0.5)
    grad_key = jnp.einsum(
        "kgtu,tkgd->ukd", grad_scores, rotated_query, preferred_element_type=jnp.float32
    ) * HEAD_SIZE ** (-0.5)
    grad_query = unrotate(
        rounded(grad_query.reshape(token_total, QUERY_HEADS, HEAD_SIZE)), cosine_table, sine_values
    ).astype(jnp.bfloat16)
    grad_key = unrotate(rounded(grad_key), cosine_table, sine_values).astype(jnp.bfloat16)
    grad_proj = jnp.concatenate(
        [
            grad_query.reshape(token_total, query_width),
            grad_key.reshape(token_total, key_value_width),
            grad_value.astype(jnp.bfloat16).reshape(token_total, key_value_width),
        ],
        axis=1,
    )
    qkv_halves = weight_halves(attn_moved, grad_proj)
    grad_normed = lax.dot_general(
        grad_proj, qkv_full, (((1,), (1,)), ((), ())), preferred_element_type=jnp.float32
    )
    gain_one_grad = jnp.sum(grad_normed * normed, axis=0)
    grad_input = grad_h1 + norm_back(grad_normed * gain_one.astype(jnp.float32), normed, inverse)
    return (grad_input, qkv_halves, proj_sum, gain_one_grad)


def on_device(
    hidden_in,
    cotangent,
    seq_lengths,
    seq_owner,
    routes,
    query_key_value_weight,
    out_weight,
    router_weight,
    gain_attn,
    gain_mlp,
    expert_in,
    expert_out,
):
    layers = range(LAYER_COUNT)
    last = LAYER_COUNT - 1
    device = lax.axis_index(AXES)
    order = order_table()
    own_dense = [
        (
            query_key_value_weight[layer],
            out_weight[layer],
            router_weight[layer],
            gain_attn[layer],
            gain_mlp[layer],
        )
        for layer in layers
    ]
    lead = [part.reshape(8, -1) for part in own_dense[0]]
    fill = jnp.zeros((8, 128 - E - 2), jnp.bfloat16)
    position, live_row, allowed = seq_layout(seq_lengths, seq_owner, device)
    routed, chosen = dispatch_table(routes, live_row)
    own_experts = [
        jnp.concatenate([expert_in[layer], expert_out[layer]], axis=1) for layer in layers
    ]
    beside = order, routed, chosen, own_experts
    lead, beside = sent_by_chips(jnp.concatenate(lead + [fill], axis=1), beside)
    order, routed, chosen, own_experts = beside
    live = live_row.astype(jnp.float32)
    cosine_table, sine_values = rope_tables(position)
    other_expert = lax.ppermute(own_experts[0], "zl", SWAP)
    lead, own_dense = lax.optimization_barrier((lead, own_dense))
    dense = [cut_weights(lead, DENSE_WIDTHS), None]
    dense[1] = cut_weights(sent_together(own_dense[1], AXES), DENSE_WIDTHS)
    hidden = hidden_in.astype(jnp.float32)
    grad_hidden = cotangent.astype(jnp.float32)
    saved, experts = [], []
    for layer in layers:
        attn_stash = attend_forward(
            hidden, dense[layer][0], dense[layer][3], live, allowed, cosine_table, sine_values
        )
        mixed_low = attn_stash[-1]
        hidden = hidden + jnp.dot(mixed_low, dense[layer][1], preferred_element_type=jnp.float32)
        rows, route_stash = route_rows(hidden, dense[layer], routed, chosen)
        rows, other_expert = lax.optimization_barrier((rows, other_expert))
        rows_here = trade_rows(rows)
        expert = gather_core(join_chip(own_experts[layer], other_expert))
        moved = reorder(attn_stash[2], order), reorder(mixed_low, order)
        grad_rows = None
        if layer == last:
            slots = slot_gradients(grad_hidden, route_stash[-1])
            slots, rows_here = lax.optimization_barrier((slots, rows_here))
            grad_rows = trade_rows(slots)
        experts.append(expert)
        results, pre = feed_forward(rows_here, expert)
        if layer == last:
            results, grad_rows = lax.optimization_barrier((results, grad_rows))
        returned = trade_rows(results)
        if layer != last:
            returned, own_expert = lax.optimization_barrier((returned, own_experts[layer + 1]))
            other_expert = lax.ppermute(own_expert, "zl", SWAP)
        hidden = hidden + jnp.dot(route_stash[-1], returned, preferred_element_type=jnp.float32)
        saved.append((attn_stash, moved, route_stash, rows_here, pre, returned, grad_rows))
    output_low = hidden.astype(jnp.bfloat16)
    expert_sums = [None] * LAYER_COUNT
    for layer in reversed(layers):
        attn_stash, moved, route_stash, rows_here, pre, returned, grad_rows = saved[layer]
        if grad_rows is None:
            slots = slot_gradients(grad_hidden, route_stash[-1])
            grad_rows, sums = lax.optimization_barrier((trade_rows(slots), sums))
            joined = jnp.concatenate(sums, axis=1)
        grad_in_rows, expert_grads = feed_backward(grad_rows, rows_here, pre, experts[layer])
        grad_slots = trade_rows(grad_in_rows)
        router_grad, grad_routed = route_backward(
            grad_hidden, dense[layer], chosen, returned, route_stash
        )
        expert_sums[layer] = scatter_expert(expert_grads)
        if layer != last:
            grad_slots, joined = lax.optimization_barrier((grad_slots, joined))
            done_last = chip_sum(joined)
        grad_h1, gain_two_grad = rows_backward(
            grad_hidden, dense[layer], chosen, grad_slots, grad_routed, route_stash
        )
        grad_hidden, qkv_halves, proj_sum, gain_one_grad = attend_backward(
            grad_h1, dense[layer], live, allowed, cosine_table, sine_values, attn_stash, *moved
        )
        small = small_halves(router_grad, gain_one_grad, gain_two_grad, order)
        sums = [core_sum(qkv_halves), proj_sum, core_sum(small)]
    done = chip_sum(jnp.concatenate(sums, axis=1))
    first, second = [(d[:, :2048], d[:, 2048:3072], d[:, 3072:]) for d in (done, done_last)]
    qkv, proj, small = [jnp.stack(pair) for pair in zip(first, second)]
    both = jnp.stack(expert_sums).astype(jnp.float32)
    return (
        output_low,
        grad_hidden,
        qkv,
        proj,
        small[:, :, :E],
        small[:, :, E],
        small[:, :, E + 1],
        both[:, :, : 2 * MODEL_WIDTH],
        both[:, :, 2 * MODEL_WIDTH :],
    )


def solution(mesh):
    grid = Mesh(mesh.devices.reshape(4, 4, 2, 2, 2), AXES)
    placed = (
        P(AXES, None),
        P(AXES, None),
        P(),
        P(),
        P(AXES, None),
        P(None, AXES, None),
        P(None, AXES, None),
        P(None, AXES, None),
        P(None, AXES),
        P(None, AXES),
        P(None, AXES, None),
        P(None, AXES, None),
    )
    return jax.shard_map(
        on_device,
        mesh=grid,
        in_specs=placed,
        out_specs=(
            P(AXES, None),
            P(AXES, None),
            P(None, AXES, None),
            P(None, AXES, None),
            P(None, AXES, None),
            P(None, AXES),
            P(None, AXES),
            P(None, AXES, None),
            P(None, AXES, None),
        ),
        check_vma=False,
    )
```

```python
import math

import jax
import jax.numpy as jnp
from jax import lax
from jax.experimental import pallas as pl
from jax.experimental.pallas import tpu as pltpu
from jax.sharding import Mesh, PartitionSpec as P

MODEL_WIDTH = 1024
QUERY_HEADS = 16
KEY_VALUE_HEADS = 8
HEAD_SIZE = 64
E = 32
TOPK = 8
LAYER_COUNT = 2
SEQ_DEV = 4
TOK_DEV = 128
CAP = 36


EPSILON = 1e-06
ROPE_BASE = 10000.0
MASKED = -1e30

ROOM = 40
ROWS = E * ROOM
ROW_BLOCK = 256
AXES = ("x", "y", "zh", "zl", "c")
EXPERT_AXES = ("x", "y", "zh")
CHIP_AXES = ("x", "y", "zh", "zl")
Z_AXES = ("zh", "zl")
GROUP_AXES = ("zl", "c")
DENSE_WIDTHS = (2048, 1024, E, 1, 1)
HALF = MODEL_WIDTH // 2
SWAP = [(0, 1), (1, 0)]


def sent_together(arrays, axis):
    both = jnp.concatenate([a.reshape(a.shape[0], -1) for a in arrays], axis=1)
    return lax.all_gather(both, axis, axis=0, tiled=True)


def sent_by_chips(own, beside):
    core = lax.axis_index("c")
    copies = jnp.broadcast_to(own[None], (64,) + own.shape)
    mine = lax.all_to_all(copies, CHIP_AXES, split_axis=0, concat_axis=0, tiled=True)
    mine, beside = lax.optimization_barrier((mine, beside))
    other = lax.ppermute(mine, "c", SWAP)
    pair = [jnp.where(core == 0, mine, other), jnp.where(core == 0, other, mine)]
    return jnp.stack(pair, axis=1).reshape(MODEL_WIDTH, -1), beside


def cut_weights(gathered, widths):
    at, pieces = 0, []
    for width in widths:
        pieces.append(gathered[:, at : at + width])
        at += width
    return tuple(pieces[:-2]) + (pieces[-2][:, 0], pieces[-1][:, 0])


def seq_layout(seq_lengths, seq_owner, device):
    owned_seq = seq_owner == device
    ranking = jnp.cumsum(owned_seq.astype(jnp.int32)) - 1
    counter = jnp.arange(SEQ_DEV, dtype=jnp.int32)
    picker = (owned_seq[None, :] & (ranking[None, :] == counter[:, None])).astype(jnp.int32)
    own_lengths = jnp.sum(picker * seq_lengths[None, :], axis=1)
    seq_ends = jnp.cumsum(own_lengths)
    slot_ids = jnp.arange(TOK_DEV, dtype=jnp.int32)
    segment = jnp.sum((slot_ids[:, None] >= seq_ends[None, :]).astype(jnp.int32), axis=1)
    seq_starts = seq_ends - own_lengths
    first_slot = jnp.sum(
        jnp.where(segment[:, None] == counter[None, :], seq_starts[None, :], 0), axis=1
    )
    position = slot_ids - first_slot
    allowed = (segment[:, None] == segment[None, :]) & (slot_ids[:, None] >= slot_ids[None, :])
    return (position, segment < SEQ_DEV, allowed)


def rope_tables(position):
    half_size = HEAD_SIZE // 2
    exponent = jnp.arange(half_size, dtype=jnp.float32) * (2.0 / HEAD_SIZE)
    frequency = jnp.exp(-math.log(ROPE_BASE) * exponent)
    angles = position.astype(jnp.float32)[:, None] * frequency[None, :]
    return (jnp.cos(angles), jnp.sin(angles))


def apply_rotation(values, cosine_table, sine_values):
    half_size = values.shape[-1] // 2
    first_half = values[..., :half_size]
    second_half = values[..., half_size:]
    cos_wide = cosine_table[:, None, :]
    sin_wide = sine_values[:, None, :]
    return jnp.concatenate(
        [
            first_half * cos_wide - second_half * sin_wide,
            second_half * cos_wide + first_half * sin_wide,
        ],
        axis=-1,
    )


def unrotate(grad_rot, cosine_table, sine_values):
    half_size = grad_rot.shape[-1] // 2
    first_half = grad_rot[..., :half_size]
    second_half = grad_rot[..., half_size:]
    cos_wide = cosine_table[:, None, :]
    sin_wide = sine_values[:, None, :]
    return jnp.concatenate(
        [
            first_half * cos_wide + second_half * sin_wide,
            second_half * cos_wide - first_half * sin_wide,
        ],
        axis=-1,
    )


def rounded(values):
    return lax.optimization_barrier(values.astype(jnp.bfloat16)).astype(jnp.float32)


def dispatch_table(route_block, live_row):
    experts = jnp.arange(E, dtype=jnp.int32)
    routed = jnp.any(route_block[:, :, None] == experts[None, None, :], axis=1)
    hits = (routed & live_row[:, None]).astype(jnp.bfloat16)
    slot_ids = jnp.arange(TOK_DEV, dtype=jnp.int32)
    before = (slot_ids[None, :] < slot_ids[:, None]).astype(jnp.bfloat16)
    rank = jnp.dot(before, hits, preferred_element_type=jnp.float32)
    code = jnp.where(hits > 0, rank, -1.0).astype(jnp.bfloat16)
    spread = spread_table()
    wide = jnp.dot(code, spread, preferred_element_type=jnp.float32)
    place = (jnp.arange(ROWS, dtype=jnp.int32) % ROOM).astype(jnp.float32)
    chosen = (wide == place[None, :]).astype(jnp.bfloat16)
    return routed, chosen


def spread_table():
    rows = jnp.arange(ROWS, dtype=jnp.int32) // ROOM
    return (jnp.arange(E, dtype=jnp.int32)[:, None] == rows[None, :]).astype(jnp.bfloat16)


def trade_rows(rows):
    return lax.all_to_all(
        rows.reshape(E, ROOM, MODEL_WIDTH), EXPERT_AXES, split_axis=0, concat_axis=0, tiled=True
    ).reshape(ROWS, MODEL_WIDTH)


def join_chip(own, other):
    first = lax.axis_index("zl") == 0
    return jnp.stack([jnp.where(first, own, other), jnp.where(first, other, own)])


def gather_core(pair):
    other = lax.ppermute(pair, "c", SWAP)
    first = lax.axis_index("c") == 0
    both = [jnp.where(first, pair, other), jnp.where(first, other, pair)]
    return jnp.stack(both, axis=1).reshape(-1, pair.shape[2])


def scatter_expert(grads):
    both = jnp.concatenate(grads, axis=1).astype(jnp.bfloat16)
    return lax.psum_scatter(both, GROUP_AXES, scatter_dimension=0, tiled=True)


def order_table():
    at = jnp.arange(MODEL_WIDTH, dtype=jnp.int32)
    core = (at // HALF + lax.axis_index("c")) % 2
    depth, plane, row = at // 128 % 4, at // 8 % 16, at % 8
    source = (plane * 4 + depth) * 16 + core * 8 + row
    return (at[:, None] == source[None, :]).astype(jnp.bfloat16)


def reorder(values, order):
    return jnp.dot(values, order, preferred_element_type=jnp.float32).astype(jnp.bfloat16)


def weight_halves(left, right):
    pair = (((0,), (0,)), ((), ()))
    kept = lax.dot_general(left[:, :HALF], right, pair, preferred_element_type=jnp.float32)
    given = lax.dot_general(left[:, HALF:], right, pair, preferred_element_type=jnp.float32)
    return kept, given.astype(jnp.bfloat16)


def small_halves(router_grad, gain_one_grad, gain_two_grad, order):
    fill = jnp.zeros((MODEL_WIDTH, 128 - E - 2), jnp.float32)
    small = jnp.concatenate(
        [router_grad, gain_one_grad[:, None], gain_two_grad[:, None], fill], axis=1
    ).astype(jnp.bfloat16)
    moved = lax.dot_general(
        order, small, (((0,), (0,)), ((), ())), preferred_element_type=jnp.float32
    )
    return moved[:HALF], moved[HALF:].astype(jnp.bfloat16)


def core_sum(halves):
    kept, given = halves
    return (kept + lax.ppermute(given, "c", SWAP).astype(jnp.float32)).astype(jnp.bfloat16)


def chip_sum(parts):
    parts = parts.reshape(64, 8, -1)
    parts = lax.all_to_all(parts, Z_AXES + ("x", "y"), split_axis=0, concat_axis=0, tiled=True)
    return jnp.sum(parts.astype(jnp.float32), axis=0)


def norm_back(grad_norm, normed, inverse):
    return inverse * (grad_norm - normed * jnp.mean(grad_norm * normed, axis=-1, keepdims=True))


def probabilities(rotated_query, rotated_key, allowed):
    scores = jnp.einsum(
        "tkgd,ukd->kgtu", rotated_query, rotated_key, preferred_element_type=jnp.float32
    ) * HEAD_SIZE ** (-0.5)
    scores = jnp.where(allowed[None, None], scores, MASKED)
    biggest = jnp.max(scores, axis=-1, keepdims=True)
    exp_scores = jnp.exp(scores - biggest)
    return exp_scores / jnp.sum(exp_scores, axis=-1, keepdims=True)


def attend_forward(hidden, qkv_full, gain_one, live, allowed, cosine_table, sine_values):
    token_total = hidden.shape[0]
    query_width = QUERY_HEADS * HEAD_SIZE
    key_value_width = KEY_VALUE_HEADS * HEAD_SIZE
    inverse = lax.rsqrt(jnp.mean(hidden * hidden, axis=-1, keepdims=True) + EPSILON)
    normed = hidden * inverse
    normed_low = (normed * gain_one.astype(jnp.float32)).astype(jnp.bfloat16)
    projected_rows = jnp.dot(normed_low, qkv_full, preferred_element_type=jnp.float32)
    rotated_query = apply_rotation(
        projected_rows[:, :query_width].reshape(token_total, QUERY_HEADS, HEAD_SIZE),
        cosine_table,
        sine_values,
    ).astype(jnp.bfloat16)
    rotated_query = rotated_query.reshape(
        token_total, KEY_VALUE_HEADS, QUERY_HEADS // KEY_VALUE_HEADS, HEAD_SIZE
    )
    rotated_key = apply_rotation(
        projected_rows[:, query_width : query_width + key_value_width].reshape(
            token_total, KEY_VALUE_HEADS, HEAD_SIZE
        ),
        cosine_table,
        sine_values,
    ).astype(jnp.bfloat16)
    reduced_value = (
        projected_rows[:, query_width + key_value_width :]
        .reshape(token_total, KEY_VALUE_HEADS, HEAD_SIZE)
        .astype(jnp.bfloat16)
    )
    softmaxed = probabilities(rotated_query, rotated_key, allowed)
    mixed = jnp.einsum(
        "kgtu,ukd->tkgd",
        softmaxed.astype(jnp.bfloat16),
        reduced_value,
        preferred_element_type=jnp.float32,
    )
    mixed_low = (mixed.reshape(token_total, query_width) * live[:, None]).astype(jnp.bfloat16)
    return inverse, normed, normed_low, rotated_query, rotated_key, reduced_value, mixed_low


def route_rows(hidden, weights, routed, chosen):
    qkv_full, out_full, router_full, gain_one, gain_two = weights
    inverse_two = lax.rsqrt(jnp.mean(hidden * hidden, axis=-1, keepdims=True) + EPSILON)
    normed_two = hidden * inverse_two
    routed_in = (normed_two * gain_two.astype(jnp.float32)).astype(jnp.bfloat16)
    rows = lax.dot_general(
        chosen, routed_in, (((0,), (0,)), ((), ())), preferred_element_type=jnp.float32
    ).astype(jnp.bfloat16)
    logits = jnp.dot(routed_in, router_full, preferred_element_type=jnp.float32)
    masked = jnp.where(routed, logits, MASKED)
    exp_chosen = jnp.where(routed, jnp.exp(masked - jnp.max(masked, axis=-1, keepdims=True)), 0.0)
    gate_prob = exp_chosen / jnp.sum(exp_chosen, axis=-1, keepdims=True)
    gate_wide = jnp.dot(
        gate_prob.astype(jnp.bfloat16), spread_table(), preferred_element_type=jnp.float32
    ).astype(jnp.bfloat16)
    return rows, (inverse_two, normed_two, routed_in, gate_prob, gate_wide * chosen)


def slot_gradients(grad_out, mixing):
    return lax.dot_general(
        mixing,
        grad_out.astype(jnp.bfloat16),
        (((0,), (0,)), ((), ())),
        preferred_element_type=jnp.float32,
    ).astype(jnp.bfloat16)


ACROSS = (((1,), (1,)), ((), ()))


def forward_kernel(rows_ref, expert_ref, results_ref, gate_ref, up_ref):
    rows = rows_ref[...]
    gate_pre = lax.dot_general(
        rows, expert_ref[:, :MODEL_WIDTH], ACROSS, preferred_element_type=jnp.float32
    )
    up_pre = lax.dot_general(
        rows,
        expert_ref[:, MODEL_WIDTH : 2 * MODEL_WIDTH],
        ACROSS,
        preferred_element_type=jnp.float32,
    )
    gate_ref[...] = gate_pre
    up_ref[...] = up_pre
    units = (gate_pre / (1.0 + jnp.exp(-gate_pre)) * up_pre).astype(jnp.bfloat16)
    results_ref[...] = jnp.dot(
        units, expert_ref[:, 2 * MODEL_WIDTH :], preferred_element_type=jnp.float32
    ).astype(jnp.bfloat16)


def backward_kernel(
    grad_ref, gate_ref, up_ref, expert_ref, rows_ref, grad_gate_ref, grad_up_ref, units_ref
):
    gate_pre, up_pre = gate_ref[...], up_ref[...]
    sigmoid_pre = 1.0 / (1.0 + jnp.exp(-gate_pre))
    activated = gate_pre * sigmoid_pre
    units_ref[...] = (activated * up_pre).astype(jnp.bfloat16)
    grad_units = lax.dot_general(
        grad_ref[...],
        expert_ref[:, 2 * MODEL_WIDTH :],
        ACROSS,
        preferred_element_type=jnp.float32,
    )
    grad_gate = (
        grad_units * up_pre * (sigmoid_pre * (1.0 + gate_pre * (1.0 - sigmoid_pre)))
    ).astype(jnp.bfloat16)
    grad_up = (grad_units * activated).astype(jnp.bfloat16)
    grad_gate_ref[...] = grad_gate
    grad_up_ref[...] = grad_up
    grad_rows = jnp.dot(
        grad_gate, expert_ref[:, :MODEL_WIDTH], preferred_element_type=jnp.float32
    ) + jnp.dot(
        grad_up,
        expert_ref[:, MODEL_WIDTH : 2 * MODEL_WIDTH],
        preferred_element_type=jnp.float32,
    )
    rows_ref[...] = grad_rows.astype(jnp.bfloat16)


def row_blocks(kernel, ins, expert_at, outs):
    def blocked(width):
        return pl.BlockSpec((ROW_BLOCK, width), lambda i: (i, 0))

    specs = [
        pl.BlockSpec(a.shape, lambda i: (0, 0)) if at == expert_at else blocked(a.shape[1])
        for at, a in enumerate(ins)
    ]
    flops = 2 * ROWS * 3 * MODEL_WIDTH * ins[expert_at].shape[0]
    moved = sum(a.size * a.dtype.itemsize for a in ins)
    return pl.pallas_call(
        kernel,
        grid=(ROWS // ROW_BLOCK,),
        in_specs=specs,
        out_specs=[blocked(width) for width, _ in outs],
        out_shape=[jax.ShapeDtypeStruct((ROWS, width), kind) for width, kind in outs],
        compiler_params=pltpu.CompilerParams(vmem_limit_bytes=56 * 1024 * 1024),
        cost_estimate=pl.CostEstimate(flops=flops, bytes_accessed=2 * moved, transcendentals=0),
    )(*ins)


def feed_forward(rows_here, expert):
    hidden_units = expert.shape[0]
    outs = (
        (MODEL_WIDTH, jnp.bfloat16),
        (hidden_units, jnp.float32),
        (hidden_units, jnp.float32),
    )
    results, gate_pre, up_pre = row_blocks(forward_kernel, (rows_here, expert), 1, outs)
    return results, (gate_pre, up_pre)


def feed_backward(grad_rows, rows_here, pre, expert):
    hidden_units = expert.shape[0]
    outs = ((MODEL_WIDTH, jnp.bfloat16),) + ((hidden_units, jnp.bfloat16),) * 3
    grad_in_rows, grad_gate_pre, grad_up_pre, units = row_blocks(
        backward_kernel, (grad_rows, *pre, expert), 3, outs
    )
    pair = (((0,), (0,)), ((), ()))
    gate_w_grad, up_w_grad, out_grad = [
        lax.dot_general(left, right, pair, preferred_element_type=jnp.float32)
        for left, right in (
            (grad_gate_pre, rows_here),
            (grad_up_pre, rows_here),
            (units, grad_rows),
        )
    ]
    return grad_in_rows, (gate_w_grad, up_w_grad, out_grad)


def route_backward(grad_out, weights, chosen, returned, stash):
    qkv_full, out_full, router_full, gain_one, gain_two = weights
    inverse_two, normed_two, routed_in, gate_prob, mixing = stash
    products = lax.dot_general(
        grad_out.astype(jnp.bfloat16),
        returned,
        (((1,), (1,)), ((), ())),
        preferred_element_type=jnp.float32,
    )
    grad_gate = lax.dot_general(
        products * chosen.astype(jnp.float32),
        spread_table().astype(jnp.float32),
        (((1,), (1,)), ((), ())),
        precision=lax.Precision.HIGHEST,
        preferred_element_type=jnp.float32,
    )
    grad_chosen = gate_prob * (grad_gate - jnp.sum(gate_prob * grad_gate, axis=-1, keepdims=True))
    grad_logits = grad_chosen.astype(jnp.bfloat16)
    router_grad = lax.dot_general(
        routed_in, grad_logits, (((0,), (0,)), ((), ())), preferred_element_type=jnp.float32
    )
    grad_routed = lax.dot_general(
        grad_logits, router_full, (((1,), (1,)), ((), ())), preferred_element_type=jnp.float32
    )
    return router_grad, grad_routed


def rows_backward(grad_out, weights, chosen, grad_slots, grad_routed, stash):
    qkv_full, out_full, router_full, gain_one, gain_two = weights
    inverse_two, normed_two, routed_in, gate_prob, mixing = stash
    grad_routed = grad_routed + jnp.dot(chosen, grad_slots, preferred_element_type=jnp.float32)
    gain_two_grad = jnp.sum(grad_routed * normed_two, axis=0)
    grad_h1 = grad_out + norm_back(
        grad_routed * gain_two.astype(jnp.float32), normed_two, inverse_two
    )
    return grad_h1, gain_two_grad


def attend_backward(
    grad_h1, weights, live, allowed, cosine_table, sine_values, attn_stash, attn_moved, mixed_moved
):
    qkv_full, out_full, router_full, gain_one, gain_two = weights
    inverse, normed, normed_low, rotated_query, rotated_key, reduced_value, mixed_low = attn_stash
    token_total = grad_h1.shape[0]
    query_width = QUERY_HEADS * HEAD_SIZE
    key_value_width = KEY_VALUE_HEADS * HEAD_SIZE
    grad_low = grad_h1.astype(jnp.bfloat16)
    proj_sum = core_sum(weight_halves(mixed_moved, grad_low))
    mixed_gradient = lax.dot_general(
        grad_low, out_full, (((1,), (1,)), ((), ())), preferred_element_type=jnp.float32
    ).astype(jnp.bfloat16)
    mixed_gradient = jnp.where(live[:, None] > 0.5, mixed_gradient, jnp.zeros_like(mixed_gradient))
    mixed_gradient = mixed_gradient.reshape(
        token_total, KEY_VALUE_HEADS, QUERY_HEADS // KEY_VALUE_HEADS, HEAD_SIZE
    )
    softmaxed = probabilities(rotated_query, rotated_key, allowed)
    grad_probs = jnp.einsum(
        "tkgd,ukd->kgtu", mixed_gradient, reduced_value, preferred_element_type=jnp.float32
    )
    grad_value = jnp.einsum(
        "kgtu,tkgd->ukd",
        softmaxed.astype(jnp.bfloat16),
        mixed_gradient,
        preferred_element_type=jnp.float32,
    )
    grad_scores = (
        softmaxed * (grad_probs - jnp.sum(softmaxed * grad_probs, axis=-1, keepdims=True))
    ).astype(jnp.bfloat16)
    grad_query = jnp.einsum(
        "kgtu,ukd->tkgd", grad_scores, rotated_key, preferred_element_type=jnp.float32
    ) * HEAD_SIZE ** (-0.5)
    grad_key = jnp.einsum(
        "kgtu,tkgd->ukd", grad_scores, rotated_query, preferred_element_type=jnp.float32
    ) * HEAD_SIZE ** (-0.5)
    grad_query = unrotate(
        rounded(grad_query.reshape(token_total, QUERY_HEADS, HEAD_SIZE)), cosine_table, sine_values
    ).astype(jnp.bfloat16)
    grad_key = unrotate(rounded(grad_key), cosine_table, sine_values).astype(jnp.bfloat16)
    grad_proj = jnp.concatenate(
        [
            grad_query.reshape(token_total, query_width),
            grad_key.reshape(token_total, key_value_width),
            grad_value.astype(jnp.bfloat16).reshape(token_total, key_value_width),
        ],
        axis=1,
    )
    qkv_halves = weight_halves(attn_moved, grad_proj)
    grad_normed = lax.dot_general(
        grad_proj, qkv_full, (((1,), (1,)), ((), ())), preferred_element_type=jnp.float32
    )
    gain_one_grad = jnp.sum(grad_normed * normed, axis=0)
    grad_input = grad_h1 + norm_back(grad_normed * gain_one.astype(jnp.float32), normed, inverse)
    return (grad_input, qkv_halves, proj_sum, gain_one_grad)


def on_device(
    hidden_in,
    cotangent,
    seq_lengths,
    seq_owner,
    routes,
    query_key_value_weight,
    out_weight,
    router_weight,
    gain_attn,
    gain_mlp,
    expert_in,
    expert_out,
):
    layers = range(LAYER_COUNT)
    last = LAYER_COUNT - 1
    device = lax.axis_index(AXES)
    order = order_table()
    own_dense = [
        (
            query_key_value_weight[layer],
            out_weight[layer],
            router_weight[layer],
            gain_attn[layer],
            gain_mlp[layer],
        )
        for layer in layers
    ]
    lead = [part.reshape(8, -1) for part in own_dense[0]]
    fill = jnp.zeros((8, 128 - E - 2), jnp.bfloat16)
    position, live_row, allowed = seq_layout(seq_lengths, seq_owner, device)
    routed, chosen = dispatch_table(routes, live_row)
    own_experts = [
        jnp.concatenate([expert_in[layer], expert_out[layer]], axis=1) for layer in layers
    ]
    beside = order, routed, chosen, own_experts
    lead, beside = sent_by_chips(jnp.concatenate(lead + [fill], axis=1), beside)
    order, routed, chosen, own_experts = beside
    live = live_row.astype(jnp.float32)
    cosine_table, sine_values = rope_tables(position)
    other_expert = lax.ppermute(own_experts[0], "zl", SWAP)
    lead, own_dense = lax.optimization_barrier((lead, own_dense))
    dense = [cut_weights(lead, DENSE_WIDTHS), None]
    dense[1] = cut_weights(sent_together(own_dense[1], AXES), DENSE_WIDTHS)
    hidden = hidden_in.astype(jnp.float32)
    grad_hidden = cotangent.astype(jnp.float32)
    saved, experts = [], []
    for layer in layers:
        attn_stash = attend_forward(
            hidden, dense[layer][0], dense[layer][3], live, allowed, cosine_table, sine_values
        )
        mixed_low = attn_stash[-1]
        hidden = hidden + jnp.dot(mixed_low, dense[layer][1], preferred_element_type=jnp.float32)
        rows, route_stash = route_rows(hidden, dense[layer], routed, chosen)
        rows, other_expert = lax.optimization_barrier((rows, other_expert))
        rows_here = trade_rows(rows)
        expert = gather_core(join_chip(own_experts[layer], other_expert))
        moved = reorder(attn_stash[2], order), reorder(mixed_low, order)
        grad_rows = None
        if layer == last:
            slots = slot_gradients(grad_hidden, route_stash[-1])
            slots, rows_here = lax.optimization_barrier((slots, rows_here))
            grad_rows = trade_rows(slots)
        experts.append(expert)
        results, pre = feed_forward(rows_here, expert)
        if layer == last:
            results, grad_rows = lax.optimization_barrier((results, grad_rows))
        returned = trade_rows(results)
        if layer != last:
            returned, own_expert = lax.optimization_barrier((returned, own_experts[layer + 1]))
            other_expert = lax.ppermute(own_expert, "zl", SWAP)
        hidden = hidden + jnp.dot(route_stash[-1], returned, preferred_element_type=jnp.float32)
        saved.append((attn_stash, moved, route_stash, rows_here, pre, returned, grad_rows))
    output_low = hidden.astype(jnp.bfloat16)
    expert_sums = [None] * LAYER_COUNT
    for layer in reversed(layers):
        attn_stash, moved, route_stash, rows_here, pre, returned, grad_rows = saved[layer]
        if grad_rows is None:
            slots = slot_gradients(grad_hidden, route_stash[-1])
            grad_rows, sums = lax.optimization_barrier((trade_rows(slots), sums))
            joined = jnp.concatenate(sums, axis=1)
        grad_in_rows, expert_grads = feed_backward(grad_rows, rows_here, pre, experts[layer])
        grad_slots = trade_rows(grad_in_rows)
        router_grad, grad_routed = route_backward(
            grad_hidden, dense[layer], chosen, returned, route_stash
        )
        expert_sums[layer] = scatter_expert(expert_grads)
        if layer != last:
            grad_slots, joined = lax.optimization_barrier((grad_slots, joined))
            done_last = chip_sum(joined)
        grad_h1, gain_two_grad = rows_backward(
            grad_hidden, dense[layer], chosen, grad_slots, grad_routed, route_stash
        )
        grad_hidden, qkv_halves, proj_sum, gain_one_grad = attend_backward(
            grad_h1, dense[layer], live, allowed, cosine_table, sine_values, attn_stash, *moved
        )
        small = small_halves(router_grad, gain_one_grad, gain_two_grad, order)
        sums = [core_sum(qkv_halves), proj_sum, core_sum(small)]
    done = chip_sum(jnp.concatenate(sums, axis=1))
    first, second = [(d[:, :2048], d[:, 2048:3072], d[:, 3072:]) for d in (done, done_last)]
    qkv, proj, small = [jnp.stack(pair) for pair in zip(first, second)]
    both = jnp.stack(expert_sums).astype(jnp.float32)
    return (
        output_low,
        grad_hidden,
        qkv,
        proj,
        small[:, :, :E],
        small[:, :, E],
        small[:, :, E + 1],
        both[:, :, : 2 * MODEL_WIDTH],
        both[:, :, 2 * MODEL_WIDTH :],
    )


def solution(mesh):
    grid = Mesh(mesh.devices.reshape(4, 4, 2, 2, 2), AXES)
    placed = (
        P(AXES, None),
        P(AXES, None),
        P(),
        P(),
        P(AXES, None),
        P(None, AXES, None),
        P(None, AXES, None),
        P(None, AXES, None),
        P(None, AXES),
        P(None, AXES),
        P(None, AXES, None),
        P(None, AXES, None),
    )
    return jax.shard_map(
        on_device,
        mesh=grid,
        in_specs=placed,
        out_specs=(
            P(AXES, None),
            P(AXES, None),
            P(None, AXES, None),
            P(None, AXES, None),
            P(None, AXES, None),
            P(None, AXES),
            P(None, AXES),
            P(None, AXES, None),
            P(None, AXES, None),
        ),
        check_vma=False,
    )
```
